256 devices in a mesh: space: 64 (over x, y, z_hi, core), filt: 4 (over z_lo).
Axes of the slice: x: 4, y: 4, z: 8 (z_hi: 2, z_lo: 4; z = z_hi * 4 + z_lo), core: 2. Of those that a mesh axis runs over, the one named last changes fastest.
Arguments:
- volume: bfloat16 [128, 16, 64, 256], P('space', None, 'filt'), may hold values from -6 to 6
- weight_first: bfloat16 [27, 256, 512], P(None, None, 'filt'), may hold values from -0.078125 to 0.078125
- weight_second: bfloat16 [27, 512, 512], P(None, None, 'filt'), may hold values from -0.0546875 to 0.0546875
- cotangent: bfloat16 [64, 8, 32, 512], P('space', None, None, 'filt'), may hold values from -6 to 6
Outputs:
- grad_input: bfloat16 [128, 16, 64, 256], P('space', None, 'filt')
- grad_weight_first: float32 [27, 256, 512], P(None, 'space', 'filt')
- grad_weight_second: float32 [27, 512, 512], P(None, 'space', 'filt')
The draws below stay inside these ranges and needn't reach their ends.
All inputs are finite; a program needn't handle non-finite values.
Results may differ from the reference program's by a relative error of at most 0.023.
Values may be sent and summed in bfloat16 or wider, within the bound.
A program may use at most 128 MiB of HBM per device.

```python
import jax
import jax.numpy as jnp
from jax import lax

C0 = 256
C1 = 512
NY = 16
NX = 64
NZ = 128


def block_levels(own_key, dims, pieces, low, high):
    def one(axis_at, parts):
        steps = jax.random.uniform(jax.random.fold_in(jax.random.fold_in(own_key, 6), axis_at), (parts,), jnp.float32, low / len(pieces), high / len(pieces))
        return jnp.repeat(jnp.exp(steps), dims[axis_at] // parts).reshape((-1,) + (1,) * (len(dims) - axis_at - 1))

    loudness = one(*pieces[0])
    for cut in pieces[1:]:
        loudness = loudness * one(*cut)
    return loudness


def centred(own_key, extent, deviation, limit, split=(), kind=jnp.bfloat16):
    level = block_levels(own_key, extent, split, -0.22, 0.18) if split else 1.0
    values = jax.random.normal(own_key, extent, jnp.float32) * deviation * level
    return jnp.minimum(jnp.maximum(values, -limit), limit).astype(kind)


def setup_inputs(seed: int = 0) -> dict:
    streams_of = jax.random.split(jax.random.key(seed), 5)
    volume = centred(streams_of[0], (NZ, NY, NX, C0), 1.0, 6.0, ((0, 64), (2, 4)))
    weight_first = centred(streams_of[1], (27, C0, C1), (27 * C0) ** -0.5, 0.078125, ((2, 4),))
    weight_second = centred(streams_of[2], (27, C1, C1), (27 * C1) ** -0.5, 0.0546875, ((2, 4),))
    cotangent = centred(streams_of[3], (NZ // 2, NY // 2, NX // 2, C1), 1.0, 6.0, ((0, 64), (3, 4)))
    return dict(volume=volume, weight_first=weight_first, weight_second=weight_second, cotangent=cotangent)


def conv_full(source, kernel, stride):
    result = lax.conv_general_dilated(source[None], kernel, (stride, stride, stride), ((1, 1), (1, 1), (1, 1)), dimension_numbers=('NDHWC', 'DHWIO', 'NDHWC'), precision=lax.Precision.HIGHEST)
    return result[0]

def swish_slope(pre):
    logistic = jax.nn.sigmoid(pre)
    return logistic * (1.0 + pre * (1.0 - logistic))

def reference(volume, weight_first, weight_second, cotangent):
    kernel_first = weight_first.astype(jnp.float32).reshape(3, 3, 3, C0, C1)
    kernel_second = weight_second.astype(jnp.float32).reshape(3, 3, 3, C1, C1)
    pre_first, back_first = jax.vjp(lambda source, kernel: conv_full(source, kernel, 2), volume.astype(jnp.float32), kernel_first)
    hidden = lax.optimization_barrier(jax.nn.silu(pre_first).astype(jnp.bfloat16))
    pre_second, back_second = jax.vjp(lambda source, kernel: conv_full(source, kernel, 1), hidden.astype(jnp.float32), kernel_second)
    grad_second = lax.optimization_barrier((cotangent.astype(jnp.float32) * swish_slope(pre_second)).astype(jnp.bfloat16))
    hidden_grad, kernel_grad_second = back_second(grad_second.astype(jnp.float32))
    grad_first = lax.optimization_barrier((hidden_grad * swish_slope(pre_first)).astype(jnp.bfloat16))
    input_grad, kernel_grad_first = back_first(grad_first.astype(jnp.float32))
    return (input_grad.astype(jnp.bfloat16), kernel_grad_first.reshape(27, C0, C1), kernel_grad_second.reshape(27, C1, C1))
```

```python
import functools

import jax
import jax.numpy as jnp
from jax import lax
from jax.experimental import pallas as pl
from jax.experimental.pallas import tpu as pltpu
from jax.sharding import PartitionSpec as P

BF16 = jnp.bfloat16
F32 = jnp.float32
MESH = pl.DeviceIdType.MESH
NS = 64
NF = 4
HALF = 14


def place():
    s = lax.axis_index("space")
    f = lax.axis_index("filt")
    return s, f


def remote(src, dst, send, recv, s, f):
    return pltpu.make_async_remote_copy(
        src_ref=src,
        dst_ref=dst,
        send_sem=send,
        recv_sem=recv,
        device_id={"space": s, "filt": f},
        device_id_type=MESH,
    )


def greet(partners):
    barrier = pltpu.get_barrier_semaphore()
    total = 0
    for cond, s, f in partners:
        if cond is True:
            pl.semaphore_signal(barrier, inc=1, device_id={"space": s, "filt": f}, device_id_type=MESH)
            total = total + 1
        else:

            @pl.when(cond)
            def _():
                pl.semaphore_signal(barrier, inc=1, device_id={"space": s, "filt": f}, device_id_type=MESH)

            total = total + cond.astype(jnp.int32)
    pl.semaphore_wait(barrier, total)


def line_gather(own, main, outer, outer_own, outer_there, pair, zeros, sems, outer_both):
    out_send, out_recv, line_send, line_recv, oline_send, oline_recv, pair_send, pair_recv, local = sems
    s, f = place()
    core = s % 2
    mate = s + 1 - 2 * core
    outside = s - 1 + 2 * core
    has_outside = jnp.logical_and(outside >= 0, outside < NS)
    if outer_both:
        sends_out, gets_out, active = has_outside, has_outside, None
    else:
        sends_out = jnp.logical_and(has_outside, core == 1)
        gets_out = jnp.logical_and(has_outside, core == 0)
        active = core == 0
    right, left = f + 1, f - 1
    partners = [
        (f > 0, s, left),
        (f < NF - 1, s, right),
        (True, mate, f),
        (has_outside, outside, f),
    ]
    greet(partners)

    def when_active(cond):
        return cond if active is None else jnp.logical_and(active, cond)

    keep = pltpu.make_async_copy(own, main(f), local.at[0])
    keep.start()
    out_copy = remote(outer_own, outer_there, out_send.at[0], out_recv.at[0], outside, f)
    out_back = remote(outer_own, outer(f), out_send.at[0], out_recv.at[0], outside, f)

    @pl.when(sends_out)
    def _():
        out_copy.start()

    no_out = jnp.logical_not(gets_out)
    fill = pltpu.make_async_copy(zeros, outer(f), local.at[1])

    @pl.when(when_active(no_out))
    def _():
        fill.start()

    def line_copy(t, way, which, block):
        to = right if way == 0 else left
        snd, rcv = (line_send, line_recv) if which == 0 else (oline_send, oline_recv)
        view = (main if which == 0 else outer)(block)
        src = own if (which == 0 and t == 0) else view
        return remote(src, view, snd.at[way, t], rcv.at[way, t], s, to)

    def sent_block(t, way):
        return f - t if way == 0 else f + t

    def got_block(t, way):
        return f - 1 - t if way == 0 else f + 1 + t

    def may_send(t, way):
        if way == 0:
            return jnp.logical_and(f < NF - 1, f >= t)
        return jnp.logical_and(f > 0, f + t < NF)

    def may_get(t, way):
        return f > t if way == 0 else f + t < NF - 1

    def send(t, way, which):
        cond = may_send(t, way)

        @pl.when(cond if which == 0 else when_active(cond))
        def _():
            line_copy(t, way, which, sent_block(t, way)).start()

    def wait_send(t, way, which):
        cond = may_send(t, way)

        @pl.when(cond if which == 0 else when_active(cond))
        def _():
            line_copy(t, way, which, sent_block(t, way)).wait_send()

    def get(t, way, which):
        cond = may_get(t, way)

        @pl.when(cond if which == 0 else when_active(cond))
        def _():
            line_copy(t, way, which, got_block(t, way)).wait_recv()

    def pair_do(slot, block, cond, what):
        for c in range(2):
            ok = core == c
            if cond is not None:
                ok = jnp.logical_and(ok, cond)

            @pl.when(ok)
            def _():
                src, dst = pair(c, block)
                copy = remote(src, dst, pair_send.at[slot], pair_recv.at[slot], mate, f)
                if what == "start":
                    copy.start()
                else:
                    copy.wait_send()

            if what == "wait":
                ok = core == 1 - c
                if cond is not None:
                    ok = jnp.logical_and(ok, cond)

                @pl.when(ok)
                def _():
                    src, dst = pair(c, block)
                    remote(src, dst, pair_send.at[slot], pair_recv.at[slot], mate, f).wait_recv()

    for way in range(2):
        send(0, way, 0)
    keep.wait()
    pair_do(0, f, None, "start")

    @pl.when(sends_out)
    def _():
        out_copy.wait_send()

    @pl.when(gets_out)
    def _():
        out_back.wait_recv()

    @pl.when(when_active(no_out))
    def _():
        fill.wait()

    for way in range(2):
        send(0, way, 1)
    for t in range(NF - 1):
        for which in range(2):
            for way in range(2):
                get(t, way, which)
                if t < NF - 2:
                    send(t + 1, way, which)
                if which == 0:
                    pair_do(1 + 3 * way + t, got_block(t, way), may_get(t, way), "start")
    for t in range(NF - 1):
        for which in range(2):
            for way in range(2):
                wait_send(t, way, which)
    pair_do(0, f, None, "wait")
    for t in range(NF - 1):
        for way in range(2):
            pair_do(1 + 3 * way + t, got_block(t, way), may_get(t, way), "wait")


def line_sems():
    dma = pltpu.SemaphoreType.DMA
    return [dma((1,)), dma((1,)), dma((2, 3)), dma((2, 3)), dma((2, 3)), dma((2, 3)), dma((7,)), dma((7,)), dma((2,))]


def volume_kernel(v_ref, out_ref, zeros, *sems):
    s, f = place()
    core = s % 2
    cols = v_ref.shape[2]
    zeros[...] = jnp.zeros_like(zeros)

    def at(first, count, j):
        return out_ref.at[pl.ds(first, count), :, pl.ds(pl.multiple_of(cols * j, cols), cols), :]

    def pair(c, j):
        if c == 0:
            return at(1, 2, j), at(0, 2, j)
        return at(2, 1, j), at(3, 1, j)

    line_gather(
        v_ref,
        lambda j: at(1 + core, 2, j),
        lambda j: at(0, 1, j),
        v_ref.at[pl.ds(1, 1)],
        at(0, 1, f),
        pair,
        zeros,
        sems,
        False,
    )


def gather_volume(volume):
    planes, height, cols, chans = volume.shape
    return pl.pallas_call(
        volume_kernel,
        out_shape=jax.ShapeDtypeStruct((4, height, cols * NF, chans), BF16),
        in_specs=[pl.BlockSpec(memory_space=pl.ANY)],
        out_specs=pl.BlockSpec(memory_space=pl.ANY),
        scratch_shapes=[pltpu.VMEM((1, height, cols, chans), BF16)] + line_sems(),
        compiler_params=pltpu.CompilerParams(collective_id=0, has_side_effects=True),
        name="gather_volume",
    )(volume)


def hidden_kernel(h_ref, out_ref, zeros, *sems):
    s, f = place()
    core = s % 2
    width = h_ref.shape[1]
    zeros[...] = jnp.zeros_like(zeros)

    def at(plane, j):
        return out_ref.at[plane, :, pl.ds(pl.multiple_of(width * j, width), width)]

    line_gather(
        h_ref,
        lambda j: at(1, j),
        lambda j: at(2 * core, j),
        h_ref,
        at(2 - 2 * core, f),
        lambda c, j: (at(1, j), at(2 * c, j)),
        zeros,
        sems,
        True,
    )


def gather_hidden(hidden):
    rows, width = hidden.shape
    return pl.pallas_call(
        hidden_kernel,
        out_shape=jax.ShapeDtypeStruct((3, rows, width * NF), BF16),
        in_specs=[pl.BlockSpec(memory_space=pltpu.VMEM)],
        out_specs=pl.BlockSpec(memory_space=pltpu.VMEM),
        scratch_shapes=[pltpu.VMEM((rows, width), BF16)] + line_sems(),
        compiler_params=pltpu.CompilerParams(collective_id=1, has_side_effects=True),
        name="gather_hidden",
    )(hidden)


def terms_kernel(h3_ref, a1_ref, g2_ref, g1_ref, out_ref):
    core = lax.axis_index("space") % 2
    k = pl.program_id(0) + (HALF - 1) * core
    kz, ky, kx = k // 9, (k // 3) % 3, k % 3

    def product(source, grads):
        rows = source.shape[0] * source.shape[1]
        return lax.dot_general(
            source.reshape(rows, source.shape[2]), grads, (((0,), (0,)), ((), ())), preferred_element_type=F32
        )

    second = product(h3_ref[kx, kz, pl.ds(ky, 8)], g2_ref[0])
    second += product(h3_ref[kx, kz + 1 - 2 * core, pl.ds(ky, 8)], g2_ref[1])
    parity, start = (ky + 1) % 2, jnp.minimum(ky, 1)
    first = product(a1_ref[kx, kz + core, parity, pl.ds(start, 8)], g1_ref[0])
    first += product(a1_ref[kx, kz + 2 - 3 * core, parity, pl.ds(start, 8)], g1_ref[1])
    out_ref[0, :, :, 0:32, :] = second.reshape(4, 4, 32, 128).astype(BF16)
    out_ref[0, :, :, 32:48, :] = first.reshape(4, 4, 16, 128).astype(BF16)


def kernel_terms(h3, a1, g2, g1):
    def whole(x):
        return pl.BlockSpec(x.shape, lambda i: (0,) * x.ndim)

    return pl.pallas_call(
        terms_kernel,
        grid=(HALF,),
        out_shape=jax.ShapeDtypeStruct((HALF, 4, 4, 48, 128), BF16),
        in_specs=[whole(h3), whole(a1), whole(g2), whole(g1)],
        out_specs=pl.BlockSpec((1, 4, 4, 48, 128), lambda i: (i, 0, 0, 0, 0)),
        compiler_params=pltpu.CompilerParams(vmem_limit_bytes=40 * 2**20),
        name="kernel_terms",
    )(h3, a1, g2, g1)


def reduce_kernel(d_ref, out2_ref, out1_ref, r1x, r1y, ex, ey, r2x, r2y, total, t_send, r3, ss1, rs1, ss2, rs2, ss3, rs3):
    s, f = place()
    x, y, zh, core = s // 16, (s // 4) % 4, (s // 2) % 2, s % 2
    half = HALF // 2

    def dev(x_, y_, zh_, core_):
        return ((x_ * 4 + y_) * 2 + zh_) * 2 + core_

    xs = [(x + d) % 4 for d in (1, 2, 3)]
    ys = [(y + d) % 4 for d in (1, 2, 3)]
    ends = [(1 - zh, core), (zh, 1 - core), (1 - zh, 1 - core)]
    partners = [(True, dev(a, y, zh, core), f) for a in xs]
    partners += [(True, dev(x, b, zh, core), f) for b in ys]
    partners += [(True, dev(x, y, a, b), f) for a, b in ends]
    greet(partners)

    first = []
    for n in range(3):
        first.append(
            remote(d_ref.at[pl.ds(0, half), xs[n]], r1x.at[n], ss1.at[0, n], rs1.at[0, n], dev(xs[n], y, zh, core), f)
        )
        first.append(
            remote(d_ref.at[pl.ds(half, half), :, ys[n]], r1y.at[n], ss1.at[1, n], rs1.at[1, n], dev(x, ys[n], zh, core), f)
        )
    for copy in first:
        copy.start()
    for copy in first:
        copy.wait_recv()

    def sum_first(i, carry):
        acc = d_ref[i, x].astype(F32)
        for n in range(3):
            acc += r1x[n, i].astype(F32)
        ex[i] = acc.astype(BF16)
        acc = d_ref[half + i, :, y].astype(F32)
        for n in range(3):
            acc += r1y[n, i].astype(F32)
        ey[i] = acc.astype(BF16)
        return carry

    lax.fori_loop(0, half, sum_first, 0)
    second = []
    for n in range(3):
        second.append(remote(ex.at[:, ys[n]], r2x.at[n], ss2.at[0, n], rs2.at[0, n], dev(x, ys[n], zh, core), f))
        second.append(remote(ey.at[:, xs[n]], r2y.at[n], ss2.at[1, n], rs2.at[1, n], dev(xs[n], y, zh, core), f))
    for copy in second:
        copy.start()
    for copy in second:
        copy.wait_recv()

    def sum_second(i, carry):
        acc = ex[i, y].astype(F32)
        for n in range(3):
            acc += r2x[n, i].astype(F32)
        total[i] = acc
        acc = ey[i, x].astype(F32)
        for n in range(3):
            acc += r2y[n, i].astype(F32)
        total[half + i] = acc
        return carry

    lax.fori_loop(0, half, sum_second, 0)
    for a in range(2):
        for b in range(2):
            t_send[2 * a + b, :, 0:8] = total[:, 16 * a + 8 * b : 16 * a + 8 * b + 8]
            t_send[2 * a + b, :, 8:16] = total[:, 32 + 8 * a : 40 + 8 * a]
    third = []
    for n, (a, b) in enumerate(ends):
        third.append(remote(t_send.at[2 * a + b], r3.at[n], ss3.at[n], rs3.at[n], dev(x, y, a, b), f))
    for copy in third:
        copy.start()
    for copy in third:
        copy.wait_recv()
    mine = t_send[2 * zh + core] + r3[0]
    other = r3[1] + r3[2]
    low = jnp.where(core == 0, mine, other)
    high = jnp.where(core == 0, other, mine)
    out2_ref[0:HALF] = low[:, 0:8]
    out2_ref[HALF:27] = high[1:, 0:8]
    out1_ref[0:HALF] = jnp.where(core == 0, low[:, 8:12], low[:, 12:16])
    out1_ref[HALF:27] = jnp.where(core == 0, high[1:, 8:12], high[1:, 12:16])
    for copy in first + second + third:
        copy.wait_send()


def reduce_terms(terms):
    half = HALF // 2
    dma = pltpu.SemaphoreType.DMA
    vmem = pl.BlockSpec(memory_space=pltpu.VMEM)
    return pl.pallas_call(
        reduce_kernel,
        out_shape=(jax.ShapeDtypeStruct((27, 8, 128), F32), jax.ShapeDtypeStruct((27, 4, 128), F32)),
        in_specs=[vmem],
        out_specs=(vmem, vmem),
        scratch_shapes=[
            pltpu.VMEM((3, half, 4, 48, 128), BF16),
            pltpu.VMEM((3, half, 4, 48, 128), BF16),
            pltpu.VMEM((half, 4, 48, 128), BF16),
            pltpu.VMEM((half, 4, 48, 128), BF16),
            pltpu.VMEM((3, half, 48, 128), BF16),
            pltpu.VMEM((3, half, 48, 128), BF16),
            pltpu.VMEM((HALF, 48, 128), F32),
            pltpu.VMEM((4, HALF, 16, 128), F32),
            pltpu.VMEM((3, HALF, 16, 128), F32),
            dma((2, 3)),
            dma((2, 3)),
            dma((2, 3)),
            dma((2, 3)),
            dma((3,)),
            dma((3,)),
        ],
        compiler_params=pltpu.CompilerParams(collective_id=2, has_side_effects=True, vmem_limit_bytes=40 * 2**20),
        name="reduce_terms",
    )(terms)


def from_behind(x, axis, by):
    count = lax.axis_size(axis)
    pairs = [(i, i + by) for i in range(count) if 0 <= i + by < count]
    return lax.ppermute(x, axis, pairs)


def convolve(source, kernel, stride, padding, dilation):
    result = lax.conv_general_dilated(
        source[None],
        kernel,
        (stride, stride, stride),
        padding,
        lhs_dilation=(dilation, dilation, dilation),
        dimension_numbers=("NDHWC", "DHWIO", "NDHWC"),
        preferred_element_type=F32,
    )
    return result[0]


def swish_slope(pre):
    logistic = jax.nn.sigmoid(pre)
    return logistic * (1.0 + pre * (1.0 - logistic))


def per_device(volume, weight_first, weight_second, cotangent):
    core = lax.axis_index("space") % 2
    kernel_first = weight_first.reshape(3, 3, 3, 256, 128)
    kernel_second = weight_second.reshape(3, 3, 3, 512, 128)
    planes = gather_volume(volume)
    extended = lax.dynamic_slice_in_dim(planes, core, 3, axis=0)
    pre_first = convolve(extended, kernel_first, 2, ((0, 0), (1, 1), (1, 1)), 1)
    hidden = jax.nn.silu(pre_first).astype(BF16)
    hidden_ext = gather_hidden(hidden.reshape(256, 128)).reshape(3, 8, 32, 512)
    pre_second = convolve(hidden_ext, kernel_second, 1, ((0, 0), (1, 1), (1, 1)), 1)
    grad_second = (cotangent.astype(F32) * swish_slope(pre_second)).astype(BF16)
    grad_ext = jnp.concatenate(
        [from_behind(grad_second, "space", 1), grad_second, from_behind(grad_second, "space", -1)], axis=0
    )
    flipped_second = jnp.swapaxes(kernel_second[::-1, ::-1, ::-1], 3, 4)
    hidden_partial = convolve(grad_ext, flipped_second, 1, ((0, 0), (1, 1), (1, 1)), 1)
    hidden_grad = lax.psum_scatter(hidden_partial.astype(BF16), "filt", scatter_dimension=3, tiled=True).astype(F32)
    grad_first = (hidden_grad * swish_slope(pre_first)).astype(BF16)
    before, after = from_behind(grad_first, "space", 1), from_behind(grad_first, "space", -1)
    mate_first = jnp.where(core == 0, after, before)
    mate_second = lax.dynamic_slice_in_dim(grad_ext, 2 - 2 * core, 1, axis=0)

    wide = jnp.pad(hidden_ext, ((0, 0), (1, 1), (1, 1), (0, 0)))
    h3 = jnp.stack([wide[:, :, i : i + 32] for i in range(3)])
    cells = planes.reshape(4, 8, 2, 32, 2, 256).transpose(4, 0, 2, 1, 3, 5)
    odd, even = cells[1], cells[0]
    shifted = jnp.pad(odd, ((0, 0), (0, 0), (0, 0), (1, 0), (0, 0)))[:, :, :, :32]
    a1 = jnp.pad(jnp.stack([shifted, even, odd]), ((0, 0), (0, 0), (0, 0), (1, 0), (0, 0), (0, 0)))
    g2 = jnp.concatenate([grad_second, mate_second], axis=0).reshape(2, 256, 128)
    g1 = jnp.concatenate([grad_first, mate_first], axis=0).reshape(2, 256, 128)
    grad_weight_second, grad_weight_first = reduce_terms(kernel_terms(h3, a1, g2, g1))

    flipped_first = jnp.swapaxes(kernel_first[::-1, ::-1, ::-1], 3, 4)
    input_partial = convolve(
        jnp.concatenate([grad_first, after], axis=0), flipped_first, 1, ((1, 0), (1, 2), (1, 2)), 2
    )
    grad_volume = lax.psum_scatter(input_partial.astype(BF16), "filt", scatter_dimension=2, tiled=True)
    return (grad_volume, grad_weight_first, grad_weight_second)


def solution(mesh):
    placed = (
        P("space", None, "filt", None),
        P(None, None, "filt"),
        P(None, None, "filt"),
        P("space", None, None, "filt"),
    )
    return jax.shard_map(
        per_device,
        mesh=mesh,
        in_specs=placed,
        out_specs=(
            P("space", None, "filt", None),
            P(None, "space", "filt"),
            P(None, "space", "filt"),
        ),
        check_vma=False,
    )
```

```python
import functools

import jax
import jax.numpy as jnp
from jax import lax
from jax.experimental import pallas as pl
from jax.experimental.pallas import tpu as pltpu
from jax.sharding import PartitionSpec as P

BF16 = jnp.bfloat16
F32 = jnp.float32
MESH = pl.DeviceIdType.MESH
NS = 64
NF = 4
HALF = 14


def place():
    s = lax.axis_index("space")
    f = lax.axis_index("filt")
    return s, f


def remote(src, dst, send, recv, s, f):
    return pltpu.make_async_remote_copy(
        src_ref=src,
        dst_ref=dst,
        send_sem=send,
        recv_sem=recv,
        device_id={"space": s, "filt": f},
        device_id_type=MESH,
    )


def greet(partners):
    barrier = pltpu.get_barrier_semaphore()
    total = 0
    for cond, s, f in partners:
        if cond is True:
            pl.semaphore_signal(barrier, inc=1, device_id={"space": s, "filt": f}, device_id_type=MESH)
            total = total + 1
        else:

            @pl.when(cond)
            def _():
                pl.semaphore_signal(barrier, inc=1, device_id={"space": s, "filt": f}, device_id_type=MESH)

            total = total + cond.astype(jnp.int32)
    pl.semaphore_wait(barrier, total)


def line_gather(own, main, outer, outer_own, outer_there, pair, zeros, sems, outer_both):
    out_send, out_recv, line_send, line_recv, oline_send, oline_recv, pair_send, pair_recv, local = sems
    s, f = place()
    core = s % 2
    mate = s + 1 - 2 * core
    outside = s - 1 + 2 * core
    has_outside = jnp.logical_and(outside >= 0, outside < NS)
    if outer_both:
        sends_out, gets_out, active = has_outside, has_outside, None
    else:
        sends_out = jnp.logical_and(has_outside, core == 1)
        gets_out = jnp.logical_and(has_outside, core == 0)
        active = core == 0
    right, left = f + 1, f - 1
    def when_active(cond):
        return cond if active is None else jnp.logical_and(active, cond)

    keep = pltpu.make_async_copy(own, main(f), local.at[0])
    keep.start()
    out_copy = remote(outer_own, outer_there, out_send.at[0], out_recv.at[0], outside, f)
    out_back = remote(outer_own, outer(f), out_send.at[0], out_recv.at[0], outside, f)

    @pl.when(sends_out)
    def _():
        out_copy.start()

    no_out = jnp.logical_not(gets_out)
    fill = pltpu.make_async_copy(zeros, outer(f), local.at[1])

    @pl.when(when_active(no_out))
    def _():
        fill.start()

    def line_copy(t, way, which, block):
        to = right if way == 0 else left
        snd, rcv = (line_send, line_recv) if which == 0 else (oline_send, oline_recv)
        view = (main if which == 0 else outer)(block)
        src = own if (which == 0 and t == 0) else view
        return remote(src, view, snd.at[way, t], rcv.at[way, t], s, to)

    def sent_block(t, way):
        return f - t if way == 0 else f + t

    def got_block(t, way):
        return f - 1 - t if way == 0 else f + 1 + t

    def may_send(t, way):
        if way == 0:
            return jnp.logical_and(f < NF - 1, f >= t)
        return jnp.logical_and(f > 0, f + t < NF)

    def may_get(t, way):
        return f > t if way == 0 else f + t < NF - 1

    def send(t, way, which):
        cond = may_send(t, way)

        @pl.when(cond if which == 0 else when_active(cond))
        def _():
            line_copy(t, way, which, sent_block(t, way)).start()

    def wait_send(t, way, which):
        cond = may_send(t, way)

        @pl.when(cond if which == 0 else when_active(cond))
        def _():
            line_copy(t, way, which, sent_block(t, way)).wait_send()

    def get(t, way, which):
        cond = may_get(t, way)

        @pl.when(cond if which == 0 else when_active(cond))
        def _():
            line_copy(t, way, which, got_block(t, way)).wait_recv()

    def pair_do(slot, block, cond, what):
        for c in range(2):
            ok = core == c
            if cond is not None:
                ok = jnp.logical_and(ok, cond)

            @pl.when(ok)
            def _():
                src, dst = pair(c, block)
                copy = remote(src, dst, pair_send.at[slot], pair_recv.at[slot], mate, f)
                if what == "start":
                    copy.start()
                else:
                    copy.wait_send()

            if what == "wait":
                ok = core == 1 - c
                if cond is not None:
                    ok = jnp.logical_and(ok, cond)

                @pl.when(ok)
                def _():
                    src, dst = pair(c, block)
                    remote(src, dst, pair_send.at[slot], pair_recv.at[slot], mate, f).wait_recv()

    for way in range(2):
        send(0, way, 0)
    keep.wait()
    pair_do(0, f, None, "start")

    @pl.when(sends_out)
    def _():
        out_copy.wait_send()

    @pl.when(gets_out)
    def _():
        out_back.wait_recv()

    @pl.when(when_active(no_out))
    def _():
        fill.wait()

    for way in range(2):
        send(0, way, 1)
    for t in range(NF - 1):
        for which in range(2):
            for way in range(2):
                get(t, way, which)
                if t < NF - 2:
                    send(t + 1, way, which)
                if which == 0:
                    pair_do(1 + 3 * way + t, got_block(t, way), may_get(t, way), "start")
    for t in range(NF - 1):
        for which in range(2):
            for way in range(2):
                wait_send(t, way, which)
    pair_do(0, f, None, "wait")
    for t in range(NF - 1):
        for way in range(2):
            pair_do(1 + 3 * way + t, got_block(t, way), may_get(t, way), "wait")


def line_sems():
    dma = pltpu.SemaphoreType.DMA
    return [dma((1,)), dma((1,)), dma((2, 3)), dma((2, 3)), dma((2, 3)), dma((2, 3)), dma((7,)), dma((7,)), dma((2,))]


class Reduction:
    def __init__(self, rows, d, r1x, r1y, ex, ey, r2x, r2y, total, t_send, r3, send, recv):
        self.rows, self.d, self.r1x, self.r1y, self.ex, self.ey = rows, d, r1x, r1y, ex, ey
        self.r2x, self.r2y, self.total, self.t_send, self.r3 = r2x, r2y, total, t_send, r3
        self.send, self.recv = send, recv
        self.s, self.f = place()
        s = self.s
        self.x, self.y, self.zh, self.core = s // 16, (s // 4) % 4, (s // 2) % 2, s % 2
        self.xs = [(self.x + n) % 4 for n in (1, 2, 3)]
        self.ys = [(self.y + n) % 4 for n in (1, 2, 3)]
        self.ends = [(1 - self.zh, self.core), (self.zh, 1 - self.core), (1 - self.zh, 1 - self.core)]
        self.copies = []

    def copy(self, src, dst, stage, way, n, x, y, zh, core):
        to = ((x * 4 + y) * 2 + zh) * 2 + core
        return remote(src, dst, self.send.at[stage, way, n], self.recv.at[stage, way, n], to, self.f)

    def start_first(self):
        half = HALF // 2
        self.first = []
        for n in range(3):
            a, b = self.xs[n], self.ys[n]
            self.first.append(
                self.copy(self.d.at[pl.ds(0, half), a], self.r1x.at[n], 0, 0, n, a, self.y, self.zh, self.core)
            )
            self.first.append(
                self.copy(self.d.at[pl.ds(half, half), :, b], self.r1y.at[n], 0, 1, n, self.x, b, self.zh, self.core)
            )
        for c in self.first:
            c.start()

    def start_second(self):
        half = HALF // 2
        for c in self.first:
            c.wait_recv()
        d, x, y = self.d, self.x, self.y

        def body(i, carry):
            acc = d[i, x].astype(F32)
            for n in range(3):
                acc += self.r1x[n, i].astype(F32)
            self.ex[i] = acc.astype(BF16)
            acc = d[half + i, :, y].astype(F32)
            for n in range(3):
                acc += self.r1y[n, i].astype(F32)
            self.ey[i] = acc.astype(BF16)
            return carry

        lax.fori_loop(0, half, body, 0)
        self.second = []
        for n in range(3):
            a, b = self.xs[n], self.ys[n]
            self.second.append(self.copy(self.ex.at[:, b], self.r2x.at[n], 1, 0, n, x, b, self.zh, self.core))
            self.second.append(self.copy(self.ey.at[:, a], self.r2y.at[n], 1, 1, n, a, y, self.zh, self.core))
        for c in self.second:
            c.start()

    def start_third(self):
        half = HALF // 2
        for c in self.second:
            c.wait_recv()
        x, y = self.x, self.y

        def body(i, carry):
            acc = self.ex[i, y].astype(F32)
            for n in range(3):
                acc += self.r2x[n, i].astype(F32)
            self.total[i] = acc
            acc = self.ey[i, x].astype(F32)
            for n in range(3):
                acc += self.r2y[n, i].astype(F32)
            self.total[half + i] = acc
            return carry

        lax.fori_loop(0, half, body, 0)
        for a in range(2):
            for b in range(2):
                start = 16 * a + 8 * b if self.rows == 32 else 8 * a
                piece = self.total[:, start : start + 8]
                self.t_send[2 * a + b] = piece.reshape(half, 16, 128).astype(BF16)
        self.third = []
        for n, (a, b) in enumerate(self.ends):
            self.third.append(self.copy(self.t_send.at[2 * a + b], self.r3.at[n], 2, 0, n, x, y, a, b))
        for c in self.third:
            c.start()

    def finish(self):
        for c in self.third:
            c.wait_recv()
        start = 16 * self.zh + 8 * self.core if self.rows == 32 else 8 * self.zh
        got = [self.r3[n].astype(F32).reshape(HALF, 8, 128) for n in range(3)]
        mine = self.total[:, pl.ds(pl.multiple_of(start, 8), 8)] + got[0]
        other = got[1] + got[2]
        low = jnp.where(self.core == 0, mine, other)
        high = jnp.where(self.core == 0, other, mine)
        for c in self.first + self.second + self.third:
            c.wait_send()
        return low, high[1:]


def reduction_scratch(rows):
    half = HALF // 2
    dma = pltpu.SemaphoreType.DMA
    return [
        pltpu.VMEM((HALF, 4, 4, rows, 128), BF16),
        pltpu.VMEM((3, half, 4, rows, 128), BF16),
        pltpu.VMEM((3, half, 4, rows, 128), BF16),
        pltpu.VMEM((half, 4, rows, 128), BF16),
        pltpu.VMEM((half, 4, rows, 128), BF16),
        pltpu.VMEM((3, half, rows, 128), BF16),
        pltpu.VMEM((3, half, rows, 128), BF16),
        pltpu.VMEM((HALF, rows, 128), F32),
        pltpu.VMEM((4, half, 16, 128), BF16),
        pltpu.VMEM((3, half, 16, 128), BF16),
        dma((3, 2, 3)),
        dma((3, 2, 3)),
    ]


def swish_slope(pre):
    logistic = jax.nn.sigmoid(pre)
    return logistic * (1.0 + pre * (1.0 - logistic))


def dot_nn(a, b):
    return lax.dot_general(a, b, (((1,), (0,)), ((), ())), preferred_element_type=F32)


def dot_nt(a, b):
    return lax.dot_general(a, b, (((1,), (1,)), ((), ())), preferred_element_type=F32)


def dot_tn(a, b):
    return lax.dot_general(a, b, (((0,), (0,)), ((), ())), preferred_element_type=F32)


def rows_from(start):
    return pl.ds(pl.multiple_of(start, 32), 256)


def whole_kernel(
    v_ref, w1_hbm, w2_hbm, cot_ref, gin_ref, gw1_ref, gw2_ref,
    w1, w2, wsem, vg, t1, a1, pre1, hown, hg, t2, h3, zeros_v, zeros_h,
    gs, t3, g3, gsem_s, gsem_r, hp, ps, rp, psem_s, psem_r, gf, gfsem_s, gfsem_r, g4, s5, r5, s5_s, s5_r,
    *rest,
):
    nsem = 9
    vsems, hsems = rest[:nsem], rest[nsem : 2 * nsem]
    red2 = Reduction(32, *rest[2 * nsem : 2 * nsem + 12])
    red1 = Reduction(16, *rest[2 * nsem + 12 :])
    s, f = place()
    core, zh = s % 2, (s // 2) % 2
    mate = s + 1 - 2 * core
    outside = s - 1 + 2 * core
    has_outside = jnp.logical_and(outside >= 0, outside < NS)
    peers = [(f + n) % NF for n in (1, 2, 3)]

    load1 = pltpu.make_async_copy(w1_hbm, w1, wsem.at[0])
    load2 = pltpu.make_async_copy(w2_hbm, w2, wsem.at[1])
    load1.start()
    load2.start()

    def dev(x_, y_, zh_, core_):
        return ((x_ * 4 + y_) * 2 + zh_) * 2 + core_

    partners = [(True, s, p) for p in peers]
    partners += [(True, mate, f), (has_outside, outside, f)]
    partners += [(True, dev(a, red2.y, zh, core), f) for a in red2.xs]
    partners += [(True, dev(red2.x, b, zh, core), f) for b in red2.ys]
    partners += [(True, dev(red2.x, red2.y, 1 - zh, b), f) for b in (core, 1 - core)]
    greet(partners)

    zeros_v[...] = jnp.zeros_like(zeros_v)
    zeros_h[...] = jnp.zeros_like(zeros_h)

    def vol(first, count, j):
        return vg.at[pl.ds(first, count), :, j]

    def vol_pair(c, j):
        if c == 0:
            return vol(1, 2, j), vol(0, 2, j)
        return vol(2, 1, j), vol(3, 1, j)

    line_gather(
        v_ref,
        lambda j: vol(1 + core, 2, j),
        lambda j: vol(0, 1, j),
        v_ref.at[pl.ds(1, 1)],
        vol(0, 1, f),
        vol_pair,
        zeros_v,
        vsems,
        False,
    )

    t1[:, 0:8, :] = jnp.zeros((8, 8, 512), F32)

    def cells(i, carry):
        plane, parity = i // 2, i % 2
        for j in range(NF):
            t1[:, 8 + 8 * j : 16 + 8 * j, :] = vg[plane, parity, j].astype(F32).reshape(8, 8, 512)
        edge = jnp.zeros((32, 256), BF16)
        for kx in range(3):
            a1[kx, plane, parity, 0:32] = edge
        a1[0, plane, parity, 32:288] = t1[:, 7:39, 256:512].reshape(256, 256).astype(BF16)
        a1[1, plane, parity, 32:288] = t1[:, 8:40, 0:256].reshape(256, 256).astype(BF16)
        a1[2, plane, parity, 32:288] = t1[:, 8:40, 256:512].reshape(256, 256).astype(BF16)
        return carry

    lax.fori_loop(0, 8, cells, 0)
    load1.wait()

    def conv_first(i, acc):
        kz, ky = i // 3, i % 3
        parity, start = (ky + 1) % 2, jnp.minimum(ky, 1)
        for kx in range(3):
            acc += dot_nn(a1[kx, kz + core, parity, rows_from(32 * start)], w1[3 * i + kx])
        return acc

    pre_first = lax.fori_loop(0, 9, conv_first, jnp.zeros((256, 128), F32))
    pre1[...] = pre_first
    hown[...] = (pre_first * jax.nn.sigmoid(pre_first)).astype(BF16)

    def hid(plane, j):
        return hg.at[plane, :, pl.ds(pl.multiple_of(128 * j, 128), 128)]

    line_gather(
        hown,
        lambda j: hid(1, j),
        lambda j: hid(2 * core, j),
        hown,
        hid(2 - 2 * core, f),
        lambda c, j: (hid(1, j), hid(2 * c, j)),
        zeros_h,
        hsems,
        True,
    )

    t2[:, 0:8, :] = jnp.zeros((8, 8, 512), F32)
    t2[:, 40:48, :] = jnp.zeros((8, 8, 512), F32)

    def spread_hidden(i, carry):
        t2[:, 8:40, :] = hg[i].astype(F32).reshape(8, 32, 512)
        edge = jnp.zeros((32, 512), BF16)
        for kx in range(3):
            h3[kx, i, 0:32] = edge
            h3[kx, i, 288:320] = edge
        h3[0, i, 32:288] = t2[:, 7:39, :].reshape(256, 512).astype(BF16)
        h3[1, i, 32:288] = hg[i]
        h3[2, i, 32:288] = t2[:, 9:41, :].reshape(256, 512).astype(BF16)
        return carry

    lax.fori_loop(0, 3, spread_hidden, 0)
    load2.wait()

    def conv_second(i, acc):
        kz, ky = i // 3, i % 3
        for kx in range(3):
            acc += dot_nn(h3[kx, kz, rows_from(32 * ky)], w2[3 * i + kx])
        return acc

    pre_second = lax.fori_loop(0, 9, conv_second, jnp.zeros((256, 128), F32))
    gs[1] = (cot_ref[...].astype(F32) * swish_slope(pre_second)).astype(BF16)

    def swap(place_there, to, slot):
        return remote(gs.at[1], gs.at[place_there], gsem_s.at[slot], gsem_r.at[slot], to, f)

    to_mate = swap(2 * core, mate, 0)
    to_out = swap(2 - 2 * core, outside, 1)
    from_mate = swap(2 - 2 * core, mate, 0)
    from_out = swap(2 * core, outside, 1)
    to_mate.start()

    @pl.when(has_outside)
    def _():
        to_out.start()

    @pl.when(jnp.logical_not(has_outside))
    def _():
        gs[2 * core] = jnp.zeros((256, 128), BF16)

    t3[:, 0:8, :] = jnp.zeros((8, 8, 128), F32)
    t3[:, 40:48, :] = jnp.zeros((8, 8, 128), F32)

    def spread_grads(i):
        t3[:, 8:40, :] = gs[i].astype(F32).reshape(8, 32, 128)
        edge = jnp.zeros((32, 128), BF16)
        for kx in range(3):
            g3[kx, i, 0:32] = edge
            g3[kx, i, 288:320] = edge
        g3[0, i, 32:288] = t3[:, 9:41, :].reshape(256, 128).astype(BF16)
        g3[1, i, 32:288] = gs[i]
        g3[2, i, 32:288] = t3[:, 7:39, :].reshape(256, 128).astype(BF16)

    def back_second(plane, kz, first):
        def body(ky, carry):
            acc = hp[...]
            for kx in range(3):
                acc += dot_nt(g3[kx, plane, rows_from(32 * (2 - ky))], w2[9 * kz + 3 * ky + kx])
            hp[...] = acc
            return carry

        if first:
            hp[...] = jnp.zeros((256, 512), F32)
        lax.fori_loop(0, 3, body, 0)

    spread_grads(1)
    back_second(1, 1, True)
    from_mate.wait_recv()

    @pl.when(has_outside)
    def _():
        from_out.wait_recv()

    spread_grads(0)
    spread_grads(2)
    back_second(0, 2, False)
    back_second(2, 0, False)

    for j in range(NF):
        ps[j] = hp[:, 128 * j : 128 * j + 128].astype(BF16)
    shares = [remote(ps.at[p], rp.at[n], psem_s.at[n], psem_r.at[n], s, p) for n, p in enumerate(peers)]
    for c in shares:
        c.start()

    grads_own, grads_mate = gs[1], gs[2 - 2 * core]

    def terms_second(i, carry):
        k = i + (HALF - 1) * core
        kz, ky, kx = k // 9, (k // 3) % 3, k % 3
        acc = dot_tn(h3[kx, kz, rows_from(32 * ky)], grads_own)
        acc += dot_tn(h3[kx, kz + 1 - 2 * core, rows_from(32 * ky)], grads_mate)
        red2.d[i] = acc.reshape(4, 4, 32, 128).astype(BF16)
        return carry

    lax.fori_loop(0, HALF, terms_second, 0)
    red2.start_first()

    for c in shares:
        c.wait_recv()
    hidden_grad = ps[f].astype(F32)
    for n in range(3):
        hidden_grad += rp[n].astype(F32)
    gf[0] = (hidden_grad * swish_slope(pre1[...])).astype(BF16)

    gf_mate = remote(gf.at[0], gf.at[1], gfsem_s.at[0], gfsem_r.at[0], mate, f)
    gf_out = remote(gf.at[0], gf.at[2], gfsem_s.at[1], gfsem_r.at[1], outside, f)
    gf_mate.start()
    sends = jnp.logical_and(core == 0, has_outside)
    gets = jnp.logical_and(core == 1, has_outside)

    @pl.when(sends)
    def _():
        gf_out.start()

    t3[:, 40:48, :] = jnp.zeros((8, 8, 128), F32)

    def spread_first(z, src):
        t3[:, 8:40, :] = src.astype(F32).reshape(8, 32, 128)
        g4[0, z, 0:256] = src
        g4[1, z, 0:256] = t3[:, 9:41, :].reshape(256, 128).astype(BF16)
        for i in range(2):
            g4[i, z, 256:288] = jnp.zeros((32, 128), BF16)

    def taps(parity):
        return [(1, 0)] if parity == 0 else [(2, 0), (0, 1)]

    def back_first(zp):
        for yp in range(2):
            for xp in range(2):
                acc = None
                for kz, oz in taps(zp):
                    for ky, oy in taps(yp):
                        for kx, ox in taps(xp):
                            term = dot_nt(g4[ox, oz, 32 * oy : 32 * oy + 256], w1[9 * kz + 3 * ky + kx])
                            acc = term if acc is None else acc + term
                acc = acc.reshape(8, 32, 256)
                for j in range(NF):
                    part = acc[:, 8 * j : 8 * j + 8, :].reshape(64, 256)
                    s5[j, zp, yp, :, 256 * xp : 256 * xp + 256] = part.astype(BF16)

    def share(zp):
        return [
            remote(s5.at[p, zp], r5.at[n, zp], s5_s.at[zp, n], s5_r.at[zp, n], s, p) for n, p in enumerate(peers)
        ]

    spread_first(0, gf[0])
    back_first(0)
    even = share(0)
    for c in even:
        c.start()
    gf_mate.wait_recv()

    @pl.when(gets)
    def _():
        gf_out.wait_recv()

    @pl.when(jnp.logical_and(core == 1, jnp.logical_not(has_outside)))
    def _():
        gf[2] = jnp.zeros((256, 128), BF16)

    spread_first(1, gf[1 + core])
    back_first(1)
    odd = share(1)
    for c in odd:
        c.start()

    first_own, first_mate = gf[0], gf[1]

    def terms_first(i, carry):
        k = i + (HALF - 1) * core
        kz, ky, kx = k // 9, (k // 3) % 3, k % 3
        parity, start = (ky + 1) % 2, jnp.minimum(ky, 1)
        acc = dot_tn(a1[kx, kz + core, parity, rows_from(32 * start)], first_own)
        acc += dot_tn(a1[kx, kz + 2 - 3 * core, parity, rows_from(32 * start)], first_mate)
        red1.d[i] = acc.reshape(4, 4, 16, 128).astype(BF16)
        return carry

    lax.fori_loop(0, HALF, terms_first, 0)
    red1.start_first()
    red2.start_second()
    red2.start_third()
    red1.start_second()
    red1.start_third()
    low, high = red2.finish()
    gw2_ref[0:HALF] = low
    gw2_ref[HALF:27] = high
    low, high = red1.finish()
    gw1_ref[0:HALF] = jnp.where(core == 0, low[:, 0:4], low[:, 4:8])
    gw1_ref[HALF:27] = jnp.where(core == 0, high[:, 0:4], high[:, 4:8])

    for zp, copies in enumerate((even, odd)):
        for c in copies:
            c.wait_recv()
        acc = s5[f, zp].astype(F32)
        for n in range(3):
            acc += r5[n, zp].astype(F32)
        gin_ref[zp] = acc.astype(BF16)
    for c in shares + even + odd:
        c.wait_send()
    to_mate.wait_send()
    gf_mate.wait_send()

    @pl.when(has_outside)
    def _():
        to_out.wait_send()

    @pl.when(sends)
    def _():
        gf_out.wait_send()


def run_whole(cells, weight_first, weight_second, cotangent):
    dma = pltpu.SemaphoreType.DMA
    vmem, anywhere = pl.BlockSpec(memory_space=pltpu.VMEM), pl.BlockSpec(memory_space=pl.ANY)
    scratch = [
        pltpu.VMEM((27, 256, 128), BF16),
        pltpu.VMEM((27, 512, 128), BF16),
        dma((2,)),
        pltpu.VMEM((4, 2, NF, 64, 512), BF16),
        pltpu.VMEM((8, 40, 512), F32),
        pltpu.VMEM((3, 4, 2, 288, 256), BF16),
        pltpu.VMEM((256, 128), F32),
        pltpu.VMEM((256, 128), BF16),
        pltpu.VMEM((3, 256, 512), BF16),
        pltpu.VMEM((8, 48, 512), F32),
        pltpu.VMEM((3, 3, 320, 512), BF16),
        pltpu.VMEM((1, 2, 64, 512), BF16),
        pltpu.VMEM((256, 128), BF16),
        pltpu.VMEM((3, 256, 128), BF16),
        pltpu.VMEM((8, 48, 128), F32),
        pltpu.VMEM((3, 3, 320, 128), BF16),
        dma((2,)),
        dma((2,)),
        pltpu.VMEM((256, 512), F32),
        pltpu.VMEM((NF, 256, 128), BF16),
        pltpu.VMEM((3, 256, 128), BF16),
        dma((3,)),
        dma((3,)),
        pltpu.VMEM((3, 256, 128), BF16),
        dma((2,)),
        dma((2,)),
        pltpu.VMEM((2, 2, 288, 128), BF16),
        pltpu.VMEM((NF, 2, 2, 64, 512), BF16),
        pltpu.VMEM((3, 2, 2, 64, 512), BF16),
        dma((2, 3)),
        dma((2, 3)),
    ]
    scratch += line_sems() + line_sems() + reduction_scratch(32) + reduction_scratch(16)
    return pl.pallas_call(
        whole_kernel,
        out_shape=(
            jax.ShapeDtypeStruct((2, 2, 64, 512), BF16),
            jax.ShapeDtypeStruct((27, 4, 128), F32),
            jax.ShapeDtypeStruct((27, 8, 128), F32),
        ),
        in_specs=[vmem, anywhere, anywhere, vmem],
        out_specs=(vmem, vmem, vmem),
        scratch_shapes=scratch,
        compiler_params=pltpu.CompilerParams(collective_id=0, has_side_effects=True, vmem_limit_bytes=52 * 2**20),
        name="bottleneck",
    )(cells, weight_first, weight_second, cotangent)


def per_device(volume, weight_first, weight_second, cotangent):
    cells = volume.reshape(2, 8, 2, 8, 2, 256).transpose(0, 2, 1, 3, 4, 5).reshape(2, 2, 64, 512)
    grad, grad_first, grad_second = run_whole(cells, weight_first, weight_second, cotangent.reshape(256, 128))
    grad = grad.reshape(2, 2, 8, 8, 2, 256).transpose(0, 2, 1, 3, 4, 5).reshape(2, 16, 16, 256)
    return (grad, grad_first, grad_second)


def solution(mesh):
    placed = (
        P("space", None, "filt", None),
        P(None, None, "filt"),
        P(None, None, "filt"),
        P("space", None, None, "filt"),
    )
    return jax.shard_map(
        per_device,
        mesh=mesh,
        in_specs=placed,
        out_specs=(
            P("space", None, "filt", None),
            P(None, "space", "filt"),
            P(None, "space", "filt"),
        ),
        check_vma=False,
    )
```

```python
import functools

import jax
import jax.numpy as jnp
from jax import lax
from jax.experimental import pallas as pl
from jax.experimental.pallas import tpu as pltpu
from jax.sharding import PartitionSpec as P

BF16 = jnp.bfloat16
F32 = jnp.float32
MESH = pl.DeviceIdType.MESH
NS = 64
NF = 4
HALF = 14


def place():
    s = lax.axis_index("space")
    f = lax.axis_index("filt")
    return s, f


def remote(src, dst, send, recv, s, f):
    return pltpu.make_async_remote_copy(
        src_ref=src,
        dst_ref=dst,
        send_sem=send,
        recv_sem=recv,
        device_id={"space": s, "filt": f},
        device_id_type=MESH,
    )


def greet(partners):
    barrier = pltpu.get_barrier_semaphore()
    total = 0
    for cond, s, f in partners:
        if cond is True:
            pl.semaphore_signal(barrier, inc=1, device_id={"space": s, "filt": f}, device_id_type=MESH)
            total = total + 1
        else:

            @pl.when(cond)
            def _():
                pl.semaphore_signal(barrier, inc=1, device_id={"space": s, "filt": f}, device_id_type=MESH)

            total = total + cond.astype(jnp.int32)
    pl.semaphore_wait(barrier, total)


def line_gather(own, main, sems, work=()):
    line_send, line_recv, pair_send, pair_recv, local = sems
    s, f = place()
    core = s % 2
    mate = s + 1 - 2 * core

    keep = pltpu.make_async_copy(own, main(f), local.at[0])
    keep.start()

    def line_copy(t, way, block):
        to = f + 1 if way == 0 else f - 1
        view = main(block)
        return remote(own if t == 0 else view, view, line_send.at[way, t], line_recv.at[way, t], s, to)

    def sent_block(t, way):
        return f - t if way == 0 else f + t

    def got_block(t, way):
        return f - 1 - t if way == 0 else f + 1 + t

    def may_send(t, way):
        if way == 0:
            return jnp.logical_and(f < NF - 1, f >= t)
        return jnp.logical_and(f > 0, f + t < NF)

    def may_get(t, way):
        return f > t if way == 0 else f + t < NF - 1

    def send(t, way):
        @pl.when(may_send(t, way))
        def _():
            line_copy(t, way, sent_block(t, way)).start()

    def get(t, way):
        @pl.when(may_get(t, way))
        def _():
            line_copy(t, way, got_block(t, way)).wait_recv()

    def pair_copy(slot, view):
        return remote(view, view, pair_send.at[slot], pair_recv.at[slot], mate, f)

    def pair_start(t, way):
        @pl.when(may_get(t, way))
        def _():
            pair_copy(1 + 3 * way + t, main(got_block(t, way))).start()

    for way in range(2):
        send(0, way)
    keep.wait()
    pair_copy(0, main(f)).start()
    for job in work[:1]:
        job()
    for t in range(NF - 1):
        for way in range(2):
            get(t, way)
            if t < NF - 2:
                send(t + 1, way)
            pair_start(t, way)
        for job in work[1 + t : 2 + t]:
            job()

    def wait_pair(theirs):
        pair_copy(0, theirs(f)).wait_recv()
        for t in range(NF - 1):
            for way in range(2):

                @pl.when(may_get(t, way))
                def _():
                    pair_copy(1 + 3 * way + t, theirs(got_block(t, way))).wait_recv()

    def wait_sent():
        pair_copy(0, main(f)).wait_send()
        for t in range(NF - 1):
            for way in range(2):

                @pl.when(may_send(t, way))
                def _():
                    line_copy(t, way, sent_block(t, way)).wait_send()

                @pl.when(may_get(t, way))
                def _():
                    pair_copy(1 + 3 * way + t, main(got_block(t, way))).wait_send()

    return wait_pair, wait_sent


def line_sems():
    dma = pltpu.SemaphoreType.DMA
    return [dma((2, 3)), dma((2, 3)), dma((7,)), dma((7,)), dma((1,))]


class Reduction:
    def __init__(self, rows, d, r1x, r1y, ex, ey, r2x, r2y, total, t_send, r3, send, recv):
        self.rows, self.d, self.r1x, self.r1y, self.ex, self.ey = rows, d, r1x, r1y, ex, ey
        self.r2x, self.r2y, self.total, self.t_send, self.r3 = r2x, r2y, total, t_send, r3
        self.send, self.recv = send, recv
        self.s, self.f = place()
        s = self.s
        self.x, self.y, self.zh, self.core = s // 16, (s // 4) % 4, (s // 2) % 2, s % 2
        self.xs = [(self.x + n) % 4 for n in (1, 2, 3)]
        self.ys = [(self.y + n) % 4 for n in (1, 2, 3)]
        self.ends = [(1 - self.zh, self.core), (self.zh, 1 - self.core), (1 - self.zh, 1 - self.core)]
        self.copies = []

    def copy(self, src, dst, stage, way, n, x, y, zh, core):
        to = ((x * 4 + y) * 2 + zh) * 2 + core
        return remote(src, dst, self.send.at[stage, way, n], self.recv.at[stage, way, n], to, self.f)

    def start_first(self):
        half = HALF // 2
        self.first = []
        for n in range(3):
            a, b = self.xs[n], self.ys[n]
            self.first.append(
                self.copy(self.d.at[pl.ds(0, half), a], self.r1x.at[n], 0, 0, n, a, self.y, self.zh, self.core)
            )
            self.first.append(
                self.copy(self.d.at[pl.ds(half, half), :, b], self.r1y.at[n], 0, 1, n, self.x, b, self.zh, self.core)
            )
        for c in self.first:
            c.start()

    def start_second(self):
        half = HALF // 2
        for c in self.first:
            c.wait_recv()
        d, x, y = self.d, self.x, self.y

        def body(i, carry):
            acc = d[i, x].astype(F32)
            for n in range(3):
                acc += self.r1x[n, i].astype(F32)
            self.ex[i] = acc.astype(BF16)
            acc = d[half + i, :, y].astype(F32)
            for n in range(3):
                acc += self.r1y[n, i].astype(F32)
            self.ey[i] = acc.astype(BF16)
            return carry

        lax.fori_loop(0, half, body, 0)
        self.second = []
        for n in range(3):
            a, b = self.xs[n], self.ys[n]
            self.second.append(self.copy(self.ex.at[:, b], self.r2x.at[n], 1, 0, n, x, b, self.zh, self.core))
            self.second.append(self.copy(self.ey.at[:, a], self.r2y.at[n], 1, 1, n, a, y, self.zh, self.core))
        for c in self.second:
            c.start()

    def start_third(self):
        half = HALF // 2
        for c in self.second:
            c.wait_recv()
        x, y = self.x, self.y

        def body(i, carry):
            acc = self.ex[i, y].astype(F32)
            for n in range(3):
                acc += self.r2x[n, i].astype(F32)
            self.total[i] = acc
            acc = self.ey[i, x].astype(F32)
            for n in range(3):
                acc += self.r2y[n, i].astype(F32)
            self.total[half + i] = acc
            return carry

        lax.fori_loop(0, half, body, 0)
        for a in range(2):
            for b in range(2):
                start = 16 * a + 8 * b if self.rows == 32 else 8 * a
                piece = self.total[:, start : start + 8]
                self.t_send[2 * a + b] = piece.reshape(half, 16, 128).astype(BF16)
        self.third = []
        for n, (a, b) in enumerate(self.ends):
            self.third.append(self.copy(self.t_send.at[2 * a + b], self.r3.at[n], 2, 0, n, x, y, a, b))
        for c in self.third:
            c.start()

    def finish(self):
        for c in self.third:
            c.wait_recv()
        start = 16 * self.zh + 8 * self.core if self.rows == 32 else 8 * self.zh
        got = [self.r3[n].astype(F32).reshape(HALF, 8, 128) for n in range(3)]
        mine = self.total[:, pl.ds(pl.multiple_of(start, 8), 8)] + got[0]
        other = got[1] + got[2]
        low = jnp.where(self.core == 1, mine, other)
        high = jnp.where(self.core == 1, other, mine)
        for c in self.first + self.second + self.third:
            c.wait_send()
        return low, high[1:]


def reduction_scratch(rows):
    half = HALF // 2
    dma = pltpu.SemaphoreType.DMA
    return [
        pltpu.VMEM((HALF, 4, 4, rows, 128), BF16),
        pltpu.VMEM((3, half, 4, rows, 128), BF16),
        pltpu.VMEM((3, half, 4, rows, 128), BF16),
        pltpu.VMEM((half, 4, rows, 128), BF16),
        pltpu.VMEM((half, 4, rows, 128), BF16),
        pltpu.VMEM((3, half, rows, 128), BF16),
        pltpu.VMEM((3, half, rows, 128), BF16),
        pltpu.VMEM((HALF, rows, 128), F32),
        pltpu.VMEM((4, half, 16, 128), BF16),
        pltpu.VMEM((3, half, 16, 128), BF16),
        dma((3, 2, 3)),
        dma((3, 2, 3)),
    ]


def swish_slope(pre):
    logistic = jax.nn.sigmoid(pre)
    return logistic * (1.0 + pre * (1.0 - logistic))


def dot_nn(a, b):
    return lax.dot_general(a, b, (((1,), (0,)), ((), ())), preferred_element_type=F32)


def dot_nt(a, b):
    return lax.dot_general(a, b, (((1,), (1,)), ((), ())), preferred_element_type=F32)


def dot_tn(a, b):
    return lax.dot_general(a, b, (((0,), (0,)), ((), ())), preferred_element_type=F32)


def rows_from(start):
    return pl.ds(pl.multiple_of(start, 32), 256)


def whole_kernel(
    v_ref, w1_hbm, w2_hbm, cot_ref, gin_ref, gw1_ref, gw2_ref,
    w1, w2, wsem, vg, t1, a1, pre1, hown, hg, t2, h3, part1, part2, part_s, part_r,
    gs, t3, g3, gsem_s, gsem_r, hp, ps, rp, psem_s, psem_r, gf, gfsem_s, gfsem_r, g4, s5, r5, s5_s, s5_r, at, split, vown, ht, gc2, gc1,
    *rest,
):
    nsem = 5
    vsems, hsems = rest[:nsem], rest[nsem : 2 * nsem]
    red2 = Reduction(32, *rest[2 * nsem : 2 * nsem + 12])
    red1 = Reduction(16, *rest[2 * nsem + 12 :])
    s, f = place()
    core, zh = s % 2, (s // 2) % 2
    mate = s + 1 - 2 * core
    outside = s - 1 + 2 * core
    has_outside = jnp.logical_and(outside >= 0, outside < NS)
    peers = [(f + n) % NF for n in (1, 2, 3)]

    load1 = pltpu.make_async_copy(w1_hbm, w1, wsem.at[0])
    load2 = pltpu.make_async_copy(w2_hbm, w2, wsem.at[1])
    load1.start()
    load2.start()

    def dev(x_, y_, zh_, core_):
        return ((x_ * 4 + y_) * 2 + zh_) * 2 + core_

    for c in range(2):
        split[c] = v_ref[:, :, :, :, 128 * c : 128 * c + 128].astype(F32)
        for plane in range(2):
            for parity in range(2):
                for half in range(2):
                    part = split[c, plane, :, parity, pl.ds(half, 8, stride=2), :]
                    lane = 256 * half + 128 * c
                    vown[plane, parity, :, lane : lane + 128] = part.reshape(64, 128).astype(BF16)

    partners = [(True, s, p) for p in peers]
    partners += [(True, mate, f), (has_outside, outside, f)]
    partners += [(True, dev(a, red2.y, zh, core), f) for a in red2.xs]
    partners += [(True, dev(red2.x, b, zh, core), f) for b in red2.ys]
    partners += [(True, dev(red2.x, red2.y, 1 - zh, b), f) for b in (core, 1 - core)]
    greet(partners)

    def part_copy(slot, buf):
        return remote(buf.at[0], buf.at[1], part_s.at[slot], part_r.at[slot], outside, f)

    def vol(c, j):
        return vg.at[pl.ds(2 * c, 2), :, j]

    vol_wait, vol_sent = line_gather(vown, lambda j: vol(core, j), vsems)

    t1[:, 0:8, :] = jnp.zeros((8, 8, 512), F32)

    def cells(i, carry):
        plane, parity = i // 2, i % 2
        for j in range(NF):
            t1[:, 8 + 8 * j : 16 + 8 * j, :] = vg[plane, parity, j].astype(F32).reshape(8, 8, 512)
        edge = jnp.zeros((32, 256), BF16)
        for kx in range(3):
            a1[kx, plane, parity, 0:32] = edge
        a1[0, plane, parity, 32:288] = t1[:, 7:39, 256:512].reshape(256, 256).astype(BF16)
        a1[1, plane, parity, 32:288] = t1[:, 8:40, 0:256].reshape(256, 256).astype(BF16)
        a1[2, plane, parity, 32:288] = t1[:, 8:40, 256:512].reshape(256, 256).astype(BF16)
        return carry

    def taps_first(plane, kz):
        def body(ky, acc):
            parity, start = (ky + 1) % 2, jnp.minimum(ky, 1)
            for kx in range(3):
                acc += dot_nn(a1[kx, plane, parity, rows_from(32 * start)], w1[9 * kz + 3 * ky + kx])
            return acc

        return lax.fori_loop(0, 3, body, jnp.zeros((256, 128), F32))

    load1.wait()
    sends_part = jnp.logical_and(core == 1, has_outside)
    gets_part = jnp.logical_and(core == 0, has_outside)
    part1_copy = part_copy(0, part1)
    lax.fori_loop(4 * core, 4 * core + 4, cells, 0)

    @pl.when(sends_part)
    def _():
        part1[0] = taps_first(3, 0).astype(BF16)
        part1_copy.start()

    pre1[...] = taps_first(2 * core, 1) + taps_first(2 * core + 1, 2)
    vol_wait(lambda j: vol(1 - core, j))
    lax.fori_loop(4 - 4 * core, 8 - 4 * core, cells, 0)

    @pl.when(core == 1)
    def _():
        pre1[...] += taps_first(1, 0)

    @pl.when(gets_part)
    def _():
        part1_copy.wait_recv()
        pre1[...] += part1[1].astype(F32)

    pre_first = pre1[...]
    hown[...] = (pre_first * jax.nn.sigmoid(pre_first)).astype(BF16)

    def hid(plane, j):
        return hg.at[plane, :, pl.ds(pl.multiple_of(128 * j, 128), 128)]

    def turn(first, last):
        def body(i, carry):
            k = i + (HALF - 1) * (1 - core)
            kz, ky, kx = k // 9, (k // 3) % 3, k % 3
            parity, start = (ky + 1) % 2, jnp.minimum(ky, 1)
            plane = jnp.where(kz == 1, 0, 1)
            at[i, :, 0:256] = a1[kx, plane, parity, rows_from(32 * start)].T
            at[i, :, 256:512] = a1[kx, plane + 2, parity, rows_from(32 * start)].T
            return carry

        lax.fori_loop(first, last, body, 0)

    hid_wait, hid_sent = line_gather(
        hown,
        lambda j: hid(core, j),
        hsems,
        [lambda: turn(0, 4), lambda: turn(4, 8), lambda: turn(8, 11), lambda: turn(11, HALF)],
    )

    t2[:, 0:8, :] = jnp.zeros((8, 8, 512), F32)
    t2[:, 40:48, :] = jnp.zeros((8, 8, 512), F32)

    def spread_hidden(i):
        t2[:, 8:40, :] = hg[i].astype(F32).reshape(8, 32, 512)
        edge = jnp.zeros((32, 512), BF16)
        for kx in range(3):
            h3[kx, i, 0:32] = edge
            h3[kx, i, 288:320] = edge
        h3[0, i, 32:288] = t2[:, 7:39, :].reshape(256, 512).astype(BF16)
        h3[1, i, 32:288] = hg[i]
        h3[2, i, 32:288] = t2[:, 9:41, :].reshape(256, 512).astype(BF16)

    def taps_second(plane, kz):
        def body(ky, acc):
            for kx in range(3):
                acc += dot_nn(h3[kx, plane, rows_from(32 * ky)], w2[9 * kz + 3 * ky + kx])
            return acc

        return lax.fori_loop(0, 3, body, jnp.zeros((256, 128), F32))

    load2.wait()
    spread_hidden(core)
    part2_copy = part_copy(1, part2)

    @pl.when(has_outside)
    def _():
        part2[0] = taps_second(core, 2 - 2 * core).astype(BF16)
        part2_copy.start()

    pre_second = taps_second(core, 1)
    hid_wait(lambda j: hid(1 - core, j))
    spread_hidden(1 - core)
    pre_second += taps_second(1 - core, 2 - 2 * core)

    @pl.when(jnp.logical_not(has_outside))
    def _():
        part2[1] = jnp.zeros((256, 128), BF16)

    @pl.when(has_outside)
    def _():
        part2_copy.wait_recv()

    pre_second += part2[1].astype(F32)
    gs[1] = (cot_ref[...].astype(F32) * swish_slope(pre_second)).astype(BF16)

    def swap(place_there, to, slot):
        return remote(gs.at[1], gs.at[place_there], gsem_s.at[slot], gsem_r.at[slot], to, f)

    to_mate = swap(2 * core, mate, 0)
    to_out = swap(2 - 2 * core, outside, 1)
    from_mate = swap(2 - 2 * core, mate, 0)
    from_out = swap(2 * core, outside, 1)
    to_mate.start()

    @pl.when(has_outside)
    def _():
        to_out.start()

    @pl.when(jnp.logical_not(has_outside))
    def _():
        gs[2 * core] = jnp.zeros((256, 128), BF16)

    t3[:, 0:8, :] = jnp.zeros((8, 8, 128), F32)
    t3[:, 40:48, :] = jnp.zeros((8, 8, 128), F32)

    def spread_grads(i):
        t3[:, 8:40, :] = gs[i].astype(F32).reshape(8, 32, 128)
        edge = jnp.zeros((32, 128), BF16)
        for kx in range(3):
            g3[kx, i, 0:32] = edge
            g3[kx, i, 288:320] = edge
        g3[0, i, 32:288] = t3[:, 9:41, :].reshape(256, 128).astype(BF16)
        g3[1, i, 32:288] = gs[i]
        g3[2, i, 32:288] = t3[:, 7:39, :].reshape(256, 128).astype(BF16)

    def back_second(plane, kz, first):
        def body(ky, carry):
            acc = hp[...]
            for kx in range(3):
                acc += dot_nt(g3[kx, plane, rows_from(32 * (2 - ky))], w2[9 * kz + 3 * ky + kx])
            hp[...] = acc
            return carry

        if first:
            hp[...] = jnp.zeros((256, 512), F32)
        lax.fori_loop(0, 3, body, 0)

    spread_grads(1)
    back_second(1, 1, True)

    def turn_hidden(i, carry):
        ky, kx = i // 3, i % 3
        ht[i, :, 0:256] = h3[kx, core, rows_from(32 * ky)].T
        ht[i, :, 256:512] = h3[kx, 1 - core, rows_from(32 * ky)].T
        return carry

    lax.fori_loop(0, 9, turn_hidden, 0)
    from_mate.wait_recv()

    @pl.when(has_outside)
    def _():
        from_out.wait_recv()

    spread_grads(0)
    spread_grads(2)
    back_second(0, 2, False)
    back_second(2, 0, False)

    for j in range(NF):
        ps[j] = hp[:, 128 * j : 128 * j + 128].astype(BF16)
    shares = [remote(ps.at[p], rp.at[n], psem_s.at[n], psem_r.at[n], s, p) for n, p in enumerate(peers)]
    for c in shares:
        c.start()

    gc2[0, 0:256] = gs[2 * core]
    gc2[0, 256:512] = gs[1]
    gc2[1, 0:256] = gs[1]
    gc2[1, 256:512] = gs[2 - 2 * core]

    def terms_second(i, carry):
        k = i + (HALF - 1) * (1 - core)
        pairs = jnp.where(k // 9 == 1, 1, 0)
        red2.d[i] = dot_nn(ht[k % 9], gc2[pairs]).reshape(4, 4, 32, 128).astype(BF16)
        return carry

    lax.fori_loop(0, HALF, terms_second, 0)
    red2.start_first()

    for c in shares:
        c.wait_recv()
    hidden_grad = ps[f].astype(F32)
    for n in range(3):
        hidden_grad += rp[n].astype(F32)
    gf[0] = (hidden_grad * swish_slope(pre1[...])).astype(BF16)

    gf_mate = remote(gf.at[0], gf.at[1], gfsem_s.at[0], gfsem_r.at[0], mate, f)
    gf_out = remote(gf.at[0], gf.at[2], gfsem_s.at[1], gfsem_r.at[1], outside, f)
    gf_mate.start()
    sends = jnp.logical_and(core == 0, has_outside)
    gets = jnp.logical_and(core == 1, has_outside)

    @pl.when(sends)
    def _():
        gf_out.start()

    t3[:, 40:48, :] = jnp.zeros((8, 8, 128), F32)

    def spread_first(z, src):
        t3[:, 8:40, :] = src.astype(F32).reshape(8, 32, 128)
        g4[0, z, 0:256] = src
        g4[1, z, 0:256] = t3[:, 9:41, :].reshape(256, 128).astype(BF16)
        for i in range(2):
            g4[i, z, 256:288] = jnp.zeros((32, 128), BF16)

    def taps(parity):
        return [(1, 0)] if parity == 0 else [(2, 0), (0, 1)]

    def back_first(zp):
        for yp in range(2):
            for xp in range(2):
                acc = None
                for kz, oz in taps(zp):
                    for ky, oy in taps(yp):
                        for kx, ox in taps(xp):
                            term = dot_nt(g4[ox, oz, 32 * oy : 32 * oy + 256], w1[9 * kz + 3 * ky + kx])
                            acc = term if acc is None else acc + term
                acc = acc.reshape(8, 32, 256)
                for j in range(NF):
                    part = acc[:, 8 * j : 8 * j + 8, :].reshape(64, 256)
                    s5[j, zp, yp, :, 256 * xp : 256 * xp + 256] = part.astype(BF16)

    def share(zp):
        return [
            remote(s5.at[p, zp], r5.at[n, zp], s5_s.at[zp, n], s5_r.at[zp, n], s, p) for n, p in enumerate(peers)
        ]

    spread_first(0, gf[0])
    back_first(0)
    even = share(0)
    for c in even:
        c.start()
    gf_mate.wait_recv()

    gc1[1, 0:256] = gf[core]
    gc1[1, 256:512] = gf[1 - core]

    def terms_first(i, carry):
        n = (i + 9 * core) % HALF
        k = n + (HALF - 1) * (1 - core)
        pairs = jnp.where(k // 9 == 1, 1, 0)
        red1.d[n] = dot_nn(at[n], gc1[pairs]).reshape(4, 4, 16, 128).astype(BF16)
        return carry

    lax.fori_loop(0, 5, terms_first, 0)

    @pl.when(gets)
    def _():
        gf_out.wait_recv()

    @pl.when(jnp.logical_and(core == 1, jnp.logical_not(has_outside)))
    def _():
        gf[2] = jnp.zeros((256, 128), BF16)

    gc1[0, 0:256] = gf[0]
    gc1[0, 256:512] = gf[1 + core]
    lax.fori_loop(5, HALF, terms_first, 0)
    red1.start_first()
    spread_first(1, gf[1 + core])
    back_first(1)
    odd = share(1)
    for c in odd:
        c.start()

    red2.start_second()
    red2.start_third()
    red1.start_second()
    red1.start_third()
    low, high = red2.finish()
    gw2_ref[0:HALF] = low
    gw2_ref[HALF:27] = high
    low, high = red1.finish()
    gw1_ref[0:HALF] = jnp.where(core == 0, low[:, 0:4], low[:, 4:8])
    gw1_ref[HALF:27] = jnp.where(core == 0, high[:, 0:4], high[:, 4:8])

    for zp, copies in enumerate((even, odd)):
        for c in copies:
            c.wait_recv()
        acc = s5[f, zp].astype(F32)
        for n in range(3):
            acc += r5[n, zp].astype(F32)
        gin_ref[zp] = acc.astype(BF16)
    for c in shares + even + odd:
        c.wait_send()
    vol_sent()
    hid_sent()
    to_mate.wait_send()
    gf_mate.wait_send()

    @pl.when(sends_part)
    def _():
        part1_copy.wait_send()

    @pl.when(has_outside)
    def _():
        part2_copy.wait_send()

    @pl.when(has_outside)
    def _():
        to_out.wait_send()

    @pl.when(sends)
    def _():
        gf_out.wait_send()


def run_whole(cells, weight_first, weight_second, cotangent):
    dma = pltpu.SemaphoreType.DMA
    vmem, anywhere = pl.BlockSpec(memory_space=pltpu.VMEM), pl.BlockSpec(memory_space=pl.ANY)
    scratch = [
        pltpu.VMEM((27, 256, 128), BF16),
        pltpu.VMEM((27, 512, 128), BF16),
        dma((2,)),
        pltpu.VMEM((4, 2, NF, 64, 512), BF16),
        pltpu.VMEM((8, 40, 512), F32),
        pltpu.VMEM((3, 4, 2, 288, 256), BF16),
        pltpu.VMEM((256, 128), F32),
        pltpu.VMEM((256, 128), BF16),
        pltpu.VMEM((2, 256, 512), BF16),
        pltpu.VMEM((8, 48, 512), F32),
        pltpu.VMEM((3, 2, 320, 512), BF16),
        pltpu.VMEM((2, 256, 128), BF16),
        pltpu.VMEM((2, 256, 128), BF16),
        dma((2,)),
        dma((2,)),
        pltpu.VMEM((3, 256, 128), BF16),
        pltpu.VMEM((8, 48, 128), F32),
        pltpu.VMEM((3, 3, 320, 128), BF16),
        dma((2,)),
        dma((2,)),
        pltpu.VMEM((256, 512), F32),
        pltpu.VMEM((NF, 256, 128), BF16),
        pltpu.VMEM((3, 256, 128), BF16),
        dma((3,)),
        dma((3,)),
        pltpu.VMEM((3, 256, 128), BF16),
        dma((2,)),
        dma((2,)),
        pltpu.VMEM((2, 2, 288, 128), BF16),
        pltpu.VMEM((NF, 2, 2, 64, 512), BF16),
        pltpu.VMEM((3, 2, 2, 64, 512), BF16),
        dma((2, 3)),
        dma((2, 3)),
        pltpu.VMEM((HALF, 256, 512), BF16),
        pltpu.VMEM((2, 2, 8, 2, 16, 128), F32),
        pltpu.VMEM((2, 2, 64, 512), BF16),
        pltpu.VMEM((9, 512, 512), BF16),
        pltpu.VMEM((2, 512, 128), BF16),
        pltpu.VMEM((2, 512, 128), BF16),
    ]
    scratch += line_sems() + line_sems() + reduction_scratch(32) + reduction_scratch(16)
    return pl.pallas_call(
        whole_kernel,
        out_shape=(
            jax.ShapeDtypeStruct((2, 2, 64, 512), BF16),
            jax.ShapeDtypeStruct((27, 4, 128), F32),
            jax.ShapeDtypeStruct((27, 8, 128), F32),
        ),
        in_specs=[vmem, anywhere, anywhere, vmem],
        out_specs=(vmem, vmem, vmem),
        scratch_shapes=scratch,
        compiler_params=pltpu.CompilerParams(collective_id=0, has_side_effects=True, vmem_limit_bytes=52 * 2**20),
        name="bottleneck",
    )(cells, weight_first, weight_second, cotangent)


def per_device(volume, weight_first, weight_second, cotangent):
    grad, grad_first, grad_second = run_whole(volume.reshape(2, 8, 2, 16, 256), weight_first, weight_second, cotangent.reshape(256, 128))
    grad = grad.reshape(2, 2, 8, 8, 2, 256).transpose(0, 2, 1, 3, 4, 5).reshape(2, 16, 16, 256)
    return (grad, grad_first, grad_second)


def solution(mesh):
    placed = (
        P("space", None, "filt", None),
        P(None, None, "filt"),
        P(None, None, "filt"),
        P("space", None, None, "filt"),
    )
    return jax.shard_map(
        per_device,
        mesh=mesh,
        in_specs=placed,
        out_specs=(
            P("space", None, "filt", None),
            P(None, "space", "filt"),
            P(None, "space", "filt"),
        ),
        check_vma=False,
    )
```

```python
import functools

import jax
import jax.numpy as jnp
from jax import lax
from jax.experimental import pallas as pl
from jax.experimental.pallas import tpu as pltpu
from jax.sharding import PartitionSpec as P

BF16 = jnp.bfloat16
F32 = jnp.float32
MESH = pl.DeviceIdType.MESH
NS = 64
NF = 4
HALF = 14


def place():
    s = lax.axis_index("space")
    f = lax.axis_index("filt")
    return s, f


def remote(src, dst, send, recv, s, f):
    return pltpu.make_async_remote_copy(
        src_ref=src,
        dst_ref=dst,
        send_sem=send,
        recv_sem=recv,
        device_id={"space": s, "filt": f},
        device_id_type=MESH,
    )


def greet(partners):
    barrier = pltpu.get_barrier_semaphore()
    total = 0
    for cond, s, f in partners:
        if cond is True:
            pl.semaphore_signal(barrier, inc=1, device_id={"space": s, "filt": f}, device_id_type=MESH)
            total = total + 1
        else:

            @pl.when(cond)
            def _():
                pl.semaphore_signal(barrier, inc=1, device_id={"space": s, "filt": f}, device_id_type=MESH)

            total = total + cond.astype(jnp.int32)
    pl.semaphore_wait(barrier, total)


def line_gather(own, main, sems):
    line_send, line_recv, pair_send, pair_recv, local = sems
    s, f = place()
    mate = s + 1 - 2 * (s % 2)

    keep = [pltpu.make_async_copy(own.at[p], main(f, p), local.at[p]) for p in range(2)]
    for copy in keep:
        copy.start()

    def line_copy(t, way, block, p):
        to = f + 1 if way == 0 else f - 1
        view = main(block, p)
        return remote(own.at[p] if t == 0 else view, view, line_send.at[way, t, p], line_recv.at[way, t, p], s, to)

    def sent_block(t, way):
        return f - t if way == 0 else f + t

    def got_block(t, way):
        return f - 1 - t if way == 0 else f + 1 + t

    def may_send(t, way):
        if way == 0:
            return jnp.logical_and(f < NF - 1, f >= t)
        return jnp.logical_and(f > 0, f + t < NF)

    def may_get(t, way):
        return f > t if way == 0 else f + t < NF - 1

    def send(t, way, p):
        @pl.when(may_send(t, way))
        def _():
            line_copy(t, way, sent_block(t, way), p).start()

    def get(t, way, p):
        @pl.when(may_get(t, way))
        def _():
            line_copy(t, way, got_block(t, way), p).wait_recv()

    def pair_copy(slot, p, view):
        return remote(view, view, pair_send.at[slot, p], pair_recv.at[slot, p], mate, f)

    def pair_start(t, way, p):
        @pl.when(may_get(t, way))
        def _():
            pair_copy(1 + 3 * way + t, p, main(got_block(t, way), p)).start()

    for p in range(2):
        for way in range(2):
            send(0, way, p)
    for p in range(2):
        keep[p].wait()
        pair_copy(0, p, main(f, p)).start()
    for t in range(NF - 1):
        for p in range(2):
            for way in range(2):
                get(t, way, p)
                if t < NF - 2:
                    send(t + 1, way, p)
                pair_start(t, way, p)

    def wait_pair(theirs):
        for p in range(2):
            pair_copy(0, p, theirs(f, p)).wait_recv()
        for t in range(NF - 1):
            for way in range(2):

                @pl.when(may_get(t, way))
                def _():
                    for p in range(2):
                        pair_copy(1 + 3 * way + t, p, theirs(got_block(t, way), p)).wait_recv()

    def wait_sent():
        for p in range(2):
            pair_copy(0, p, main(f, p)).wait_send()
        for t in range(NF - 1):
            for way in range(2):

                @pl.when(may_send(t, way))
                def _():
                    for p in range(2):
                        line_copy(t, way, sent_block(t, way), p).wait_send()

                @pl.when(may_get(t, way))
                def _():
                    for p in range(2):
                        pair_copy(1 + 3 * way + t, p, main(got_block(t, way), p)).wait_send()

    return wait_pair, wait_sent


def line_sems():
    dma = pltpu.SemaphoreType.DMA
    return [dma((2, 3, 2)), dma((2, 3, 2)), dma((7, 2)), dma((7, 2)), dma((2,))]


def direct_gather(own, main, sems, work):
    send, recv, pair_send, pair_recv, local = sems
    s, f = place()
    mate = s + 1 - 2 * (s % 2)
    sent = [remote(own, main(f), send.at[n], recv.at[n], s, (f + n + 1) % NF) for n in range(3)]
    for copy in sent:
        copy.start()
    keep = pltpu.make_async_copy(own, main(f), local.at[0])
    keep.start()

    def pair_copy(n, view):
        return remote(view, view, pair_send.at[n], pair_recv.at[n], mate, f)

    blocks = [(f + NF - n - 1) % NF for n in range(3)] + [f]
    keep.wait()
    pair_copy(3, main(f)).start()
    work()
    for n in (0, 2, 1):
        remote(own, main(blocks[n]), send.at[n], recv.at[n], s, blocks[n]).wait_recv()
        pair_copy(n, main(blocks[n])).start()

    def wait_pair(theirs):
        for n in range(4):
            pair_copy(n, theirs(blocks[n])).wait_recv()

    def wait_sent():
        for copy in sent:
            copy.wait_send()
        for n in range(4):
            pair_copy(n, main(blocks[n])).wait_send()

    return wait_pair, wait_sent


def direct_sems():
    dma = pltpu.SemaphoreType.DMA
    return [dma((3,)), dma((3,)), dma((4,)), dma((4,)), dma((1,))]


def offset_of(slot, core):
    n = jnp.where(slot < 3, slot, jnp.where(slot < 7, slot + 2, jnp.where(slot < 9, slot - 4, slot)))
    return jnp.where(core == 0, HALF - 1 + n, (n + 9) % HALF)


def offsets(core):
    order = [0, 1, 2, 5, 6, 7, 8, 3, 4, 9, 10, 11, 12, 13]
    return [HALF - 1 + n if core == 0 else (n + 9) % HALF for n in order]


EARLY, LATE = ((0, 3), (7, 9)), ((3, 7), (9, 14))


class Reduction:
    def __init__(self, rows, d, r1x, r1y, ex, ey, r2x, r2y, total, t_send, r3, send, recv):
        self.rows, self.d, self.r1x, self.r1y, self.ex, self.ey = rows, d, r1x, r1y, ex, ey
        self.r2x, self.r2y, self.total, self.t_send, self.r3 = r2x, r2y, total, t_send, r3
        self.send, self.recv = send, recv
        self.s, self.f = place()
        s = self.s
        self.x, self.y, self.zh, self.core = s // 16, (s // 4) % 4, (s // 2) % 2, s % 2
        self.xs = [(self.x + n) % 4 for n in (1, 2, 3)]
        self.ys = [(self.y + n) % 4 for n in (1, 2, 3)]
        self.ends = [(1 - self.zh, self.core), (self.zh, 1 - self.core), (1 - self.zh, 1 - self.core)]
        self.first = []

    def copy(self, src, dst, stage, way, n, x, y, zh, core):
        to = ((x * 4 + y) * 2 + zh) * 2 + core
        return remote(src, dst, self.send.at[stage, way, n], self.recv.at[stage, way, n], to, self.f)

    def start_first(self, group):
        half = HALF // 2
        stage = 0 if group is EARLY else 3
        (x0, x1), (y0, y1) = group
        made = []
        for n in range(3):
            a, b = self.xs[n], self.ys[n]
            src, dst = self.d.at[pl.ds(x0, x1 - x0), a], self.r1x.at[n, pl.ds(x0, x1 - x0)]
            made.append(self.copy(src, dst, stage, 0, n, a, self.y, self.zh, self.core))
            src, dst = self.d.at[pl.ds(y0, y1 - y0), :, b], self.r1y.at[n, pl.ds(y0 - half, y1 - y0)]
            made.append(self.copy(src, dst, stage, 1, n, self.x, b, self.zh, self.core))
        for c in made:
            c.start()
        self.first += made

    def start_second(self):
        half = HALF // 2
        for c in self.first:
            c.wait_recv()
        d, x, y = self.d, self.x, self.y

        def body(i, carry):
            acc = d[i, x].astype(F32)
            for n in range(3):
                acc += self.r1x[n, i].astype(F32)
            self.ex[i] = acc.astype(BF16)
            acc = d[half + i, :, y].astype(F32)
            for n in range(3):
                acc += self.r1y[n, i].astype(F32)
            self.ey[i] = acc.astype(BF16)
            return carry

        lax.fori_loop(0, half, body, 0)
        self.second = []
        for n in range(3):
            a, b = self.xs[n], self.ys[n]
            self.second.append(self.copy(self.ex.at[:, b], self.r2x.at[n], 1, 0, n, x, b, self.zh, self.core))
            self.second.append(self.copy(self.ey.at[:, a], self.r2y.at[n], 1, 1, n, a, y, self.zh, self.core))
        for c in self.second:
            c.start()

    def start_third(self):
        half = HALF // 2
        for c in self.second:
            c.wait_recv()
        x, y = self.x, self.y

        def body(i, carry):
            acc = self.ex[i, y].astype(F32)
            for n in range(3):
                acc += self.r2x[n, i].astype(F32)
            self.total[i] = acc
            acc = self.ey[i, x].astype(F32)
            for n in range(3):
                acc += self.r2y[n, i].astype(F32)
            self.total[half + i] = acc
            return carry

        lax.fori_loop(0, half, body, 0)
        for a in range(2):
            for b in range(2):
                start = 16 * a + 8 * b if self.rows == 32 else 8 * a
                piece = self.total[:, start : start + 8]
                self.t_send[2 * a + b] = piece.reshape(half, 16, 128).astype(BF16)
        self.third = []
        for n, (a, b) in enumerate(self.ends):
            self.third.append(self.copy(self.t_send.at[2 * a + b], self.r3.at[n], 2, 0, n, x, y, a, b))
        for c in self.third:
            c.start()

    def finish(self):
        for c in self.third:
            c.wait_recv()
        start = 16 * self.zh + 8 * self.core if self.rows == 32 else 8 * self.zh
        got = [self.r3[n].astype(F32).reshape(HALF, 8, 128) for n in range(3)]
        mine = self.total[:, pl.ds(pl.multiple_of(start, 8), 8)] + got[0]
        other = got[1] + got[2]
        low = jnp.where(self.core == 1, mine, other)
        high = jnp.where(self.core == 1, other, mine)
        for c in self.first + self.second + self.third:
            c.wait_send()
        return [(k, low, i) for i, k in enumerate(offsets(1))] + [(k, high, i) for i, k in enumerate(offsets(0)) if k >= HALF]


def reduction_scratch(rows):
    half = HALF // 2
    dma = pltpu.SemaphoreType.DMA
    return [
        pltpu.VMEM((HALF, 4, 4, rows, 128), BF16),
        pltpu.VMEM((3, half, 4, rows, 128), BF16),
        pltpu.VMEM((3, half, 4, rows, 128), BF16),
        pltpu.VMEM((half, 4, rows, 128), BF16),
        pltpu.VMEM((half, 4, rows, 128), BF16),
        pltpu.VMEM((3, half, rows, 128), BF16),
        pltpu.VMEM((3, half, rows, 128), BF16),
        pltpu.VMEM((HALF, rows, 128), F32),
        pltpu.VMEM((4, half, 16, 128), BF16),
        pltpu.VMEM((3, half, 16, 128), BF16),
        dma((4, 2, 3)),
        dma((4, 2, 3)),
    ]


def swish_slope(pre):
    logistic = jax.nn.sigmoid(pre)
    return logistic * (1.0 + pre * (1.0 - logistic))


def dot_nn(a, b):
    return lax.dot_general(a, b, (((1,), (0,)), ((), ())), preferred_element_type=F32)


def dot_nt(a, b):
    return lax.dot_general(a, b, (((1,), (1,)), ((), ())), preferred_element_type=F32)


def dot_tn(a, b):
    return lax.dot_general(a, b, (((0,), (0,)), ((), ())), preferred_element_type=F32)


def rows_from(start):
    return pl.ds(pl.multiple_of(start, 32), 256)


def whole_kernel(
    v_ref, w1_hbm, w2_hbm, cot_ref, gin_ref, gw1_ref, gw2_ref,
    w1, w2, wsem, vg, t1, a1, pre1, hown, hg, t2, h3, part1, part2, part_s, part_r,
    gs, t3, g3, gsem_s, gsem_r, hp, ps, rp, psem_s, psem_r, gf, gfsem_s, gfsem_r, g4, s5, r5, s5_s, s5_r, at, split, vown, ht, gc2, gc1,
    *rest,
):
    nsem = 5
    vsems, hsems = rest[:nsem], rest[nsem : 2 * nsem]
    red2 = Reduction(32, *rest[2 * nsem : 2 * nsem + 12])
    red1 = Reduction(16, *rest[2 * nsem + 12 :])
    s, f = place()
    core, zh = s % 2, (s // 2) % 2
    mate = s + 1 - 2 * core
    outside = s - 1 + 2 * core
    has_outside = jnp.logical_and(outside >= 0, outside < NS)
    peers = [(f + n) % NF for n in (1, 2, 3)]

    load1 = pltpu.make_async_copy(w1_hbm, w1, wsem.at[0])
    load2 = pltpu.make_async_copy(w2_hbm, w2, wsem.at[1])
    load1.start()
    load2.start()

    def dev(x_, y_, zh_, core_):
        return ((x_ * 4 + y_) * 2 + zh_) * 2 + core_

    for c in range(2):
        split[c] = v_ref[:, :, :, :, 128 * c : 128 * c + 128].astype(F32)
        for plane in range(2):
            for parity in range(2):
                for half in range(2):
                    part = split[c, plane, :, parity, pl.ds(half, 8, stride=2), :]
                    lane = 256 * half + 128 * c
                    vown[plane, parity, :, lane : lane + 128] = part.reshape(64, 128).astype(BF16)

    partners = [(True, s, p) for p in peers]
    partners += [(True, mate, f), (has_outside, outside, f)]
    partners += [(True, dev(a, red2.y, zh, core), f) for a in red2.xs]
    partners += [(True, dev(red2.x, b, zh, core), f) for b in red2.ys]
    partners += [(True, dev(red2.x, red2.y, 1 - zh, b), f) for b in (core, 1 - core)]
    greet(partners)

    def part_copy(slot, buf):
        return remote(buf.at[0], buf.at[1], part_s.at[slot], part_r.at[slot], outside, f)

    def vol(c, j, p):
        return vg.at[2 * c + p, :, j]

    vol_wait, vol_sent = line_gather(vown, lambda j, p: vol(core, j, p), vsems)

    t1[:, 0:8, :] = jnp.zeros((8, 8, 512), F32)

    def cells(i, carry):
        plane, parity = i // 2, i % 2
        for j in range(NF):
            t1[:, 8 + 8 * j : 16 + 8 * j, :] = vg[plane, parity, j].astype(F32).reshape(8, 8, 512)
        edge = jnp.zeros((32, 256), BF16)
        for kx in range(3):
            a1[kx, plane, parity, 0:32] = edge
        a1[0, plane, parity, 32:288] = t1[:, 7:39, 256:512].reshape(256, 256).astype(BF16)
        a1[1, plane, parity, 32:288] = t1[:, 8:40, 0:256].reshape(256, 256).astype(BF16)
        a1[2, plane, parity, 32:288] = t1[:, 8:40, 256:512].reshape(256, 256).astype(BF16)
        return carry

    def taps_first(plane, kz):
        def body(ky, acc):
            parity, start = (ky + 1) % 2, jnp.minimum(ky, 1)
            for kx in range(3):
                acc += dot_nn(a1[kx, plane, parity, rows_from(32 * start)], w1[9 * kz + 3 * ky + kx])
            return acc

        return lax.fori_loop(0, 3, body, jnp.zeros((256, 128), F32))

    load1.wait()
    sends_part = jnp.logical_and(core == 1, has_outside)
    gets_part = jnp.logical_and(core == 0, has_outside)
    part1_copy = part_copy(0, part1)
    lax.fori_loop(4 * core, 4 * core + 4, cells, 0)

    @pl.when(sends_part)
    def _():
        part1[0] = taps_first(3, 0).astype(BF16)
        part1_copy.start()

    pre1[...] = taps_first(2 * core, 1) + taps_first(2 * core + 1, 2)
    vol_wait(lambda j, p: vol(1 - core, j, p))
    lax.fori_loop(4 - 4 * core, 8 - 4 * core, cells, 0)

    @pl.when(core == 1)
    def _():
        pre1[...] += taps_first(1, 0)

    @pl.when(gets_part)
    def _():
        part1_copy.wait_recv()
        pre1[...] += part1[1].astype(F32)

    pre_first = pre1[...]
    hown[...] = (pre_first * jax.nn.sigmoid(pre_first)).astype(BF16)

    def hid(plane, j):
        return hg.at[plane, :, pl.ds(pl.multiple_of(128 * j, 128), 128)]

    def turn(i, carry):
        k = offset_of(i, core)
        kz, ky, kx = k // 9, (k // 3) % 3, k % 3
        parity, start = (ky + 1) % 2, jnp.minimum(ky, 1)
        plane = jnp.where(kz == 1, 0, 1)
        at[i, :, 0:256] = a1[kx, plane, parity, rows_from(32 * start)].T
        at[i, :, 256:512] = a1[kx, plane + 2, parity, rows_from(32 * start)].T
        return carry

    hid_wait, hid_sent = direct_gather(
        hown, lambda j: hid(core, j), hsems, lambda: lax.fori_loop(0, HALF, turn, 0)
    )

    t2[:, 0:8, :] = jnp.zeros((8, 8, 512), F32)
    t2[:, 40:48, :] = jnp.zeros((8, 8, 512), F32)

    def spread_hidden(i):
        t2[:, 8:40, :] = hg[i].astype(F32).reshape(8, 32, 512)
        edge = jnp.zeros((32, 512), BF16)
        for kx in range(3):
            h3[kx, i, 0:32] = edge
            h3[kx, i, 288:320] = edge
        h3[0, i, 32:288] = t2[:, 7:39, :].reshape(256, 512).astype(BF16)
        h3[1, i, 32:288] = hg[i]
        h3[2, i, 32:288] = t2[:, 9:41, :].reshape(256, 512).astype(BF16)

    def taps_second(plane, kz):
        def body(ky, acc):
            for kx in range(3):
                acc += dot_nn(h3[kx, plane, rows_from(32 * ky)], w2[9 * kz + 3 * ky + kx])
            return acc

        return lax.fori_loop(0, 3, body, jnp.zeros((256, 128), F32))

    load2.wait()
    spread_hidden(core)
    part2_copy = part_copy(1, part2)

    @pl.when(has_outside)
    def _():
        part2[0] = taps_second(core, 2 - 2 * core).astype(BF16)
        part2_copy.start()

    pre_second = taps_second(core, 1)
    hid_wait(lambda j: hid(1 - core, j))
    spread_hidden(1 - core)
    pre_second += taps_second(1 - core, 2 - 2 * core)

    @pl.when(jnp.logical_not(has_outside))
    def _():
        part2[1] = jnp.zeros((256, 128), BF16)

    @pl.when(has_outside)
    def _():
        part2_copy.wait_recv()

    pre_second += part2[1].astype(F32)
    gs[1] = (cot_ref[...].astype(F32) * swish_slope(pre_second)).astype(BF16)

    def swap(place_there, to, slot):
        return remote(gs.at[1], gs.at[place_there], gsem_s.at[slot], gsem_r.at[slot], to, f)

    to_mate = swap(2 * core, mate, 0)
    to_out = swap(2 - 2 * core, outside, 1)
    from_mate = swap(2 - 2 * core, mate, 0)
    from_out = swap(2 * core, outside, 1)
    to_mate.start()

    @pl.when(has_outside)
    def _():
        to_out.start()

    @pl.when(jnp.logical_not(has_outside))
    def _():
        gs[2 * core] = jnp.zeros((256, 128), BF16)

    t3[:, 0:8, :] = jnp.zeros((8, 8, 128), F32)
    t3[:, 40:48, :] = jnp.zeros((8, 8, 128), F32)

    def spread_grads(i):
        t3[:, 8:40, :] = gs[i].astype(F32).reshape(8, 32, 128)
        edge = jnp.zeros((32, 128), BF16)
        for kx in range(3):
            g3[kx, i, 0:32] = edge
            g3[kx, i, 288:320] = edge
        g3[0, i, 32:288] = t3[:, 9:41, :].reshape(256, 128).astype(BF16)
        g3[1, i, 32:288] = gs[i]
        g3[2, i, 32:288] = t3[:, 7:39, :].reshape(256, 128).astype(BF16)

    def back_second(plane, kz, first):
        def body(ky, carry):
            acc = hp[...]
            for kx in range(3):
                acc += dot_nt(g3[kx, plane, rows_from(32 * (2 - ky))], w2[9 * kz + 3 * ky + kx])
            hp[...] = acc
            return carry

        if first:
            hp[...] = jnp.zeros((256, 512), F32)
        lax.fori_loop(0, 3, body, 0)

    spread_grads(1)
    back_second(1, 1, True)

    def turn_hidden(i, carry):
        ky, kx = i // 3, i % 3
        ht[i, :, 0:256] = h3[kx, core, rows_from(32 * ky)].T
        ht[i, :, 256:512] = h3[kx, 1 - core, rows_from(32 * ky)].T
        return carry

    lax.fori_loop(0, 9, turn_hidden, 0)
    from_mate.wait_recv()

    gc2[1, 0:256] = gs[1]
    gc2[1, 256:512] = gs[2 - 2 * core]

    def terms_second(i, carry):
        k = offset_of(i, core)
        pairs = jnp.where(k // 9 == 1, 1, 0)
        red2.d[i] = dot_nn(ht[k % 9], gc2[pairs]).reshape(4, 4, 32, 128).astype(BF16)
        return carry

    for first, last in EARLY:
        lax.fori_loop(first, last, terms_second, 0)
    red2.start_first(EARLY)

    @pl.when(has_outside)
    def _():
        from_out.wait_recv()

    spread_grads(0)
    spread_grads(2)
    back_second(0, 2, False)
    back_second(2, 0, False)

    for j in range(NF):
        ps[j] = hp[:, 128 * j : 128 * j + 128].astype(BF16)
    shares = [remote(ps.at[p], rp.at[n], psem_s.at[n], psem_r.at[n], s, p) for n, p in enumerate(peers)]
    for c in shares:
        c.start()

    gc2[0, 0:256] = gs[2 * core]
    gc2[0, 256:512] = gs[1]
    for first, last in LATE:
        lax.fori_loop(first, last, terms_second, 0)
    red2.start_first(LATE)

    for c in shares:
        c.wait_recv()
    hidden_grad = ps[f].astype(F32)
    for n in range(3):
        hidden_grad += rp[n].astype(F32)
    gf[0] = (hidden_grad * swish_slope(pre1[...])).astype(BF16)

    gf_mate = remote(gf.at[0], gf.at[1], gfsem_s.at[0], gfsem_r.at[0], mate, f)
    gf_out = remote(gf.at[0], gf.at[2], gfsem_s.at[1], gfsem_r.at[1], outside, f)
    gf_mate.start()
    sends = jnp.logical_and(core == 0, has_outside)
    gets = jnp.logical_and(core == 1, has_outside)

    @pl.when(sends)
    def _():
        gf_out.start()

    t3[:, 40:48, :] = jnp.zeros((8, 8, 128), F32)

    def spread_first(z, src):
        t3[:, 8:40, :] = src.astype(F32).reshape(8, 32, 128)
        g4[0, z, 0:256] = src
        g4[1, z, 0:256] = t3[:, 9:41, :].reshape(256, 128).astype(BF16)
        for i in range(2):
            g4[i, z, 256:288] = jnp.zeros((32, 128), BF16)

    def taps(parity):
        return [(1, 0)] if parity == 0 else [(2, 0), (0, 1)]

    def back_first(zp):
        for yp in range(2):
            for xp in range(2):
                acc = None
                for kz, oz in taps(zp):
                    for ky, oy in taps(yp):
                        for kx, ox in taps(xp):
                            term = dot_nt(g4[ox, oz, 32 * oy : 32 * oy + 256], w1[9 * kz + 3 * ky + kx])
                            acc = term if acc is None else acc + term
                acc = acc.reshape(8, 32, 256)
                for j in range(NF):
                    part = acc[:, 8 * j : 8 * j + 8, :].reshape(64, 256)
                    s5[j, zp, yp, :, 256 * xp : 256 * xp + 256] = part.astype(BF16)

    def share(zp):
        return [
            remote(s5.at[p, zp], r5.at[n, zp], s5_s.at[zp, n], s5_r.at[zp, n], s, p) for n, p in enumerate(peers)
        ]

    spread_first(0, gf[0])
    back_first(0)
    even = share(0)
    for c in even:
        c.start()
    gf_mate.wait_recv()

    gc1[1, 0:256] = gf[core]
    gc1[1, 256:512] = gf[1 - core]

    def terms_first(i, carry):
        pairs = jnp.where(offset_of(i, core) // 9 == 1, 1, 0)
        red1.d[i] = dot_nn(at[i], gc1[pairs]).reshape(4, 4, 16, 128).astype(BF16)
        return carry

    for first, last in EARLY:
        lax.fori_loop(first, last, terms_first, 0)
    red1.start_first(EARLY)

    @pl.when(gets)
    def _():
        gf_out.wait_recv()

    @pl.when(jnp.logical_and(core == 1, jnp.logical_not(has_outside)))
    def _():
        gf[2] = jnp.zeros((256, 128), BF16)

    gc1[0, 0:256] = gf[0]
    gc1[0, 256:512] = gf[1 + core]
    for first, last in LATE:
        lax.fori_loop(first, last, terms_first, 0)
    red1.start_first(LATE)
    spread_first(1, gf[1 + core])
    back_first(1)
    odd = share(1)
    for c in odd:
        c.start()

    red2.start_second()
    red2.start_third()
    red1.start_second()
    red1.start_third()
    for k, values, i in red2.finish():
        gw2_ref[k] = values[i]
    for k, values, i in red1.finish():
        gw1_ref[k] = jnp.where(core == 0, values[i, 0:4], values[i, 4:8])

    for zp, copies in enumerate((even, odd)):
        for c in copies:
            c.wait_recv()
        acc = s5[f, zp].astype(F32)
        for n in range(3):
            acc += r5[n, zp].astype(F32)
        gin_ref[zp] = acc.astype(BF16)
    for c in shares + even + odd:
        c.wait_send()
    vol_sent()
    hid_sent()
    to_mate.wait_send()
    gf_mate.wait_send()

    @pl.when(sends_part)
    def _():
        part1_copy.wait_send()

    @pl.when(has_outside)
    def _():
        part2_copy.wait_send()

    @pl.when(has_outside)
    def _():
        to_out.wait_send()

    @pl.when(sends)
    def _():
        gf_out.wait_send()


def run_whole(cells, weight_first, weight_second, cotangent):
    dma = pltpu.SemaphoreType.DMA
    vmem, anywhere = pl.BlockSpec(memory_space=pltpu.VMEM), pl.BlockSpec(memory_space=pl.ANY)
    scratch = [
        pltpu.VMEM((27, 256, 128), BF16),
        pltpu.VMEM((27, 512, 128), BF16),
        dma((2,)),
        pltpu.VMEM((4, 2, NF, 64, 512), BF16),
        pltpu.VMEM((8, 40, 512), F32),
        pltpu.VMEM((3, 4, 2, 288, 256), BF16),
        pltpu.VMEM((256, 128), F32),
        pltpu.VMEM((256, 128), BF16),
        pltpu.VMEM((2, 256, 512), BF16),
        pltpu.VMEM((8, 48, 512), F32),
        pltpu.VMEM((3, 2, 320, 512), BF16),
        pltpu.VMEM((2, 256, 128), BF16),
        pltpu.VMEM((2, 256, 128), BF16),
        dma((2,)),
        dma((2,)),
        pltpu.VMEM((3, 256, 128), BF16),
        pltpu.VMEM((8, 48, 128), F32),
        pltpu.VMEM((3, 3, 320, 128), BF16),
        dma((2,)),
        dma((2,)),
        pltpu.VMEM((256, 512), F32),
        pltpu.VMEM((NF, 256, 128), BF16),
        pltpu.VMEM((3, 256, 128), BF16),
        dma((3,)),
        dma((3,)),
        pltpu.VMEM((3, 256, 128), BF16),
        dma((2,)),
        dma((2,)),
        pltpu.VMEM((2, 2, 288, 128), BF16),
        pltpu.VMEM((NF, 2, 2, 64, 512), BF16),
        pltpu.VMEM((3, 2, 2, 64, 512), BF16),
        dma((2, 3)),
        dma((2, 3)),
        pltpu.VMEM((HALF, 256, 512), BF16),
        pltpu.VMEM((2, 2, 8, 2, 16, 128), F32),
        pltpu.VMEM((2, 2, 64, 512), BF16),
        pltpu.VMEM((9, 512, 512), BF16),
        pltpu.VMEM((2, 512, 128), BF16),
        pltpu.VMEM((2, 512, 128), BF16),
    ]
    scratch += line_sems() + direct_sems() + reduction_scratch(32) + reduction_scratch(16)
    return pl.pallas_call(
        whole_kernel,
        out_shape=(
            jax.ShapeDtypeStruct((2, 2, 64, 512), BF16),
            jax.ShapeDtypeStruct((27, 4, 128), F32),
            jax.ShapeDtypeStruct((27, 8, 128), F32),
        ),
        in_specs=[vmem, anywhere, anywhere, vmem],
        out_specs=(vmem, vmem, vmem),
        scratch_shapes=scratch,
        compiler_params=pltpu.CompilerParams(collective_id=0, has_side_effects=True, vmem_limit_bytes=52 * 2**20),
        name="bottleneck",
    )(cells, weight_first, weight_second, cotangent)


def per_device(volume, weight_first, weight_second, cotangent):
    grad, grad_first, grad_second = run_whole(volume.reshape(2, 8, 2, 16, 256), weight_first, weight_second, cotangent.reshape(256, 128))
    grad = grad.reshape(2, 2, 8, 8, 2, 256).transpose(0, 2, 1, 3, 4, 5).reshape(2, 16, 16, 256)
    return (grad, grad_first, grad_second)


def solution(mesh):
    placed = (
        P("space", None, "filt", None),
        P(None, None, "filt"),
        P(None, None, "filt"),
        P("space", None, None, "filt"),
    )
    return jax.shard_map(
        per_device,
        mesh=mesh,
        in_specs=placed,
        out_specs=(
            P("space", None, "filt", None),
            P(None, "space", "filt"),
            P(None, "space", "filt"),
        ),
        check_vma=False,
    )
```

```python
import functools

import jax
import jax.numpy as jnp
from jax import lax
from jax.experimental import pallas as pl
from jax.experimental.pallas import tpu as pltpu
from jax.sharding import PartitionSpec as P

BF16 = jnp.bfloat16
F32 = jnp.float32
MESH = pl.DeviceIdType.MESH
NS = 64
NF = 4
HALF = 14


def place():
    s = lax.axis_index("space")
    f = lax.axis_index("filt")
    return s, f


def remote(src, dst, send, recv, s, f):
    return pltpu.make_async_remote_copy(
        src_ref=src,
        dst_ref=dst,
        send_sem=send,
        recv_sem=recv,
        device_id={"space": s, "filt": f},
        device_id_type=MESH,
    )


def greet(partners):
    barrier = pltpu.get_barrier_semaphore()
    total = 0
    for cond, s, f in partners:
        if cond is True:
            pl.semaphore_signal(barrier, inc=1, device_id={"space": s, "filt": f}, device_id_type=MESH)
            total = total + 1
        else:

            @pl.when(cond)
            def _():
                pl.semaphore_signal(barrier, inc=1, device_id={"space": s, "filt": f}, device_id_type=MESH)

            total = total + cond.astype(jnp.int32)
    pl.semaphore_wait(barrier, total)


def line_gather(own, main, sems):
    line_send, line_recv, pair_send, pair_recv, local = sems
    s, f = place()
    mate = s + 1 - 2 * (s % 2)

    keep = [pltpu.make_async_copy(own.at[p], main(f, p), local.at[p]) for p in range(2)]
    for copy in keep:
        copy.start()

    def line_copy(t, way, block, p):
        to = f + 1 if way == 0 else f - 1
        view = main(block, p)
        return remote(own.at[p] if t == 0 else view, view, line_send.at[way, t, p], line_recv.at[way, t, p], s, to)

    def sent_block(t, way):
        return f - t if way == 0 else f + t

    def got_block(t, way):
        return f - 1 - t if way == 0 else f + 1 + t

    def may_send(t, way):
        if way == 0:
            return jnp.logical_and(f < NF - 1, f >= t)
        return jnp.logical_and(f > 0, f + t < NF)

    def may_get(t, way):
        return f > t if way == 0 else f + t < NF - 1

    def send(t, way, p):
        @pl.when(may_send(t, way))
        def _():
            line_copy(t, way, sent_block(t, way), p).start()

    def get(t, way, p):
        @pl.when(may_get(t, way))
        def _():
            line_copy(t, way, got_block(t, way), p).wait_recv()

    def pair_copy(slot, p, view):
        return remote(view, view, pair_send.at[slot, p], pair_recv.at[slot, p], mate, f)

    def pair_start(t, way, p):
        @pl.when(may_get(t, way))
        def _():
            pair_copy(1 + 3 * way + t, p, main(got_block(t, way), p)).start()

    for p in range(2):
        for way in range(2):
            send(0, way, p)
    for p in range(2):
        keep[p].wait()
        pair_copy(0, p, main(f, p)).start()
    for t in range(NF - 1):
        for p in range(2):
            for way in range(2):
                get(t, way, p)
                if t < NF - 2:
                    send(t + 1, way, p)
                pair_start(t, way, p)

    def wait_pair(theirs):
        for p in range(2):
            pair_copy(0, p, theirs(f, p)).wait_recv()
        for t in range(NF - 1):
            for way in range(2):

                @pl.when(may_get(t, way))
                def _():
                    for p in range(2):
                        pair_copy(1 + 3 * way + t, p, theirs(got_block(t, way), p)).wait_recv()

    def wait_sent():
        for p in range(2):
            pair_copy(0, p, main(f, p)).wait_send()
        for t in range(NF - 1):
            for way in range(2):

                @pl.when(may_send(t, way))
                def _():
                    for p in range(2):
                        line_copy(t, way, sent_block(t, way), p).wait_send()

                @pl.when(may_get(t, way))
                def _():
                    for p in range(2):
                        pair_copy(1 + 3 * way + t, p, main(got_block(t, way), p)).wait_send()

    return wait_pair, wait_sent


def line_sems():
    dma = pltpu.SemaphoreType.DMA
    return [dma((2, 3, 2)), dma((2, 3, 2)), dma((7, 2)), dma((7, 2)), dma((2,))]


def direct_gather(own, main, sems, work):
    send, recv, pair_send, pair_recv, local = sems
    s, f = place()
    mate = s + 1 - 2 * (s % 2)
    sent = [remote(own, main(f), send.at[n], recv.at[n], s, (f + n + 1) % NF) for n in range(3)]
    for copy in sent:
        copy.start()
    keep = pltpu.make_async_copy(own, main(f), local.at[0])
    keep.start()

    def pair_copy(n, view):
        return remote(view, view, pair_send.at[n], pair_recv.at[n], mate, f)

    blocks = [(f + NF - n - 1) % NF for n in range(3)] + [f]
    keep.wait()
    pair_copy(3, main(f)).start()
    work()
    for n in (0, 2, 1):
        remote(own, main(blocks[n]), send.at[n], recv.at[n], s, blocks[n]).wait_recv()
        pair_copy(n, main(blocks[n])).start()

    def wait_pair(theirs):
        for n in range(4):
            pair_copy(n, theirs(blocks[n])).wait_recv()

    def wait_sent():
        for copy in sent:
            copy.wait_send()
        for n in range(4):
            pair_copy(n, main(blocks[n])).wait_send()

    return wait_pair, wait_sent


def direct_sems():
    dma = pltpu.SemaphoreType.DMA
    return [dma((3,)), dma((3,)), dma((4,)), dma((4,)), dma((1,))]


def offset_of(slot, core):
    n = jnp.where(slot < 3, slot, jnp.where(slot < 7, slot + 2, jnp.where(slot < 9, slot - 4, slot)))
    return jnp.where(core == 0, HALF - 1 + n, (n + 9) % HALF)


def offsets(core):
    order = [0, 1, 2, 5, 6, 7, 8, 3, 4, 9, 10, 11, 12, 13]
    return [HALF - 1 + n if core == 0 else (n + 9) % HALF for n in order]


EARLY, LATE = ((0, 3), (7, 9)), ((3, 7), (9, 14))


class Spread:
    def __init__(self, w1, wx, send, recv):
        self.w1, self.wx, self.send, self.recv = w1, wx, send, recv
        self.s, self.f = place()
        s = self.s
        self.x, self.y, self.zh, self.core = s // 16, (s // 4) % 4, (s // 2) % 2, s % 2

    def copy(self, stage, n, src, dst, x, y, core, f):
        to = ((x * 4 + y) * 2 + self.zh) * 2 + core
        return remote(src, dst, self.send.at[stage, n], self.recv.at[stage, n], to, f)

    def fetch(self):
        part = pl.ds(pl.multiple_of(16 * (4 * self.x + self.y), 16), 16)
        src = self.w1.at[pl.ds((HALF - 1) * self.core, HALF), part]
        dst = self.wx.at[self.core, :, self.x, self.y]
        return self.copy(0, 0, src, dst, self.x, self.y, self.core, (self.f + 2) % NF)

    def over(self, stage, c, n, got):
        x, y = self.x, self.y
        step = NF - n - 1 if got else n + 1
        along_x = (stage == 1) == (c == 0)
        px, py = ((x + step) % 4, y) if along_x else (x, (y + step) % 4)
        hx, hy = (px, py) if got else (x, y)
        if stage == 1:
            view = self.wx.at[c, :, hx, hy]
        else:
            view = self.wx.at[c, :, hx] if along_x else self.wx.at[c, :, :, hy]
        return self.copy(stage, n, view, view, px, py, c, self.f)

    def each(self, stage, what):
        for c in range(2):

            @pl.when(self.core == c)
            def _():
                for n in range(3):
                    if what == "start":
                        self.over(stage, c, n, False).start()
                    elif what == "get":
                        self.over(stage, c, n, True).wait_recv()
                    else:
                        self.over(stage, c, n, False).wait_send()

    def swap(self, c):
        view = self.wx.at[c]
        return self.copy(3, 0, view, view, self.x, self.y, 1 - self.core, self.f)


class Reduction:
    def __init__(self, rows, d, r1x, r1y, ex, ey, r2x, r2y, total, t_send, r3, send, recv):
        self.rows, self.d, self.r1x, self.r1y, self.ex, self.ey = rows, d, r1x, r1y, ex, ey
        self.r2x, self.r2y, self.total, self.t_send, self.r3 = r2x, r2y, total, t_send, r3
        self.send, self.recv = send, recv
        self.s, self.f = place()
        s = self.s
        self.x, self.y, self.zh, self.core = s // 16, (s // 4) % 4, (s // 2) % 2, s % 2
        self.xs = [(self.x + n) % 4 for n in (1, 2, 3)]
        self.ys = [(self.y + n) % 4 for n in (1, 2, 3)]
        self.ends = [(1 - self.zh, self.core), (self.zh, 1 - self.core), (1 - self.zh, 1 - self.core)]
        self.first = []

    def copy(self, src, dst, stage, way, n, x, y, zh, core):
        to = ((x * 4 + y) * 2 + zh) * 2 + core
        return remote(src, dst, self.send.at[stage, way, n], self.recv.at[stage, way, n], to, self.f)

    def start_first(self, group):
        half = HALF // 2
        stage = 0 if group is EARLY else 3
        (x0, x1), (y0, y1) = group
        made = []
        for n in range(3):
            a, b = self.xs[n], self.ys[n]
            src, dst = self.d.at[pl.ds(x0, x1 - x0), a], self.r1x.at[n, pl.ds(x0, x1 - x0)]
            made.append(self.copy(src, dst, stage, 0, n, a, self.y, self.zh, self.core))
            src, dst = self.d.at[pl.ds(y0, y1 - y0), :, b], self.r1y.at[n, pl.ds(y0 - half, y1 - y0)]
            made.append(self.copy(src, dst, stage, 1, n, self.x, b, self.zh, self.core))
        for c in made:
            c.start()
        self.first += made

    def start_second(self):
        half = HALF // 2
        for c in self.first:
            c.wait_recv()
        d, x, y = self.d, self.x, self.y

        def body(i, carry):
            acc = d[i, x].astype(F32)
            for n in range(3):
                acc += self.r1x[n, i].astype(F32)
            self.ex[i] = acc.astype(BF16)
            acc = d[half + i, :, y].astype(F32)
            for n in range(3):
                acc += self.r1y[n, i].astype(F32)
            self.ey[i] = acc.astype(BF16)
            return carry

        lax.fori_loop(0, half, body, 0)
        self.second = []
        for n in range(3):
            a, b = self.xs[n], self.ys[n]
            self.second.append(self.copy(self.ex.at[:, b], self.r2x.at[n], 1, 0, n, x, b, self.zh, self.core))
            self.second.append(self.copy(self.ey.at[:, a], self.r2y.at[n], 1, 1, n, a, y, self.zh, self.core))
        for c in self.second:
            c.start()

    def start_third(self):
        half = HALF // 2
        for c in self.second:
            c.wait_recv()
        x, y = self.x, self.y

        def body(i, carry):
            acc = self.ex[i, y].astype(F32)
            for n in range(3):
                acc += self.r2x[n, i].astype(F32)
            self.total[i] = acc
            acc = self.ey[i, x].astype(F32)
            for n in range(3):
                acc += self.r2y[n, i].astype(F32)
            self.total[half + i] = acc
            return carry

        lax.fori_loop(0, half, body, 0)
        for a in range(2):
            for b in range(2):
                start = 16 * a + 8 * b if self.rows == 32 else 8 * a
                piece = self.total[:, start : start + 8]
                self.t_send[2 * a + b] = piece.reshape(half, 16, 128).astype(BF16)
        self.third = []
        for n, (a, b) in enumerate(self.ends):
            self.third.append(self.copy(self.t_send.at[2 * a + b], self.r3.at[n], 2, 0, n, x, y, a, b))
        for c in self.third:
            c.start()

    def finish(self):
        for c in self.third:
            c.wait_recv()
        start = 16 * self.zh + 8 * self.core if self.rows == 32 else 8 * self.zh
        got = [self.r3[n].astype(F32).reshape(HALF, 8, 128) for n in range(3)]
        mine = self.total[:, pl.ds(pl.multiple_of(start, 8), 8)] + got[0]
        other = got[1] + got[2]
        low = jnp.where(self.core == 1, mine, other)
        high = jnp.where(self.core == 1, other, mine)
        for c in self.first + self.second + self.third:
            c.wait_send()
        return [(k, low, i) for i, k in enumerate(offsets(1))] + [(k, high, i) for i, k in enumerate(offsets(0)) if k >= HALF]


def reduction_scratch(rows):
    half = HALF // 2
    dma = pltpu.SemaphoreType.DMA
    return [
        pltpu.VMEM((HALF, 4, 4, rows, 128), BF16),
        pltpu.VMEM((3, half, 4, rows, 128), BF16),
        pltpu.VMEM((3, half, 4, rows, 128), BF16),
        pltpu.VMEM((half, 4, rows, 128), BF16),
        pltpu.VMEM((half, 4, rows, 128), BF16),
        pltpu.VMEM((3, half, rows, 128), BF16),
        pltpu.VMEM((3, half, rows, 128), BF16),
        pltpu.VMEM((HALF, rows, 128), F32),
        pltpu.VMEM((4, half, 16, 128), BF16),
        pltpu.VMEM((3, half, 16, 128), BF16),
        dma((4, 2, 3)),
        dma((4, 2, 3)),
    ]


def swish_slope(pre):
    logistic = jax.nn.sigmoid(pre)
    return logistic * (1.0 + pre * (1.0 - logistic))


def dot_nn(a, b):
    return lax.dot_general(a, b, (((1,), (0,)), ((), ())), preferred_element_type=F32)


def dot_nt(a, b):
    return lax.dot_general(a, b, (((1,), (1,)), ((), ())), preferred_element_type=F32)


def dot_tn(a, b):
    return lax.dot_general(a, b, (((0,), (0,)), ((), ())), preferred_element_type=F32)


def rows_from(start):
    return pl.ds(pl.multiple_of(start, 32), 256)


def whole_kernel(
    v_ref, w1_hbm, w2_hbm, cot_ref, gin_ref, gw1_ref, gw2_ref,
    w1, w2, wsem, vg, t1, a1, pre1, hown, hg, t2, h3, part1, part2, part_s, part_r,
    gs, t3, g3, gsem_s, gsem_r, hp, ps, rp, psem_s, psem_r, gf, gfsem_s, gfsem_r, g4, s5, r5, s5_s, s5_r, at, split, vown, ht, gc2, gc1, wx, wx_s, wx_r, gx, gx_s, gx_r, k5,
    *rest,
):
    nsem = 5
    vsems, hsems = rest[:nsem], rest[nsem : 2 * nsem]
    red2 = Reduction(32, *rest[2 * nsem : 2 * nsem + 12])
    red1 = Reduction(16, *rest[2 * nsem + 12 :])
    s, f = place()
    core, zh = s % 2, (s // 2) % 2
    mate = s + 1 - 2 * core
    outside = s - 1 + 2 * core
    has_outside = jnp.logical_and(outside >= 0, outside < NS)
    peers = [(f + n) % NF for n in (1, 2, 3)]

    load1 = pltpu.make_async_copy(w1_hbm, w1, wsem.at[0])
    load2 = pltpu.make_async_copy(w2_hbm, w2, wsem.at[1])
    load1.start()
    load2.start()

    def dev(x_, y_, zh_, core_):
        return ((x_ * 4 + y_) * 2 + zh_) * 2 + core_

    for c in range(2):
        split[c] = v_ref[:, :, :, :, 128 * c : 128 * c + 128].astype(F32)
        for plane in range(2):
            for parity in range(2):
                for half in range(2):
                    part = split[c, plane, :, parity, pl.ds(half, 8, stride=2), :]
                    lane = 256 * half + 128 * c
                    vown[plane, parity, :, lane : lane + 128] = part.reshape(64, 128).astype(BF16)

    partners = [(True, s, p) for p in peers]
    partners += [(True, mate, f), (has_outside, outside, f)]
    partners += [(True, dev(a, red2.y, zh, core), f) for a in red2.xs]
    partners += [(True, dev(red2.x, b, zh, core), f) for b in red2.ys]
    partners += [(True, dev(red2.x, red2.y, 1 - zh, b), f) for b in (core, 1 - core)]
    greet(partners)
    spread = Spread(w1, wx, wx_s, wx_r)

    def part_copy(slot, buf):
        return remote(buf.at[0], buf.at[1], part_s.at[slot], part_r.at[slot], outside, f)

    def vol(c, j, p):
        return vg.at[2 * c + p, :, j]

    vol_wait, vol_sent = line_gather(vown, lambda j, p: vol(core, j, p), vsems)

    t1[:, 0:8, :] = jnp.zeros((8, 8, 512), F32)

    def cells(i, carry):
        plane, parity = i // 2, i % 2
        for j in range(NF):
            t1[:, 8 + 8 * j : 16 + 8 * j, :] = vg[plane, parity, j].astype(F32).reshape(8, 8, 512)
        edge = jnp.zeros((32, 256), BF16)
        for kx in range(3):
            a1[kx, plane, parity, 0:32] = edge
        a1[0, plane, parity, 32:288] = t1[:, 7:39, 256:512].reshape(256, 256).astype(BF16)
        a1[1, plane, parity, 32:288] = t1[:, 8:40, 0:256].reshape(256, 256).astype(BF16)
        a1[2, plane, parity, 32:288] = t1[:, 8:40, 256:512].reshape(256, 256).astype(BF16)
        return carry

    def taps_first(plane, kz):
        def body(ky, acc):
            parity, start = (ky + 1) % 2, jnp.minimum(ky, 1)
            for kx in range(3):
                acc += dot_nn(a1[kx, plane, parity, rows_from(32 * start)], w1[9 * kz + 3 * ky + kx])
            return acc

        return lax.fori_loop(0, 3, body, jnp.zeros((256, 128), F32))

    load1.wait()
    spread.fetch().start()
    sends_part = jnp.logical_and(core == 1, has_outside)
    gets_part = jnp.logical_and(core == 0, has_outside)
    part1_copy = part_copy(0, part1)
    lax.fori_loop(4 * core, 4 * core + 4, cells, 0)

    @pl.when(sends_part)
    def _():
        part1[0] = taps_first(3, 0).astype(BF16)
        part1_copy.start()

    pre1[...] = taps_first(2 * core, 1) + taps_first(2 * core + 1, 2)
    vol_wait(lambda j, p: vol(1 - core, j, p))

    @pl.when(core == 1)
    def _():
        lax.fori_loop(2, 4, cells, 0)
        pre1[...] += taps_first(1, 0)

    @pl.when(gets_part)
    def _():
        part1_copy.wait_recv()
        pre1[...] += part1[1].astype(F32)

    pre_first = pre1[...]
    hown[...] = (pre_first * jax.nn.sigmoid(pre_first)).astype(BF16)

    def hid(plane, j):
        return hg.at[plane, :, pl.ds(pl.multiple_of(128 * j, 128), 128)]

    def turn(i, carry):
        k = offset_of(i, core)
        kz, ky, kx = k // 9, (k // 3) % 3, k % 3
        parity, start = (ky + 1) % 2, jnp.minimum(ky, 1)
        plane = jnp.where(kz == 1, 0, 1)
        at[i, :, 0:256] = a1[kx, plane, parity, rows_from(32 * start)].T
        at[i, :, 256:512] = a1[kx, plane + 2, parity, rows_from(32 * start)].T
        return carry

    def windows():
        spread.fetch().wait_recv()
        spread.each(1, "start")
        lax.fori_loop(4 - 4 * core, 8 - 6 * core, cells, 0)
        lax.fori_loop(0, HALF, turn, 0)

    hid_wait, hid_sent = direct_gather(hown, lambda j: hid(core, j), hsems, windows)

    spread.each(1, "get")
    spread.each(2, "start")
    t2[:, 0:8, :] = jnp.zeros((8, 8, 512), F32)
    t2[:, 40:48, :] = jnp.zeros((8, 8, 512), F32)

    def spread_hidden(i):
        t2[:, 8:40, :] = hg[i].astype(F32).reshape(8, 32, 512)
        edge = jnp.zeros((32, 512), BF16)
        for kx in range(3):
            h3[kx, i, 0:32] = edge
            h3[kx, i, 288:320] = edge
        h3[0, i, 32:288] = t2[:, 7:39, :].reshape(256, 512).astype(BF16)
        h3[1, i, 32:288] = hg[i]
        h3[2, i, 32:288] = t2[:, 9:41, :].reshape(256, 512).astype(BF16)

    def taps_second(plane, kz):
        def body(ky, acc):
            for kx in range(3):
                acc += dot_nn(h3[kx, plane, rows_from(32 * ky)], w2[9 * kz + 3 * ky + kx])
            return acc

        return lax.fori_loop(0, 3, body, jnp.zeros((256, 128), F32))

    load2.wait()
    spread_hidden(core)
    part2_copy = part_copy(1, part2)

    @pl.when(has_outside)
    def _():
        part2[0] = taps_second(core, 2 - 2 * core).astype(BF16)
        part2_copy.start()

    pre_second = taps_second(core, 1)
    hid_wait(lambda j: hid(1 - core, j))
    spread_hidden(1 - core)
    pre_second += taps_second(1 - core, 2 - 2 * core)

    def turn_hidden(i, carry):
        ky, kx = i // 3, i % 3
        ht[i, :, 0:256] = h3[kx, core, rows_from(32 * ky)].T
        ht[i, :, 256:512] = h3[kx, 1 - core, rows_from(32 * ky)].T
        return carry

    lax.fori_loop(0, 9, turn_hidden, 0)

    @pl.when(jnp.logical_not(has_outside))
    def _():
        part2[1] = jnp.zeros((256, 128), BF16)

    @pl.when(has_outside)
    def _():
        part2_copy.wait_recv()

    pre_second += part2[1].astype(F32)
    gs[1] = (cot_ref[...].astype(F32) * swish_slope(pre_second)).astype(BF16)

    def swap(place_there, to, slot):
        return remote(gs.at[1], gs.at[place_there], gsem_s.at[slot], gsem_r.at[slot], to, f)

    to_mate = swap(2 * core, mate, 0)
    to_out = swap(2 - 2 * core, outside, 1)
    from_mate = swap(2 - 2 * core, mate, 0)
    from_out = swap(2 * core, outside, 1)
    to_mate.start()

    @pl.when(has_outside)
    def _():
        to_out.start()

    @pl.when(jnp.logical_not(has_outside))
    def _():
        gs[2 * core] = jnp.zeros((256, 128), BF16)

    spread.each(2, "get")
    spread.swap(core).start()
    t3[:, 0:8, :] = jnp.zeros((8, 8, 128), F32)
    t3[:, 40:48, :] = jnp.zeros((8, 8, 128), F32)

    def spread_grads(i):
        t3[:, 8:40, :] = gs[i].astype(F32).reshape(8, 32, 128)
        edge = jnp.zeros((32, 128), BF16)
        for kx in range(3):
            g3[kx, i, 0:32] = edge
            g3[kx, i, 288:320] = edge
        g3[0, i, 32:288] = t3[:, 9:41, :].reshape(256, 128).astype(BF16)
        g3[1, i, 32:288] = gs[i]
        g3[2, i, 32:288] = t3[:, 7:39, :].reshape(256, 128).astype(BF16)

    def back_second(plane, kz, first):
        def body(ky, carry):
            acc = hp[...]
            for kx in range(3):
                acc += dot_nt(g3[kx, plane, rows_from(32 * (2 - ky))], w2[9 * kz + 3 * ky + kx])
            hp[...] = acc
            return carry

        if first:
            hp[...] = jnp.zeros((256, 512), F32)
        lax.fori_loop(0, 3, body, 0)

    spread_grads(1)
    back_second(1, 1, True)
    from_mate.wait_recv()

    gc2[1, 0:256] = gs[1]
    gc2[1, 256:512] = gs[2 - 2 * core]

    def terms_second(i, carry):
        k = offset_of(i, core)
        pairs = jnp.where(k // 9 == 1, 1, 0)
        red2.d[i] = dot_nn(ht[k % 9], gc2[pairs]).reshape(4, 4, 32, 128).astype(BF16)
        return carry

    for first, last in EARLY:
        lax.fori_loop(first, last, terms_second, 0)
    red2.start_first(EARLY)

    @pl.when(has_outside)
    def _():
        from_out.wait_recv()

    spread_grads(0)
    spread_grads(2)
    back_second(0, 2, False)
    back_second(2, 0, False)

    for j in range(NF):
        ps[j] = hp[:, 128 * j : 128 * j + 128].astype(BF16)
    shares = [remote(ps.at[p], rp.at[n], psem_s.at[n], psem_r.at[n], s, p) for n, p in enumerate(peers)]
    for c in shares:
        c.start()

    gc2[0, 0:256] = gs[2 * core]
    gc2[0, 256:512] = gs[1]
    for first, last in LATE:
        lax.fori_loop(first, last, terms_second, 0)
    red2.start_first(LATE)

    for c in shares:
        c.wait_recv()
    hidden_grad = ps[f].astype(F32)
    for n in range(3):
        hidden_grad += rp[n].astype(F32)
    gf[0] = (hidden_grad * swish_slope(pre1[...])).astype(BF16)

    gf_mate = remote(gf.at[0], gf.at[1], gfsem_s.at[0], gfsem_r.at[0], mate, f)
    gf_out = remote(gf.at[0], gf.at[2], gfsem_s.at[1], gfsem_r.at[1], outside, f)
    gf_mate.start()
    sends = jnp.logical_and(core == 0, has_outside)
    gets = jnp.logical_and(core == 1, has_outside)

    @pl.when(sends)
    def _():
        gf_out.start()

    far, near = (f + 2) % NF, f + 1 - 2 * (f % 2)
    gx_own = remote(gf.at[0], gx.at[0], gx_s.at[0], gx_r.at[0], s, far)
    gx_out = remote(gf.at[2], gx.at[1], gx_s.at[1], gx_r.at[1], s, far)
    gx_give = remote(gx.at[0], gx.at[1], gx_s.at[2], gx_r.at[2], mate, f)
    gx_own.start()
    t3[:, 40:48, :] = jnp.zeros((8, 8, 128), F32)

    def spread_first(q, z, src):
        t3[:, 8:40, :] = src.astype(F32).reshape(8, 32, 128)
        for i in range(2):
            half = jnp.where(f < 2, t3[:, 8 + i : 24 + i, :], t3[:, 24 + i : 40 + i, :])
            g4[q, i, z, 0:128] = half.reshape(128, 128).astype(BF16)
            g4[q, i, z, 128:144] = jnp.zeros((16, 128), BF16)

    def taps(parity):
        return [(1, 0)] if parity == 0 else [(2, 0), (0, 1)]

    def back_first(zp):
        for yp in range(2):
            for xp in range(2):
                acc = jnp.zeros((128, 256), F32)
                for kz, oz in taps(zp):
                    for ky, oy in taps(yp):
                        for kx, ox in taps(xp):
                            k = 9 * kz + 3 * ky + kx
                            there = wx[k // HALF, k - (HALF - 1) * (k // HALF)].reshape(256, 128)
                            acc += dot_nt(g4[0, ox, oz, 16 * oy : 16 * oy + 128], w1[k])
                            acc += dot_nt(g4[1, ox, oz, 16 * oy : 16 * oy + 128], there)
                acc = acc.reshape(8, 16, 256)
                lower, upper = acc[:, 0:8, :].reshape(64, 256), acc[:, 8:16, :].reshape(64, 256)
                lanes = slice(256 * xp, 256 * xp + 256)
                k5[zp, yp, :, lanes] = jnp.where(f % 2 == 0, lower, upper)
                s5[zp, yp, :, lanes] = jnp.where(f % 2 == 0, upper, lower).astype(BF16)

    def share(zp):
        return remote(s5.at[zp], r5.at[zp], s5_s.at[zp], s5_r.at[zp], s, near)

    gf_mate.wait_recv()

    gc1[1, 0:256] = gf[core]
    gc1[1, 256:512] = gf[1 - core]

    def terms_first(i, carry):
        pairs = jnp.where(offset_of(i, core) // 9 == 1, 1, 0)
        red1.d[i] = dot_nn(at[i], gc1[pairs]).reshape(4, 4, 16, 128).astype(BF16)
        return carry

    for first, last in EARLY:
        lax.fori_loop(first, last, terms_first, 0)
    red1.start_first(EARLY)
    red2.start_second()

    @pl.when(gets)
    def _():
        gf_out.wait_recv()

    @pl.when(jnp.logical_and(core == 1, jnp.logical_not(has_outside)))
    def _():
        gf[2] = jnp.zeros((256, 128), BF16)

    gc1[0, 0:256] = gf[0]
    gc1[0, 256:512] = gf[1 + core]
    for first, last in LATE:
        lax.fori_loop(first, last, terms_first, 0)
    red1.start_first(LATE)

    @pl.when(core == 1)
    def _():
        gx_out.start()

    spread.swap(1 - core).wait_recv()
    spread_first(0, 0, gf[0])
    gx_own.wait_recv()

    @pl.when(core == 1)
    def _():
        gx_give.start()

    spread_first(1, 0, gx[0])
    back_first(0)
    even, odd = share(0), share(1)
    even.start()
    red2.start_third()
    spread_first(0, 1, gf[1 + core])

    @pl.when(core == 1)
    def _():
        gx_out.wait_recv()

    @pl.when(core == 0)
    def _():
        gx_give.wait_recv()

    spread_first(1, 1, gx[1])
    back_first(1)
    odd.start()
    red1.start_second()
    red1.start_third()
    for k, values, i in red2.finish():
        gw2_ref[k] = values[i]
    for k, values, i in red1.finish():
        gw1_ref[k] = jnp.where(core == 0, values[i, 0:4], values[i, 4:8])

    for zp, copy in enumerate((even, odd)):
        copy.wait_recv()
        gin_ref[zp] = (k5[zp] + r5[zp].astype(F32)).astype(BF16)
    for c in shares + [even, odd, gx_own, spread.fetch(), spread.swap(core)]:
        c.wait_send()
    for stage in (1, 2):
        spread.each(stage, "sent")

    @pl.when(core == 1)
    def _():
        gx_out.wait_send()
        gx_give.wait_send()

    vol_sent()
    hid_sent()
    to_mate.wait_send()
    gf_mate.wait_send()

    @pl.when(sends_part)
    def _():
        part1_copy.wait_send()

    @pl.when(has_outside)
    def _():
        part2_copy.wait_send()

    @pl.when(has_outside)
    def _():
        to_out.wait_send()

    @pl.when(sends)
    def _():
        gf_out.wait_send()


def run_whole(cells, weight_first, weight_second, cotangent):
    dma = pltpu.SemaphoreType.DMA
    vmem, anywhere = pl.BlockSpec(memory_space=pltpu.VMEM), pl.BlockSpec(memory_space=pl.ANY)
    scratch = [
        pltpu.VMEM((27, 256, 128), BF16),
        pltpu.VMEM((27, 512, 128), BF16),
        dma((2,)),
        pltpu.VMEM((4, 2, NF, 64, 512), BF16),
        pltpu.VMEM((8, 40, 512), F32),
        pltpu.VMEM((3, 4, 2, 288, 256), BF16),
        pltpu.VMEM((256, 128), F32),
        pltpu.VMEM((256, 128), BF16),
        pltpu.VMEM((2, 256, 512), BF16),
        pltpu.VMEM((8, 48, 512), F32),
        pltpu.VMEM((3, 2, 320, 512), BF16),
        pltpu.VMEM((2, 256, 128), BF16),
        pltpu.VMEM((2, 256, 128), BF16),
        dma((2,)),
        dma((2,)),
        pltpu.VMEM((3, 256, 128), BF16),
        pltpu.VMEM((8, 48, 128), F32),
        pltpu.VMEM((3, 3, 320, 128), BF16),
        dma((2,)),
        dma((2,)),
        pltpu.VMEM((256, 512), F32),
        pltpu.VMEM((NF, 256, 128), BF16),
        pltpu.VMEM((3, 256, 128), BF16),
        dma((3,)),
        dma((3,)),
        pltpu.VMEM((3, 256, 128), BF16),
        dma((2,)),
        dma((2,)),
        pltpu.VMEM((2, 2, 2, 144, 128), BF16),
        pltpu.VMEM((2, 2, 64, 512), BF16),
        pltpu.VMEM((2, 2, 64, 512), BF16),
        dma((2,)),
        dma((2,)),
        pltpu.VMEM((HALF, 256, 512), BF16),
        pltpu.VMEM((2, 2, 8, 2, 16, 128), F32),
        pltpu.VMEM((2, 2, 64, 512), BF16),
        pltpu.VMEM((9, 512, 512), BF16),
        pltpu.VMEM((2, 512, 128), BF16),
        pltpu.VMEM((2, 512, 128), BF16),
        pltpu.VMEM((2, HALF, 4, 4, 16, 128), BF16),
        dma((4, 3)),
        dma((4, 3)),
        pltpu.VMEM((2, 256, 128), BF16),
        dma((3,)),
        dma((3,)),
        pltpu.VMEM((2, 2, 64, 512), F32),
    ]
    scratch += line_sems() + direct_sems() + reduction_scratch(32) + reduction_scratch(16)
    return pl.pallas_call(
        whole_kernel,
        out_shape=(
            jax.ShapeDtypeStruct((2, 2, 64, 512), BF16),
            jax.ShapeDtypeStruct((27, 4, 128), F32),
            jax.ShapeDtypeStruct((27, 8, 128), F32),
        ),
        in_specs=[vmem, anywhere, anywhere, vmem],
        out_specs=(vmem, vmem, vmem),
        scratch_shapes=scratch,
        compiler_params=pltpu.CompilerParams(collective_id=0, has_side_effects=True, vmem_limit_bytes=52 * 2**20),
        name="bottleneck",
    )(cells, weight_first, weight_second, cotangent)


def per_device(volume, weight_first, weight_second, cotangent):
    grad, grad_first, grad_second = run_whole(volume.reshape(2, 8, 2, 16, 256), weight_first, weight_second, cotangent.reshape(256, 128))
    grad = grad.reshape(2, 2, 8, 8, 2, 256).transpose(0, 2, 1, 3, 4, 5).reshape(2, 16, 16, 256)
    return (grad, grad_first, grad_second)


def solution(mesh):
    placed = (
        P("space", None, "filt", None),
        P(None, None, "filt"),
        P(None, None, "filt"),
        P("space", None, None, "filt"),
    )
    return jax.shard_map(
        per_device,
        mesh=mesh,
        in_specs=placed,
        out_specs=(
            P("space", None, "filt", None),
            P(None, "space", "filt"),
            P(None, "space", "filt"),
        ),
        check_vma=False,
    )
```

```python
import functools

import jax
import jax.numpy as jnp
from jax import lax
from jax.experimental import pallas as pl
from jax.experimental.pallas import tpu as pltpu
from jax.sharding import PartitionSpec as P

BF16 = jnp.bfloat16
F32 = jnp.float32
MESH = pl.DeviceIdType.MESH
NS = 64
NF = 4
HALF = 14


def place():
    s = lax.axis_index("space")
    f = lax.axis_index("filt")
    return s, f


def remote(src, dst, send, recv, s, f):
    return pltpu.make_async_remote_copy(
        src_ref=src,
        dst_ref=dst,
        send_sem=send,
        recv_sem=recv,
        device_id={"space": s, "filt": f},
        device_id_type=MESH,
    )


def greet(partners):
    barrier = pltpu.get_barrier_semaphore()
    total = 0
    for cond, s, f in partners:
        if cond is True:
            pl.semaphore_signal(barrier, inc=1, device_id={"space": s, "filt": f}, device_id_type=MESH)
            total = total + 1
        else:

            @pl.when(cond)
            def _():
                pl.semaphore_signal(barrier, inc=1, device_id={"space": s, "filt": f}, device_id_type=MESH)

            total = total + cond.astype(jnp.int32)
    pl.semaphore_wait(barrier, total)


def line_gather(own, main, sems, work):
    line_send, line_recv, pair_send, pair_recv, local = sems
    s, f = place()
    mate = s + 1 - 2 * (s % 2)

    keep = [pltpu.make_async_copy(own.at[p], main(f, p), local.at[p]) for p in range(2)]
    for copy in keep:
        copy.start()

    def line_copy(t, way, block, p):
        to = f + 1 if way == 0 else f - 1
        view = main(block, p)
        return remote(own.at[p] if t == 0 else view, view, line_send.at[way, t, p], line_recv.at[way, t, p], s, to)

    def sent_block(t, way):
        return f - t if way == 0 else f + t

    def got_block(t, way):
        return f - 1 - t if way == 0 else f + 1 + t

    def may_send(t, way):
        if way == 0:
            return jnp.logical_and(f < NF - 1, f >= t)
        return jnp.logical_and(f > 0, f + t < NF)

    def may_get(t, way):
        return f > t if way == 0 else f + t < NF - 1

    def send(t, way, p):
        @pl.when(may_send(t, way))
        def _():
            line_copy(t, way, sent_block(t, way), p).start()

    def get(t, way, p):
        @pl.when(may_get(t, way))
        def _():
            line_copy(t, way, got_block(t, way), p).wait_recv()

    def pair_copy(slot, p, view):
        return remote(view, view, pair_send.at[slot, p], pair_recv.at[slot, p], mate, f)

    def pair_start(t, way, p):
        @pl.when(may_get(t, way))
        def _():
            pair_copy(1 + 3 * way + t, p, main(got_block(t, way), p)).start()

    for p in (1, 0):
        for way in range(2):
            send(0, way, p)
    for p in (1, 0):
        keep[p].wait()
        pair_copy(0, p, main(f, p)).start()
    for t in range(NF - 1):
        for p in (1, 0):
            for way in range(2):
                get(t, way, p)
                if t < NF - 2:
                    send(t + 1, way, p)
                pair_start(t, way, p)
            if t == NF - 2 and p == 1:
                work()

    def wait_pair(theirs):
        for p in range(2):
            pair_copy(0, p, theirs(f, p)).wait_recv()
        for t in range(NF - 1):
            for way in range(2):

                @pl.when(may_get(t, way))
                def _():
                    for p in range(2):
                        pair_copy(1 + 3 * way + t, p, theirs(got_block(t, way), p)).wait_recv()

    def wait_sent():
        for p in range(2):
            pair_copy(0, p, main(f, p)).wait_send()
        for t in range(NF - 1):
            for way in range(2):

                @pl.when(may_send(t, way))
                def _():
                    for p in range(2):
                        line_copy(t, way, sent_block(t, way), p).wait_send()

                @pl.when(may_get(t, way))
                def _():
                    for p in range(2):
                        pair_copy(1 + 3 * way + t, p, main(got_block(t, way), p)).wait_send()

    return wait_pair, wait_sent


def line_sems():
    dma = pltpu.SemaphoreType.DMA
    return [dma((2, 3, 2)), dma((2, 3, 2)), dma((7, 2)), dma((7, 2)), dma((2,))]


def direct_gather(own, main, sems, work):
    send, recv, pair_send, pair_recv, local = sems
    s, f = place()
    mate = s + 1 - 2 * (s % 2)
    sent = [remote(own, main(f), send.at[n], recv.at[n], s, (f + n + 1) % NF) for n in range(3)]
    for copy in sent:
        copy.start()
    keep = pltpu.make_async_copy(own, main(f), local.at[0])
    keep.start()

    def pair_copy(n, view):
        return remote(view, view, pair_send.at[n], pair_recv.at[n], mate, f)

    blocks = [(f + NF - n - 1) % NF for n in range(3)] + [f]
    keep.wait()
    pair_copy(3, main(f)).start()
    work()
    for n in (0, 2, 1):
        remote(own, main(blocks[n]), send.at[n], recv.at[n], s, blocks[n]).wait_recv()
        pair_copy(n, main(blocks[n])).start()

    def wait_pair(theirs):
        for n in range(4):
            pair_copy(n, theirs(blocks[n])).wait_recv()

    def wait_sent():
        for copy in sent:
            copy.wait_send()
        for n in range(4):
            pair_copy(n, main(blocks[n])).wait_send()

    return wait_pair, wait_sent


def direct_sems():
    dma = pltpu.SemaphoreType.DMA
    return [dma((3,)), dma((3,)), dma((4,)), dma((4,)), dma((1,))]


def offset_of(slot, core):
    n = jnp.where(slot < 3, slot, jnp.where(slot < 7, slot + 2, jnp.where(slot < 9, slot - 4, slot)))
    return jnp.where(core == 0, HALF - 1 + n, (n + 9) % HALF)


def offsets(core):
    order = [0, 1, 2, 5, 6, 7, 8, 3, 4, 9, 10, 11, 12, 13]
    return [HALF - 1 + n if core == 0 else (n + 9) % HALF for n in order]


EARLY, LATE = ((0, 3), (7, 9)), ((3, 7), (9, 14))


class Spread:
    def __init__(self, w1, wx, send, recv):
        self.w1, self.wx, self.send, self.recv = w1, wx, send, recv
        self.s, self.f = place()
        s = self.s
        self.x, self.y, self.zh, self.core = s // 16, (s // 4) % 4, (s // 2) % 2, s % 2

    def copy(self, stage, n, src, dst, x, y, core, f):
        to = ((x * 4 + y) * 2 + self.zh) * 2 + core
        return remote(src, dst, self.send.at[stage, n], self.recv.at[stage, n], to, f)

    def fetch(self):
        part = pl.ds(pl.multiple_of(16 * (4 * self.x + self.y), 16), 16)
        src = self.w1.at[pl.ds((HALF - 1) * self.core, HALF), part]
        dst = self.wx.at[self.core, :, self.x, self.y]
        return self.copy(0, 0, src, dst, self.x, self.y, self.core, (self.f + 2) % NF)

    def over(self, stage, c, n, got):
        x, y = self.x, self.y
        step = NF - n - 1 if got else n + 1
        along_x = (stage == 1) == (c == 0)
        px, py = ((x + step) % 4, y) if along_x else (x, (y + step) % 4)
        hx, hy = (px, py) if got else (x, y)
        if stage == 1:
            view = self.wx.at[c, :, hx, hy]
        else:
            view = self.wx.at[c, :, hx] if along_x else self.wx.at[c, :, :, hy]
        return self.copy(stage, n, view, view, px, py, c, self.f)

    def each(self, stage, what):
        for c in range(2):

            @pl.when(self.core == c)
            def _():
                for n in range(3):
                    if what == "start":
                        self.over(stage, c, n, False).start()
                    elif what == "get":
                        self.over(stage, c, n, True).wait_recv()
                    else:
                        self.over(stage, c, n, False).wait_send()

    def swap(self, c):
        view = self.wx.at[c]
        return self.copy(3, 0, view, view, self.x, self.y, 1 - self.core, self.f)


class Reduction:
    def __init__(self, rows, d, r1x, r1y, ex, ey, r2x, r2y, total, t_send, r3, send, recv):
        self.rows, self.d, self.r1x, self.r1y, self.ex, self.ey = rows, d, r1x, r1y, ex, ey
        self.r2x, self.r2y, self.total, self.t_send, self.r3 = r2x, r2y, total, t_send, r3
        self.send, self.recv = send, recv
        self.s, self.f = place()
        s = self.s
        self.x, self.y, self.zh, self.core = s // 16, (s // 4) % 4, (s // 2) % 2, s % 2
        self.xs = [(self.x + n) % 4 for n in (1, 2, 3)]
        self.ys = [(self.y + n) % 4 for n in (1, 2, 3)]
        self.ends = [(1 - self.zh, self.core), (self.zh, 1 - self.core), (1 - self.zh, 1 - self.core)]
        self.first = []

    def copy(self, src, dst, stage, way, n, x, y, zh, core):
        to = ((x * 4 + y) * 2 + zh) * 2 + core
        return remote(src, dst, self.send.at[stage, way, n], self.recv.at[stage, way, n], to, self.f)

    def start_first(self, group):
        half = HALF // 2
        stage = 0 if group is EARLY else 3
        (x0, x1), (y0, y1) = group
        made = []
        for n in range(3):
            a, b = self.xs[n], self.ys[n]
            src, dst = self.d.at[pl.ds(x0, x1 - x0), a], self.r1x.at[n, pl.ds(x0, x1 - x0)]
            made.append(self.copy(src, dst, stage, 0, n, a, self.y, self.zh, self.core))
            src, dst = self.d.at[pl.ds(y0, y1 - y0), :, b], self.r1y.at[n, pl.ds(y0 - half, y1 - y0)]
            made.append(self.copy(src, dst, stage, 1, n, self.x, b, self.zh, self.core))
        for c in made:
            c.start()
        self.first += made

    def start_second(self):
        half = HALF // 2
        d, x, y = self.d, self.x, self.y

        def over_x(i, carry):
            acc = d[i, x].astype(F32)
            for n in range(3):
                acc += self.r1x[n, i].astype(F32)
            self.ex[i] = acc.astype(BF16)
            return carry

        def over_y(i, carry):
            acc = d[half + i, :, y].astype(F32)
            for n in range(3):
                acc += self.r1y[n, i].astype(F32)
            self.ey[i] = acc.astype(BF16)
            return carry

        self.second = [[], []]
        for way, body in enumerate((over_x, over_y)):
            for c in self.first[way::2]:
                c.wait_recv()
            lax.fori_loop(0, half, body, 0)
            for n in range(3):
                a, b = self.xs[n], self.ys[n]
                if way == 0:
                    c = self.copy(self.ex.at[:, b], self.r2x.at[n], 1, 0, n, x, b, self.zh, self.core)
                else:
                    c = self.copy(self.ey.at[:, a], self.r2y.at[n], 1, 1, n, a, y, self.zh, self.core)
                c.start()
                self.second[way].append(c)

    def start_third(self):
        half = HALF // 2
        x, y = self.x, self.y

        def over_y(i, carry):
            acc = self.ex[i, y].astype(F32)
            for n in range(3):
                acc += self.r2x[n, i].astype(F32)
            self.total[i] = acc
            return carry

        def over_x(i, carry):
            acc = self.ey[i, x].astype(F32)
            for n in range(3):
                acc += self.r2y[n, i].astype(F32)
            self.total[half + i] = acc
            return carry

        for way, body in enumerate((over_y, over_x)):
            for c in self.second[way]:
                c.wait_recv()
            lax.fori_loop(0, half, body, 0)
        for a in range(2):
            for b in range(2):
                start = 16 * a + 8 * b if self.rows == 32 else 8 * a
                piece = self.total[:, start : start + 8]
                self.t_send[2 * a + b] = piece.reshape(half, 16, 128).astype(BF16)
        self.third = []
        for n, (a, b) in enumerate(self.ends):
            self.third.append(self.copy(self.t_send.at[2 * a + b], self.r3.at[n], 2, 0, n, x, y, a, b))
        for c in self.third:
            c.start()

    def finish(self):
        for c in self.third:
            c.wait_recv()
        start = 16 * self.zh + 8 * self.core if self.rows == 32 else 8 * self.zh
        got = [self.r3[n].astype(F32).reshape(HALF, 8, 128) for n in range(3)]
        mine = self.total[:, pl.ds(pl.multiple_of(start, 8), 8)] + got[0]
        other = got[1] + got[2]
        low = jnp.where(self.core == 1, mine, other)
        high = jnp.where(self.core == 1, other, mine)
        for c in self.first + self.second[0] + self.second[1] + self.third:
            c.wait_send()
        return [(k, low, i) for i, k in enumerate(offsets(1))] + [(k, high, i) for i, k in enumerate(offsets(0)) if k >= HALF]


def reduction_scratch(rows):
    half = HALF // 2
    dma = pltpu.SemaphoreType.DMA
    return [
        pltpu.VMEM((HALF, 4, 4, rows, 128), BF16),
        pltpu.VMEM((3, half, 4, rows, 128), BF16),
        pltpu.VMEM((3, half, 4, rows, 128), BF16),
        pltpu.VMEM((half, 4, rows, 128), BF16),
        pltpu.VMEM((half, 4, rows, 128), BF16),
        pltpu.VMEM((3, half, rows, 128), BF16),
        pltpu.VMEM((3, half, rows, 128), BF16),
        pltpu.VMEM((HALF, rows, 128), F32),
        pltpu.VMEM((4, half, 16, 128), BF16),
        pltpu.VMEM((3, half, 16, 128), BF16),
        dma((4, 2, 3)),
        dma((4, 2, 3)),
    ]


def swish_slope(pre):
    logistic = jax.nn.sigmoid(pre)
    return logistic * (1.0 + pre * (1.0 - logistic))


def dot_nn(a, b):
    return lax.dot_general(a, b, (((1,), (0,)), ((), ())), preferred_element_type=F32)


def dot_nt(a, b):
    return lax.dot_general(a, b, (((1,), (1,)), ((), ())), preferred_element_type=F32)


def dot_tn(a, b):
    return lax.dot_general(a, b, (((0,), (0,)), ((), ())), preferred_element_type=F32)


def rows_from(start):
    return pl.ds(pl.multiple_of(start, 32), 256)


def whole_kernel(
    v_ref, w1_hbm, w2_hbm, cot_ref, gin_ref, gw1_ref, gw2_ref,
    w1, w2, wsem, vg, t1, a1, pre1, hown, hg, t2, h3, part1, part2, part_s, part_r,
    gs, t3, g3, gsem_s, gsem_r, hp, ps, rp, psem_s, psem_r, gf, gfsem_s, gfsem_r, g4, s5, r5, s5_s, s5_r, at, split, vown, ht, gc2, gc1, wx, wx_s, wx_r, gx, gx_s, gx_r, k5,
    *rest,
):
    nsem = 5
    vsems, hsems = rest[:nsem], rest[nsem : 2 * nsem]
    red2 = Reduction(32, *rest[2 * nsem : 2 * nsem + 12])
    red1 = Reduction(16, *rest[2 * nsem + 12 :])
    s, f = place()
    core, zh = s % 2, (s // 2) % 2
    mate = s + 1 - 2 * core
    outside = s - 1 + 2 * core
    has_outside = jnp.logical_and(outside >= 0, outside < NS)
    peers = [(f + n) % NF for n in (1, 2, 3)]

    load1 = pltpu.make_async_copy(w1_hbm, w1, wsem.at[0])
    load2 = pltpu.make_async_copy(w2_hbm, w2, wsem.at[1])
    load1.start()
    load2.start()

    def dev(x_, y_, zh_, core_):
        return ((x_ * 4 + y_) * 2 + zh_) * 2 + core_

    for c in range(2):
        split[c] = v_ref[:, :, :, :, 128 * c : 128 * c + 128].astype(F32)
        for plane in range(2):
            for parity in range(2):
                for half in range(2):
                    part = split[c, plane, :, parity, pl.ds(half, 8, stride=2), :]
                    lane = 256 * half + 128 * c
                    vown[plane, parity, :, lane : lane + 128] = part.reshape(64, 128).astype(BF16)

    partners = [(True, s, p) for p in peers]
    partners += [(True, mate, f), (has_outside, outside, f)]
    partners += [(True, dev(a, red2.y, zh, core), f) for a in red2.xs]
    partners += [(True, dev(red2.x, b, zh, core), f) for b in red2.ys]
    partners += [(True, dev(red2.x, red2.y, 1 - zh, b), f) for b in (core, 1 - core)]
    greet(partners)
    spread = Spread(w1, wx, wx_s, wx_r)

    def part_copy(slot, buf):
        return remote(buf.at[0], buf.at[1], part_s.at[slot], part_r.at[slot], outside, f)

    def vol(c, j, p):
        return vg.at[2 * c + p, :, j]

    t1[:, 0:8, :] = jnp.zeros((8, 8, 512), F32)

    def cells(i, carry):
        plane, parity = i // 2, i % 2
        for j in range(NF):
            t1[:, 8 + 8 * j : 16 + 8 * j, :] = vg[plane, parity, j].astype(F32).reshape(8, 8, 512)
        edge = jnp.zeros((32, 256), BF16)
        for kx in range(3):
            a1[kx, plane, parity, 0:32] = edge
        a1[0, plane, parity, 32:288] = t1[:, 7:39, 256:512].reshape(256, 256).astype(BF16)
        a1[1, plane, parity, 32:288] = t1[:, 8:40, 0:256].reshape(256, 256).astype(BF16)
        a1[2, plane, parity, 32:288] = t1[:, 8:40, 256:512].reshape(256, 256).astype(BF16)
        return carry

    def taps_first(plane, kz):
        def body(ky, acc):
            parity, start = (ky + 1) % 2, jnp.minimum(ky, 1)
            for kx in range(3):
                acc += dot_nn(a1[kx, plane, parity, rows_from(32 * start)], w1[9 * kz + 3 * ky + kx])
            return acc

        return lax.fori_loop(0, 3, body, jnp.zeros((256, 128), F32))

    sends_part = jnp.logical_and(core == 1, has_outside)
    gets_part = jnp.logical_and(core == 0, has_outside)
    part1_copy = part_copy(0, part1)

    def top_plane():
        load1.wait()
        lax.fori_loop(4 * core + 2, 4 * core + 4, cells, 0)

        @pl.when(sends_part)
        def _():
            part1[0] = taps_first(3, 0).astype(BF16)
            part1_copy.start()

    vol_wait, vol_sent = line_gather(vown, lambda j, p: vol(core, j, p), vsems, top_plane)
    spread.fetch().start()
    lax.fori_loop(4 * core, 4 * core + 2, cells, 0)
    pre1[...] = taps_first(2 * core, 1) + taps_first(2 * core + 1, 2)
    vol_wait(lambda j, p: vol(1 - core, j, p))

    @pl.when(core == 1)
    def _():
        lax.fori_loop(2, 4, cells, 0)
        pre1[...] += taps_first(1, 0)

    @pl.when(gets_part)
    def _():
        part1_copy.wait_recv()
        pre1[...] += part1[1].astype(F32)

    pre_first = pre1[...]
    hown[...] = (pre_first * jax.nn.sigmoid(pre_first)).astype(BF16)

    def hid(plane, j):
        return hg.at[plane, :, pl.ds(pl.multiple_of(128 * j, 128), 128)]

    def turn(i, carry):
        k = offset_of(i, core)
        kz, ky, kx = k // 9, (k // 3) % 3, k % 3
        parity, start = (ky + 1) % 2, jnp.minimum(ky, 1)
        plane = jnp.where(kz == 1, 0, 1)
        at[i, :, 0:256] = a1[kx, plane, parity, rows_from(32 * start)].T
        at[i, :, 256:512] = a1[kx, plane + 2, parity, rows_from(32 * start)].T
        return carry

    def windows():
        spread.fetch().wait_recv()
        spread.each(1, "start")
        lax.fori_loop(4 - 4 * core, 8 - 6 * core, cells, 0)
        lax.fori_loop(0, HALF, turn, 0)

    hid_wait, hid_sent = direct_gather(hown, lambda j: hid(core, j), hsems, windows)

    t2[:, 0:8, :] = jnp.zeros((8, 8, 512), F32)
    t2[:, 40:48, :] = jnp.zeros((8, 8, 512), F32)

    def spread_hidden(i):
        t2[:, 8:40, :] = hg[i].astype(F32).reshape(8, 32, 512)
        edge = jnp.zeros((32, 512), BF16)
        for kx in range(3):
            h3[kx, i, 0:32] = edge
            h3[kx, i, 288:320] = edge
        h3[0, i, 32:288] = t2[:, 7:39, :].reshape(256, 512).astype(BF16)
        h3[1, i, 32:288] = hg[i]
        h3[2, i, 32:288] = t2[:, 9:41, :].reshape(256, 512).astype(BF16)

    def taps_second(plane, kz):
        def body(ky, acc):
            for kx in range(3):
                acc += dot_nn(h3[kx, plane, rows_from(32 * ky)], w2[9 * kz + 3 * ky + kx])
            return acc

        return lax.fori_loop(0, 3, body, jnp.zeros((256, 128), F32))

    load2.wait()
    spread_hidden(core)
    part2_copy = part_copy(1, part2)

    @pl.when(has_outside)
    def _():
        part2[0] = taps_second(core, 2 - 2 * core).astype(BF16)
        part2_copy.start()

    pre_second = taps_second(core, 1)
    hid_wait(lambda j: hid(1 - core, j))
    spread_hidden(1 - core)
    pre_second += taps_second(1 - core, 2 - 2 * core)

    def turn_hidden(i, carry):
        ky, kx = i // 3, i % 3
        ht[i, :, 0:256] = h3[kx, core, rows_from(32 * ky)].T
        ht[i, :, 256:512] = h3[kx, 1 - core, rows_from(32 * ky)].T
        return carry

    lax.fori_loop(4 - 4 * core, 9 - 4 * core, turn_hidden, 0)

    @pl.when(jnp.logical_not(has_outside))
    def _():
        part2[1] = jnp.zeros((256, 128), BF16)

    @pl.when(has_outside)
    def _():
        part2_copy.wait_recv()

    pre_second += part2[1].astype(F32)
    gs[1] = (cot_ref[...].astype(F32) * swish_slope(pre_second)).astype(BF16)

    spread.each(1, "get")
    spread.each(2, "start")

    def swap(place_there, to, slot):
        return remote(gs.at[1], gs.at[place_there], gsem_s.at[slot], gsem_r.at[slot], to, f)

    to_mate = swap(2 * core, mate, 0)
    to_out = swap(2 - 2 * core, outside, 1)
    from_mate = swap(2 - 2 * core, mate, 0)
    from_out = swap(2 * core, outside, 1)
    to_mate.start()

    @pl.when(has_outside)
    def _():
        to_out.start()

    @pl.when(jnp.logical_not(has_outside))
    def _():
        gs[2 * core] = jnp.zeros((256, 128), BF16)

    t3[:, 0:8, :] = jnp.zeros((8, 8, 128), F32)
    t3[:, 40:48, :] = jnp.zeros((8, 8, 128), F32)

    def spread_grads(i):
        t3[:, 8:40, :] = gs[i].astype(F32).reshape(8, 32, 128)
        edge = jnp.zeros((32, 128), BF16)
        for kx in range(3):
            g3[kx, i, 0:32] = edge
            g3[kx, i, 288:320] = edge
        g3[0, i, 32:288] = t3[:, 9:41, :].reshape(256, 128).astype(BF16)
        g3[1, i, 32:288] = gs[i]
        g3[2, i, 32:288] = t3[:, 7:39, :].reshape(256, 128).astype(BF16)

    def back_second(plane, kz, first):
        def body(ky, carry):
            acc = hp[...]
            for kx in range(3):
                acc += dot_nt(g3[kx, plane, rows_from(32 * (2 - ky))], w2[9 * kz + 3 * ky + kx])
            hp[...] = acc
            return carry

        if first:
            hp[...] = jnp.zeros((256, 512), F32)
        lax.fori_loop(0, 3, body, 0)

    spread_grads(1)
    back_second(1, 1, True)
    from_mate.wait_recv()
    spread_grads(2 - 2 * core)
    back_second(2 - 2 * core, 2 * core, False)

    gc2[1, 0:256] = gs[1]
    gc2[1, 256:512] = gs[2 - 2 * core]

    def terms_second(i, carry):
        k = offset_of(i, core)
        pairs = jnp.where(k // 9 == 1, 1, 0)
        red2.d[i] = dot_nn(ht[k % 9], gc2[pairs]).reshape(4, 4, 32, 128).astype(BF16)
        return carry

    for first, last in EARLY:
        lax.fori_loop(first, last, terms_second, 0)
    red2.start_first(EARLY)
    lax.fori_loop(5 * core, 4 + 5 * core, turn_hidden, 0)

    @pl.when(has_outside)
    def _():
        from_out.wait_recv()

    spread_grads(2 * core)
    back_second(2 * core, 2 - 2 * core, False)

    for j in range(NF):
        ps[j] = hp[:, 128 * j : 128 * j + 128].astype(BF16)
    shares = [remote(ps.at[p], rp.at[n], psem_s.at[n], psem_r.at[n], s, p) for n, p in enumerate(peers)]
    for c in shares:
        c.start()

    gc2[0, 0:256] = gs[2 * core]
    gc2[0, 256:512] = gs[1]
    for first, last in LATE:
        lax.fori_loop(first, last, terms_second, 0)
    red2.start_first(LATE)
    spread.each(2, "get")
    spread.swap(core).start()

    for c in shares:
        c.wait_recv()
    hidden_grad = ps[f].astype(F32)
    for n in range(3):
        hidden_grad += rp[n].astype(F32)
    gf[0] = (hidden_grad * swish_slope(pre1[...])).astype(BF16)

    gf_mate = remote(gf.at[0], gf.at[1], gfsem_s.at[0], gfsem_r.at[0], mate, f)
    gf_out = remote(gf.at[0], gf.at[2], gfsem_s.at[1], gfsem_r.at[1], outside, f)
    sends = jnp.logical_and(core == 0, has_outside)
    gets = jnp.logical_and(core == 1, has_outside)

    @pl.when(sends)
    def _():
        gf_out.start()

    gf_mate.start()

    far, near = (f + 2) % NF, f + 1 - 2 * (f % 2)
    gx_own = remote(gf.at[0], gx.at[0], gx_s.at[0], gx_r.at[0], s, far)
    gx_out = remote(gf.at[2], gx.at[1], gx_s.at[1], gx_r.at[1], s, far)
    gx_give = remote(gx.at[0], gx.at[1], gx_s.at[2], gx_r.at[2], mate, f)
    t3[:, 40:48, :] = jnp.zeros((8, 8, 128), F32)

    def spread_first(q, z, src):
        t3[:, 8:40, :] = src.astype(F32).reshape(8, 32, 128)
        for i in range(2):
            half = jnp.where(f < 2, t3[:, 8 + i : 24 + i, :], t3[:, 24 + i : 40 + i, :])
            g4[q, i, z, 0:128] = half.reshape(128, 128).astype(BF16)
            g4[q, i, z, 128:144] = jnp.zeros((16, 128), BF16)

    def taps(parity):
        return [(1, 0)] if parity == 0 else [(2, 0), (0, 1)]

    def back_first(zp):
        for yp in range(2):
            for xp in range(2):
                acc = jnp.zeros((128, 256), F32)
                for kz, oz in taps(zp):
                    for ky, oy in taps(yp):
                        for kx, ox in taps(xp):
                            k = 9 * kz + 3 * ky + kx
                            there = wx[k // HALF, k - (HALF - 1) * (k // HALF)].reshape(256, 128)
                            acc += dot_nt(g4[0, ox, oz, 16 * oy : 16 * oy + 128], w1[k])
                            acc += dot_nt(g4[1, ox, oz, 16 * oy : 16 * oy + 128], there)
                acc = acc.reshape(8, 16, 256)
                lower, upper = acc[:, 0:8, :].reshape(64, 256), acc[:, 8:16, :].reshape(64, 256)
                lanes = slice(256 * xp, 256 * xp + 256)
                k5[zp, yp, :, lanes] = jnp.where(f % 2 == 0, lower, upper)
                s5[zp, yp, :, lanes] = jnp.where(f % 2 == 0, upper, lower).astype(BF16)

    def share(zp):
        return remote(s5.at[zp], r5.at[zp], s5_s.at[zp], s5_r.at[zp], s, near)

    gf_mate.wait_recv()

    gc1[1, 0:256] = gf[core]
    gc1[1, 256:512] = gf[1 - core]

    def terms_first(i, carry):
        pairs = jnp.where(offset_of(i, core) // 9 == 1, 1, 0)
        red1.d[i] = dot_nn(at[i], gc1[pairs]).reshape(4, 4, 16, 128).astype(BF16)
        return carry

    for first, last in EARLY:
        lax.fori_loop(first, last, terms_first, 0)
    red1.start_first(EARLY)
    gx_own.start()
    red2.start_second()

    @pl.when(gets)
    def _():
        gf_out.wait_recv()

    @pl.when(jnp.logical_and(core == 1, jnp.logical_not(has_outside)))
    def _():
        gf[2] = jnp.zeros((256, 128), BF16)

    gc1[0, 0:256] = gf[0]
    gc1[0, 256:512] = gf[1 + core]
    for first, last in LATE:
        lax.fori_loop(first, last, terms_first, 0)
    red1.start_first(LATE)

    @pl.when(core == 1)
    def _():
        gx_out.start()

    spread.swap(1 - core).wait_recv()
    spread_first(0, 0, gf[0])
    gx_own.wait_recv()

    @pl.when(core == 1)
    def _():
        gx_give.start()

    spread_first(1, 0, gx[0])
    back_first(0)
    even, odd = share(0), share(1)
    even.start()
    red2.start_third()
    spread_first(0, 1, gf[1 + core])

    @pl.when(core == 1)
    def _():
        gx_out.wait_recv()

    @pl.when(core == 0)
    def _():
        gx_give.wait_recv()

    spread_first(1, 1, gx[1])
    back_first(1)
    odd.start()
    red1.start_second()
    red1.start_third()
    for k, values, i in red2.finish():
        gw2_ref[k] = values[i]
    for k, values, i in red1.finish():
        gw1_ref[k] = jnp.where(core == 0, values[i, 0:4], values[i, 4:8])

    for zp, copy in enumerate((even, odd)):
        copy.wait_recv()
        gin_ref[zp] = (k5[zp] + r5[zp].astype(F32)).astype(BF16)
    for c in shares + [even, odd, gx_own, spread.fetch(), spread.swap(core)]:
        c.wait_send()
    for stage in (1, 2):
        spread.each(stage, "sent")

    @pl.when(core == 1)
    def _():
        gx_out.wait_send()
        gx_give.wait_send()

    vol_sent()
    hid_sent()
    to_mate.wait_send()
    gf_mate.wait_send()

    @pl.when(sends_part)
    def _():
        part1_copy.wait_send()

    @pl.when(has_outside)
    def _():
        part2_copy.wait_send()

    @pl.when(has_outside)
    def _():
        to_out.wait_send()

    @pl.when(sends)
    def _():
        gf_out.wait_send()


def run_whole(cells, weight_first, weight_second, cotangent):
    dma = pltpu.SemaphoreType.DMA
    vmem, anywhere = pl.BlockSpec(memory_space=pltpu.VMEM), pl.BlockSpec(memory_space=pl.ANY)
    scratch = [
        pltpu.VMEM((27, 256, 128), BF16),
        pltpu.VMEM((27, 512, 128), BF16),
        dma((2,)),
        pltpu.VMEM((4, 2, NF, 64, 512), BF16),
        pltpu.VMEM((8, 40, 512), F32),
        pltpu.VMEM((3, 4, 2, 288, 256), BF16),
        pltpu.VMEM((256, 128), F32),
        pltpu.VMEM((256, 128), BF16),
        pltpu.VMEM((2, 256, 512), BF16),
        pltpu.VMEM((8, 48, 512), F32),
        pltpu.VMEM((3, 2, 320, 512), BF16),
        pltpu.VMEM((2, 256, 128), BF16),
        pltpu.VMEM((2, 256, 128), BF16),
        dma((2,)),
        dma((2,)),
        pltpu.VMEM((3, 256, 128), BF16),
        pltpu.VMEM((8, 48, 128), F32),
        pltpu.VMEM((3, 3, 320, 128), BF16),
        dma((2,)),
        dma((2,)),
        pltpu.VMEM((256, 512), F32),
        pltpu.VMEM((NF, 256, 128), BF16),
        pltpu.VMEM((3, 256, 128), BF16),
        dma((3,)),
        dma((3,)),
        pltpu.VMEM((3, 256, 128), BF16),
        dma((2,)),
        dma((2,)),
        pltpu.VMEM((2, 2, 2, 144, 128), BF16),
        pltpu.VMEM((2, 2, 64, 512), BF16),
        pltpu.VMEM((2, 2, 64, 512), BF16),
        dma((2,)),
        dma((2,)),
        pltpu.VMEM((HALF, 256, 512), BF16),
        pltpu.VMEM((2, 2, 8, 2, 16, 128), F32),
        pltpu.VMEM((2, 2, 64, 512), BF16),
        pltpu.VMEM((9, 512, 512), BF16),
        pltpu.VMEM((2, 512, 128), BF16),
        pltpu.VMEM((2, 512, 128), BF16),
        pltpu.VMEM((2, HALF, 4, 4, 16, 128), BF16),
        dma((4, 3)),
        dma((4, 3)),
        pltpu.VMEM((2, 256, 128), BF16),
        dma((3,)),
        dma((3,)),
        pltpu.VMEM((2, 2, 64, 512), F32),
    ]
    scratch += line_sems() + direct_sems() + reduction_scratch(32) + reduction_scratch(16)
    return pl.pallas_call(
        whole_kernel,
        out_shape=(
            jax.ShapeDtypeStruct((2, 2, 64, 512), BF16),
            jax.ShapeDtypeStruct((27, 4, 128), F32),
            jax.ShapeDtypeStruct((27, 8, 128), F32),
        ),
        in_specs=[vmem, anywhere, anywhere, vmem],
        out_specs=(vmem, vmem, vmem),
        scratch_shapes=scratch,
        compiler_params=pltpu.CompilerParams(collective_id=0, has_side_effects=True, vmem_limit_bytes=52 * 2**20),
        name="bottleneck",
    )(cells, weight_first, weight_second, cotangent)


def per_device(volume, weight_first, weight_second, cotangent):
    grad, grad_first, grad_second = run_whole(volume.reshape(2, 8, 2, 16, 256), weight_first, weight_second, cotangent.reshape(256, 128))
    grad = grad.reshape(2, 2, 8, 8, 2, 256).transpose(0, 2, 1, 3, 4, 5).reshape(2, 16, 16, 256)
    return (grad, grad_first, grad_second)


def solution(mesh):
    placed = (
        P("space", None, "filt", None),
        P(None, None, "filt"),
        P(None, None, "filt"),
        P("space", None, None, "filt"),
    )
    return jax.shard_map(
        per_device,
        mesh=mesh,
        in_specs=placed,
        out_specs=(
            P("space", None, "filt", None),
            P(None, "space", "filt"),
            P(None, "space", "filt"),
        ),
        check_vma=False,
    )
```

```python
import functools

import jax
import jax.numpy as jnp
from jax import lax
from jax.experimental import pallas as pl
from jax.experimental.pallas import tpu as pltpu
from jax.sharding import PartitionSpec as P

BF16 = jnp.bfloat16
F32 = jnp.float32
MESH = pl.DeviceIdType.MESH
NS = 64
NF = 4
HALF = 14


def place():
    s = lax.axis_index("space")
    f = lax.axis_index("filt")
    return s, f


def remote(src, dst, send, recv, s, f):
    return pltpu.make_async_remote_copy(
        src_ref=src,
        dst_ref=dst,
        send_sem=send,
        recv_sem=recv,
        device_id={"space": s, "filt": f},
        device_id_type=MESH,
    )


def greet(partners):
    barrier = pltpu.get_barrier_semaphore()
    total = 0
    for cond, s, f in partners:
        if cond is True:
            pl.semaphore_signal(barrier, inc=1, device_id={"space": s, "filt": f}, device_id_type=MESH)
            total = total + 1
        else:

            @pl.when(cond)
            def _():
                pl.semaphore_signal(barrier, inc=1, device_id={"space": s, "filt": f}, device_id_type=MESH)

            total = total + cond.astype(jnp.int32)
    pl.semaphore_wait(barrier, total)


def line_gather(own, main, sems, work):
    line_send, line_recv, pair_send, pair_recv, local = sems
    s, f = place()
    mate = s + 1 - 2 * (s % 2)

    keep = [pltpu.make_async_copy(own.at[p], main(f, p), local.at[p]) for p in range(2)]
    for copy in keep:
        copy.start()

    def line_copy(t, way, block, p):
        to = f + 1 if way == 0 else f - 1
        view = main(block, p)
        return remote(own.at[p] if t == 0 else view, view, line_send.at[way, t, p], line_recv.at[way, t, p], s, to)

    def sent_block(t, way):
        return f - t if way == 0 else f + t

    def got_block(t, way):
        return f - 1 - t if way == 0 else f + 1 + t

    def may_send(t, way):
        if way == 0:
            return jnp.logical_and(f < NF - 1, f >= t)
        return jnp.logical_and(f > 0, f + t < NF)

    def may_get(t, way):
        return f > t if way == 0 else f + t < NF - 1

    def send(t, way, p):
        @pl.when(may_send(t, way))
        def _():
            line_copy(t, way, sent_block(t, way), p).start()

    def get(t, way, p):
        @pl.when(may_get(t, way))
        def _():
            line_copy(t, way, got_block(t, way), p).wait_recv()

    def pair_copy(slot, p, view):
        return remote(view, view, pair_send.at[slot, p], pair_recv.at[slot, p], mate, f)

    def pair_start(t, way, p):
        @pl.when(may_get(t, way))
        def _():
            pair_copy(1 + 3 * way + t, p, main(got_block(t, way), p)).start()

    for p in (1, 0):
        for way in range(2):
            send(0, way, p)
    for p in (1, 0):
        keep[p].wait()
        pair_copy(0, p, main(f, p)).start()
    for t in range(NF - 1):
        for p in (1, 0):
            for way in range(2):
                get(t, way, p)
                if t < NF - 2:
                    send(t + 1, way, p)
                pair_start(t, way, p)
            if t == NF - 2 and p == 1:
                work()

    def wait_pair(theirs):
        for p in range(2):
            pair_copy(0, p, theirs(f, p)).wait_recv()
        for t in range(NF - 1):
            for way in range(2):

                @pl.when(may_get(t, way))
                def _():
                    for p in range(2):
                        pair_copy(1 + 3 * way + t, p, theirs(got_block(t, way), p)).wait_recv()

    def wait_sent():
        for p in range(2):
            pair_copy(0, p, main(f, p)).wait_send()
        for t in range(NF - 1):
            for way in range(2):

                @pl.when(may_send(t, way))
                def _():
                    for p in range(2):
                        line_copy(t, way, sent_block(t, way), p).wait_send()

                @pl.when(may_get(t, way))
                def _():
                    for p in range(2):
                        pair_copy(1 + 3 * way + t, p, main(got_block(t, way), p)).wait_send()

    return wait_pair, wait_sent


def line_sems():
    dma = pltpu.SemaphoreType.DMA
    return [dma((2, 3, 2)), dma((2, 3, 2)), dma((7, 2)), dma((7, 2)), dma((2,))]


def direct_gather(own, main, sems, work):
    send, recv, pair_send, pair_recv, local = sems
    s, f = place()
    mate = s + 1 - 2 * (s % 2)
    sent = [remote(own, main(f), send.at[n], recv.at[n], s, (f + n + 1) % NF) for n in range(3)]
    for copy in sent:
        copy.start()
    keep = pltpu.make_async_copy(own, main(f), local.at[0])
    keep.start()

    def pair_copy(n, view):
        return remote(view, view, pair_send.at[n], pair_recv.at[n], mate, f)

    blocks = [(f + NF - n - 1) % NF for n in range(3)] + [f]
    keep.wait()
    pair_copy(3, main(f)).start()
    work()
    for n in (0, 2, 1):
        remote(own, main(blocks[n]), send.at[n], recv.at[n], s, blocks[n]).wait_recv()
        pair_copy(n, main(blocks[n])).start()

    def wait_pair(theirs):
        for n in range(4):
            pair_copy(n, theirs(blocks[n])).wait_recv()

    def wait_sent():
        for copy in sent:
            copy.wait_send()
        for n in range(4):
            pair_copy(n, main(blocks[n])).wait_send()

    return wait_pair, wait_sent


def direct_sems():
    dma = pltpu.SemaphoreType.DMA
    return [dma((3,)), dma((3,)), dma((4,)), dma((4,)), dma((1,))]


def offset_of(slot, core):
    n = jnp.where(slot < 3, slot, jnp.where(slot < 7, slot + 2, jnp.where(slot < 9, slot - 4, slot)))
    return jnp.where(core == 0, HALF - 1 + n, (n + 9) % HALF)


def offsets(core):
    order = [0, 1, 2, 5, 6, 7, 8, 3, 4, 9, 10, 11, 12, 13]
    return [HALF - 1 + n if core == 0 else (n + 9) % HALF for n in order]


EARLY, LATE = ((0, 3), (7, 9)), ((3, 7), (9, 14))


class Spread:
    def __init__(self, w1, wx, send, recv):
        self.w1, self.wx, self.send, self.recv = w1, wx, send, recv
        self.s, self.f = place()
        s = self.s
        self.x, self.y, self.zh, self.core = s // 16, (s // 4) % 4, (s // 2) % 2, s % 2

    def copy(self, stage, n, src, dst, x, y, core, f):
        to = ((x * 4 + y) * 2 + self.zh) * 2 + core
        return remote(src, dst, self.send.at[stage, n], self.recv.at[stage, n], to, f)

    def fetch(self):
        part = pl.ds(pl.multiple_of(16 * (4 * self.x + self.y), 16), 16)
        src = self.w1.at[pl.ds((HALF - 1) * self.core, HALF), part]
        dst = self.wx.at[self.core, :, self.x, self.y]
        return self.copy(0, 0, src, dst, self.x, self.y, self.core, (self.f + 2) % NF)

    def over(self, stage, c, n, got):
        x, y = self.x, self.y
        step = NF - n - 1 if got else n + 1
        along_x = (stage == 1) == (c == 0)
        px, py = ((x + step) % 4, y) if along_x else (x, (y + step) % 4)
        hx, hy = (px, py) if got else (x, y)
        if stage == 1:
            view = self.wx.at[c, :, hx, hy]
        else:
            view = self.wx.at[c, :, hx] if along_x else self.wx.at[c, :, :, hy]
        return self.copy(stage, n, view, view, px, py, c, self.f)

    def each(self, stage, what):
        for c in range(2):

            @pl.when(self.core == c)
            def _():
                for n in range(3):
                    if what == "start":
                        self.over(stage, c, n, False).start()
                    elif what == "get":
                        self.over(stage, c, n, True).wait_recv()
                    else:
                        self.over(stage, c, n, False).wait_send()

    def swap(self, c):
        view = self.wx.at[c]
        return self.copy(3, 0, view, view, self.x, self.y, 1 - self.core, self.f)


class Reduction:
    def __init__(self, rows, d, r1x, r1y, ex, ey, r2x, r2y, total, t_send, r3, done, send, recv):
        self.rows, self.d, self.r1x, self.r1y, self.ex, self.ey = rows, d, r1x, r1y, ex, ey
        self.r2x, self.r2y, self.total, self.t_send, self.r3 = r2x, r2y, total, t_send, r3
        self.done, self.send, self.recv = done, send, recv
        self.s, self.f = place()
        s = self.s
        self.x, self.y, self.zh, self.core = s // 16, (s // 4) % 4, (s // 2) % 2, s % 2
        self.xs = [(self.x + n) % 4 for n in (1, 2, 3)]
        self.ys = [(self.y + n) % 4 for n in (1, 2, 3)]
        self.ends = [(1 - self.zh, self.core), (self.zh, 1 - self.core), (1 - self.zh, 1 - self.core)]
        self.first = []

    def copy(self, src, dst, stage, way, n, x, y, zh, core):
        to = ((x * 4 + y) * 2 + zh) * 2 + core
        return remote(src, dst, self.send.at[stage, way, n], self.recv.at[stage, way, n], to, self.f)

    def start_first(self, group):
        half = HALF // 2
        stage = 0 if group is EARLY else 3
        (x0, x1), (y0, y1) = group
        made = []
        for n in range(3):
            a, b = self.xs[n], self.ys[n]
            src, dst = self.d.at[pl.ds(x0, x1 - x0), a], self.r1x.at[n, pl.ds(x0, x1 - x0)]
            made.append(self.copy(src, dst, stage, 0, n, a, self.y, self.zh, self.core))
            src, dst = self.d.at[pl.ds(y0, y1 - y0), :, b], self.r1y.at[n, pl.ds(y0 - half, y1 - y0)]
            made.append(self.copy(src, dst, stage, 1, n, self.x, b, self.zh, self.core))
        for c in made:
            c.start()
        self.first += made

    def start_second(self):
        half = HALF // 2
        d, x, y = self.d, self.x, self.y

        def over_x(i, carry):
            acc = d[i, x].astype(F32)
            for n in range(3):
                acc += self.r1x[n, i].astype(F32)
            self.ex[i] = acc.astype(BF16)
            return carry

        def over_y(i, carry):
            acc = d[half + i, :, y].astype(F32)
            for n in range(3):
                acc += self.r1y[n, i].astype(F32)
            self.ey[i] = acc.astype(BF16)
            return carry

        self.second = [[], []]
        for way, body in enumerate((over_x, over_y)):
            for c in self.first[way::2]:
                c.wait_recv()
            lax.fori_loop(0, half, body, 0)
            for n in range(3):
                a, b = self.xs[n], self.ys[n]
                if way == 0:
                    c = self.copy(self.ex.at[:, b], self.r2x.at[n], 1, 0, n, x, b, self.zh, self.core)
                else:
                    c = self.copy(self.ey.at[:, a], self.r2y.at[n], 1, 1, n, a, y, self.zh, self.core)
                c.start()
                self.second[way].append(c)

    def start_third(self):
        half = HALF // 2
        x, y = self.x, self.y

        def over_y(i, carry):
            acc = self.ex[i, y].astype(F32)
            for n in range(3):
                acc += self.r2x[n, i].astype(F32)
            self.total[i] = acc
            return carry

        def over_x(i, carry):
            acc = self.ey[i, x].astype(F32)
            for n in range(3):
                acc += self.r2y[n, i].astype(F32)
            self.total[half + i] = acc
            return carry

        for way, body in enumerate((over_y, over_x)):
            for c in self.second[way]:
                c.wait_recv()
            lax.fori_loop(0, half, body, 0)
        for a in range(2):
            for b in range(2):
                start = 16 * a + 8 * b if self.rows == 32 else 8 * a
                piece = self.total[:, start : start + 8]
                self.t_send[2 * a + b] = piece.reshape(half, 16, 128).astype(BF16)
        self.third = []
        for n, (a, b) in enumerate(self.ends if self.rows == 32 else self.ends[:1]):
            self.third.append(self.copy(self.t_send.at[2 * a + b], self.r3.at[n], 2, 0, n, x, y, a, b))
        for c in self.third:
            c.start()

    def join(self):
        self.third[0].wait_recv()
        rows = pl.ds(pl.multiple_of(8 * self.zh, 8), 8)
        self.done[0] = self.total[:, rows] + self.r3[0].astype(F32).reshape(HALF, 8, 128)
        self.give = self.copy(self.done.at[0], self.done.at[1], 2, 1, 0, self.x, self.y, self.zh, 1 - self.core)
        self.give.start()

    def finish(self):
        if self.rows == 32:
            for c in self.third:
                c.wait_recv()
            rows = pl.ds(pl.multiple_of(16 * self.zh + 8 * self.core, 8), 8)
            got = [self.r3[n].astype(F32).reshape(HALF, 8, 128) for n in range(3)]
            mine, other = self.total[:, rows] + got[0], got[1] + got[2]
        else:
            self.give.wait()
            mine, other = self.done[0], self.done[1]
        low = jnp.where(self.core == 1, mine, other)
        high = jnp.where(self.core == 1, other, mine)
        for c in self.first + self.second[0] + self.second[1] + self.third:
            c.wait_send()
        return [(k, low, i) for i, k in enumerate(offsets(1))] + [(k, high, i) for i, k in enumerate(offsets(0)) if k >= HALF]


def reduction_scratch(rows):
    half = HALF // 2
    dma = pltpu.SemaphoreType.DMA
    return [
        pltpu.VMEM((HALF, 4, 4, rows, 128), BF16),
        pltpu.VMEM((3, half, 4, rows, 128), BF16),
        pltpu.VMEM((3, half, 4, rows, 128), BF16),
        pltpu.VMEM((half, 4, rows, 128), BF16),
        pltpu.VMEM((half, 4, rows, 128), BF16),
        pltpu.VMEM((3, half, rows, 128), BF16),
        pltpu.VMEM((3, half, rows, 128), BF16),
        pltpu.VMEM((HALF, rows, 128), F32),
        pltpu.VMEM((4, half, 16, 128), BF16),
        pltpu.VMEM((3, half, 16, 128), BF16),
        pltpu.VMEM((2, HALF, 8, 128), F32),
        dma((4, 2, 3)),
        dma((4, 2, 3)),
    ]


def swish_slope(pre):
    logistic = jax.nn.sigmoid(pre)
    return logistic * (1.0 + pre * (1.0 - logistic))


def dot_nn(a, b):
    return lax.dot_general(a, b, (((1,), (0,)), ((), ())), preferred_element_type=F32)


def dot_nt(a, b):
    return lax.dot_general(a, b, (((1,), (1,)), ((), ())), preferred_element_type=F32)


def dot_tn(a, b):
    return lax.dot_general(a, b, (((0,), (0,)), ((), ())), preferred_element_type=F32)


def rows_from(start):
    return pl.ds(pl.multiple_of(start, 32), 256)


def whole_kernel(
    v_ref, w1_hbm, w2_hbm, cot_ref, gin_ref, gw1_ref, gw2_ref,
    w1, w2, wsem, vg, t1, a1, pre1, hown, hg, t2, h3, part1, part2, part_s, part_r,
    gs, t3, g3, gsem_s, gsem_r, hp, ps, rp, psem_s, psem_r, gf, gfsem_s, gfsem_r, g4, s5, r5, s5_s, s5_r, at, split, vown, ht, gc2, gc1, wx, wx_s, wx_r, gx, gx_s, gx_r, k5,
    *rest,
):
    nsem = 5
    vsems, hsems = rest[:nsem], rest[nsem : 2 * nsem]
    red2 = Reduction(32, *rest[2 * nsem : 2 * nsem + 13])
    red1 = Reduction(16, *rest[2 * nsem + 13 :])
    s, f = place()
    core, zh = s % 2, (s // 2) % 2
    mate = s + 1 - 2 * core
    outside = s - 1 + 2 * core
    has_outside = jnp.logical_and(outside >= 0, outside < NS)
    peers = [(f + n) % NF for n in (1, 2, 3)]

    load1 = pltpu.make_async_copy(w1_hbm, w1, wsem.at[0])
    load2 = pltpu.make_async_copy(w2_hbm, w2, wsem.at[1])
    load1.start()
    load2.start()

    def dev(x_, y_, zh_, core_):
        return ((x_ * 4 + y_) * 2 + zh_) * 2 + core_

    for c in range(2):
        split[c] = v_ref[:, :, :, :, 128 * c : 128 * c + 128].astype(F32)
        for plane in range(2):
            for parity in range(2):
                for half in range(2):
                    part = split[c, plane, :, parity, pl.ds(half, 8, stride=2), :]
                    lane = 256 * half + 128 * c
                    vown[plane, parity, :, lane : lane + 128] = part.reshape(64, 128).astype(BF16)

    partners = [(True, s, p) for p in peers]
    partners += [(True, mate, f), (has_outside, outside, f)]
    partners += [(True, dev(a, red2.y, zh, core), f) for a in red2.xs]
    partners += [(True, dev(red2.x, b, zh, core), f) for b in red2.ys]
    partners += [(True, dev(red2.x, red2.y, 1 - zh, b), f) for b in (core, 1 - core)]
    greet(partners)
    spread = Spread(w1, wx, wx_s, wx_r)

    def part_copy(slot, buf):
        return remote(buf.at[0], buf.at[1], part_s.at[slot], part_r.at[slot], outside, f)

    def vol(c, j, p):
        return vg.at[2 * c + p, :, j]

    t1[:, 0:8, :] = jnp.zeros((8, 8, 512), F32)

    def cells(i, carry):
        plane, parity = i // 2, i % 2
        for j in range(NF):
            t1[:, 8 + 8 * j : 16 + 8 * j, :] = vg[plane, parity, j].astype(F32).reshape(8, 8, 512)
        edge = jnp.zeros((32, 256), BF16)
        for kx in range(3):
            a1[kx, plane, parity, 0:32] = edge
        a1[0, plane, parity, 32:288] = t1[:, 7:39, 256:512].reshape(256, 256).astype(BF16)
        a1[1, plane, parity, 32:288] = t1[:, 8:40, 0:256].reshape(256, 256).astype(BF16)
        a1[2, plane, parity, 32:288] = t1[:, 8:40, 256:512].reshape(256, 256).astype(BF16)
        return carry

    def taps_first(plane, kz):
        def body(ky, acc):
            parity, start = (ky + 1) % 2, jnp.minimum(ky, 1)
            for kx in range(3):
                acc += dot_nn(a1[kx, plane, parity, rows_from(32 * start)], w1[9 * kz + 3 * ky + kx])
            return acc

        return lax.fori_loop(0, 3, body, jnp.zeros((256, 128), F32))

    sends_part = jnp.logical_and(core == 1, has_outside)
    gets_part = jnp.logical_and(core == 0, has_outside)
    part1_copy = part_copy(0, part1)

    def top_plane():
        load1.wait()
        lax.fori_loop(4 * core + 2, 4 * core + 4, cells, 0)

        @pl.when(sends_part)
        def _():
            part1[0] = taps_first(3, 0).astype(BF16)
            part1_copy.start()

    vol_wait, vol_sent = line_gather(vown, lambda j, p: vol(core, j, p), vsems, top_plane)
    spread.fetch().start()
    lax.fori_loop(4 * core, 4 * core + 2, cells, 0)
    pre1[...] = taps_first(2 * core, 1) + taps_first(2 * core + 1, 2)
    vol_wait(lambda j, p: vol(1 - core, j, p))

    @pl.when(core == 1)
    def _():
        lax.fori_loop(2, 4, cells, 0)
        pre1[...] += taps_first(1, 0)

    @pl.when(gets_part)
    def _():
        part1_copy.wait_recv()
        pre1[...] += part1[1].astype(F32)

    pre_first = pre1[...]
    hown[...] = (pre_first * jax.nn.sigmoid(pre_first)).astype(BF16)

    def hid(plane, j):
        return hg.at[plane, :, pl.ds(pl.multiple_of(128 * j, 128), 128)]

    def turn(i, carry):
        k = offset_of(i, core)
        kz, ky, kx = k // 9, (k // 3) % 3, k % 3
        parity, start = (ky + 1) % 2, jnp.minimum(ky, 1)
        plane = jnp.where(kz == 1, 0, 1)
        at[i, :, 0:256] = a1[kx, plane, parity, rows_from(32 * start)].T
        at[i, :, 256:512] = a1[kx, plane + 2, parity, rows_from(32 * start)].T
        return carry

    def windows():
        spread.fetch().wait_recv()
        spread.each(1, "start")
        lax.fori_loop(4 - 4 * core, 8 - 6 * core, cells, 0)
        lax.fori_loop(0, HALF, turn, 0)

    hid_wait, hid_sent = direct_gather(hown, lambda j: hid(core, j), hsems, windows)

    t2[:, 0:8, :] = jnp.zeros((8, 8, 512), F32)
    t2[:, 40:48, :] = jnp.zeros((8, 8, 512), F32)

    def spread_hidden(i):
        t2[:, 8:40, :] = hg[i].astype(F32).reshape(8, 32, 512)
        edge = jnp.zeros((32, 512), BF16)
        for kx in range(3):
            h3[kx, i, 0:32] = edge
            h3[kx, i, 288:320] = edge
        h3[0, i, 32:288] = t2[:, 7:39, :].reshape(256, 512).astype(BF16)
        h3[1, i, 32:288] = hg[i]
        h3[2, i, 32:288] = t2[:, 9:41, :].reshape(256, 512).astype(BF16)

    def taps_second(plane, kz):
        def body(ky, acc):
            for kx in range(3):
                acc += dot_nn(h3[kx, plane, rows_from(32 * ky)], w2[9 * kz + 3 * ky + kx])
            return acc

        return lax.fori_loop(0, 3, body, jnp.zeros((256, 128), F32))

    load2.wait()
    spread_hidden(core)
    part2_copy = part_copy(1, part2)

    @pl.when(has_outside)
    def _():
        part2[0] = taps_second(core, 2 - 2 * core).astype(BF16)
        part2_copy.start()

    pre_second = taps_second(core, 1)
    hid_wait(lambda j: hid(1 - core, j))
    spread_hidden(1 - core)
    pre_second += taps_second(1 - core, 2 - 2 * core)

    def turn_hidden(i, carry):
        ky, kx = i // 3, i % 3
        ht[i, :, 0:256] = h3[kx, core, rows_from(32 * ky)].T
        ht[i, :, 256:512] = h3[kx, 1 - core, rows_from(32 * ky)].T
        return carry

    lax.fori_loop(4 - 4 * core, 9 - 4 * core, turn_hidden, 0)

    @pl.when(jnp.logical_not(has_outside))
    def _():
        part2[1] = jnp.zeros((256, 128), BF16)

    @pl.when(has_outside)
    def _():
        part2_copy.wait_recv()

    pre_second += part2[1].astype(F32)
    gs[1] = (cot_ref[...].astype(F32) * swish_slope(pre_second)).astype(BF16)

    spread.each(1, "get")
    spread.each(2, "start")

    def swap(place_there, to, slot):
        return remote(gs.at[1], gs.at[place_there], gsem_s.at[slot], gsem_r.at[slot], to, f)

    to_mate = swap(2 * core, mate, 0)
    to_out = swap(2 - 2 * core, outside, 1)
    from_mate = swap(2 - 2 * core, mate, 0)
    from_out = swap(2 * core, outside, 1)
    to_mate.start()

    @pl.when(has_outside)
    def _():
        to_out.start()

    @pl.when(jnp.logical_not(has_outside))
    def _():
        gs[2 * core] = jnp.zeros((256, 128), BF16)

    t3[:, 0:8, :] = jnp.zeros((8, 8, 128), F32)
    t3[:, 40:48, :] = jnp.zeros((8, 8, 128), F32)

    def spread_grads(i):
        t3[:, 8:40, :] = gs[i].astype(F32).reshape(8, 32, 128)
        edge = jnp.zeros((32, 128), BF16)
        for kx in range(3):
            g3[kx, i, 0:32] = edge
            g3[kx, i, 288:320] = edge
        g3[0, i, 32:288] = t3[:, 9:41, :].reshape(256, 128).astype(BF16)
        g3[1, i, 32:288] = gs[i]
        g3[2, i, 32:288] = t3[:, 7:39, :].reshape(256, 128).astype(BF16)

    def back_second(plane, kz, first):
        def body(ky, carry):
            acc = hp[...]
            for kx in range(3):
                acc += dot_nt(g3[kx, plane, rows_from(32 * (2 - ky))], w2[9 * kz + 3 * ky + kx])
            hp[...] = acc
            return carry

        if first:
            hp[...] = jnp.zeros((256, 512), F32)
        lax.fori_loop(0, 3, body, 0)

    spread_grads(1)
    back_second(1, 1, True)
    from_mate.wait_recv()
    spread_grads(2 - 2 * core)
    back_second(2 - 2 * core, 2 * core, False)

    gc2[1, 0:256] = gs[1]
    gc2[1, 256:512] = gs[2 - 2 * core]

    def terms_second(i, carry):
        k = offset_of(i, core)
        pairs = jnp.where(k // 9 == 1, 1, 0)
        red2.d[i] = dot_nn(ht[k % 9], gc2[pairs]).reshape(4, 4, 32, 128).astype(BF16)
        return carry

    for first, last in EARLY:
        lax.fori_loop(first, last, terms_second, 0)
    red2.start_first(EARLY)
    lax.fori_loop(5 * core, 4 + 5 * core, turn_hidden, 0)

    @pl.when(has_outside)
    def _():
        from_out.wait_recv()

    spread_grads(2 * core)
    back_second(2 * core, 2 - 2 * core, False)

    for j in range(NF):
        ps[j] = hp[:, 128 * j : 128 * j + 128].astype(BF16)
    shares = [remote(ps.at[p], rp.at[n], psem_s.at[n], psem_r.at[n], s, p) for n, p in enumerate(peers)]
    for c in shares:
        c.start()

    gc2[0, 0:256] = gs[2 * core]
    gc2[0, 256:512] = gs[1]
    for first, last in LATE:
        lax.fori_loop(first, last, terms_second, 0)
    red2.start_first(LATE)
    spread.each(2, "get")
    spread.swap(core).start()

    for c in shares:
        c.wait_recv()
    hidden_grad = ps[f].astype(F32)
    for n in range(3):
        hidden_grad += rp[n].astype(F32)
    gf[0] = (hidden_grad * swish_slope(pre1[...])).astype(BF16)

    gf_mate = remote(gf.at[0], gf.at[1], gfsem_s.at[0], gfsem_r.at[0], mate, f)
    gf_out = remote(gf.at[0], gf.at[2], gfsem_s.at[1], gfsem_r.at[1], outside, f)
    sends = jnp.logical_and(core == 0, has_outside)
    gets = jnp.logical_and(core == 1, has_outside)

    @pl.when(sends)
    def _():
        gf_out.start()

    gf_mate.start()

    far, near = (f + 2) % NF, f + 1 - 2 * (f % 2)
    gx_own = remote(gf.at[0], gx.at[0], gx_s.at[0], gx_r.at[0], s, far)
    gx_out = remote(gf.at[2], gx.at[1], gx_s.at[1], gx_r.at[1], s, far)
    gx_give = remote(gx.at[0], gx.at[1], gx_s.at[2], gx_r.at[2], mate, f)
    t3[:, 40:48, :] = jnp.zeros((8, 8, 128), F32)

    def spread_first(q, z, src):
        t3[:, 8:40, :] = src.astype(F32).reshape(8, 32, 128)
        for i in range(2):
            half = jnp.where(f < 2, t3[:, 8 + i : 24 + i, :], t3[:, 24 + i : 40 + i, :])
            g4[q, i, z, 0:128] = half.reshape(128, 128).astype(BF16)
            g4[q, i, z, 128:144] = jnp.zeros((16, 128), BF16)

    def taps(parity):
        return [(1, 0)] if parity == 0 else [(2, 0), (0, 1)]

    def back_first(zp):
        for yp in range(2):
            for xp in range(2):
                acc = jnp.zeros((128, 256), F32)
                for kz, oz in taps(zp):
                    for ky, oy in taps(yp):
                        for kx, ox in taps(xp):
                            k = 9 * kz + 3 * ky + kx
                            there = wx[k // HALF, k - (HALF - 1) * (k // HALF)].reshape(256, 128)
                            acc += dot_nt(g4[0, ox, oz, 16 * oy : 16 * oy + 128], w1[k])
                            acc += dot_nt(g4[1, ox, oz, 16 * oy : 16 * oy + 128], there)
                acc = acc.reshape(8, 16, 256)
                lower, upper = acc[:, 0:8, :].reshape(64, 256), acc[:, 8:16, :].reshape(64, 256)
                lanes = slice(256 * xp, 256 * xp + 256)
                k5[zp, yp, :, lanes] = jnp.where(f % 2 == 0, lower, upper)
                s5[zp, yp, :, lanes] = jnp.where(f % 2 == 0, upper, lower).astype(BF16)

    def share(zp):
        return remote(s5.at[zp], r5.at[zp], s5_s.at[zp], s5_r.at[zp], s, near)

    gf_mate.wait_recv()

    gc1[1, 0:256] = gf[core]
    gc1[1, 256:512] = gf[1 - core]

    def terms_first(i, carry):
        pairs = jnp.where(offset_of(i, core) // 9 == 1, 1, 0)
        red1.d[i] = dot_nn(at[i], gc1[pairs]).reshape(4, 4, 16, 128).astype(BF16)
        return carry

    for first, last in EARLY:
        lax.fori_loop(first, last, terms_first, 0)
    red1.start_first(EARLY)
    gx_own.start()
    red2.start_second()

    @pl.when(gets)
    def _():
        gf_out.wait_recv()

    @pl.when(jnp.logical_and(core == 1, jnp.logical_not(has_outside)))
    def _():
        gf[2] = jnp.zeros((256, 128), BF16)

    gc1[0, 0:256] = gf[0]
    gc1[0, 256:512] = gf[1 + core]
    for first, last in LATE:
        lax.fori_loop(first, last, terms_first, 0)
    red1.start_first(LATE)

    @pl.when(core == 1)
    def _():
        gx_out.start()

    spread.swap(1 - core).wait_recv()
    spread_first(0, 0, gf[0])
    gx_own.wait_recv()

    @pl.when(core == 1)
    def _():
        gx_give.start()

    spread_first(1, 0, gx[0])
    back_first(0)
    even, odd = share(0), share(1)
    even.start()
    red2.start_third()
    spread_first(0, 1, gf[1 + core])

    @pl.when(core == 1)
    def _():
        gx_out.wait_recv()

    @pl.when(core == 0)
    def _():
        gx_give.wait_recv()

    spread_first(1, 1, gx[1])
    back_first(1)
    odd.start()
    red1.start_second()
    red1.start_third()
    for k, values, i in red2.finish():
        gw2_ref[k] = values[i]
    red1.join()

    for zp, copy in enumerate((even, odd)):
        copy.wait_recv()
        for yp in range(2):
            total = (k5[zp, yp] + r5[zp, yp].astype(F32)).reshape(8, 8, 512)
            for xp in range(2):
                for c in range(2):
                    lane = 256 * xp + 128 * c
                    split[c, zp, :, yp, pl.ds(xp, 8, stride=2), :] = total[:, :, lane : lane + 128]
        for c in range(2):
            gin_ref[zp, :, :, :, 128 * c : 128 * c + 128] = split[c, zp].astype(BF16)
    for k, values, i in red1.finish():
        gw1_ref[k] = jnp.where(core == 0, values[i, 0:4], values[i, 4:8])
    for c in shares + [even, odd, gx_own, spread.fetch(), spread.swap(core)]:
        c.wait_send()
    for stage in (1, 2):
        spread.each(stage, "sent")

    @pl.when(core == 1)
    def _():
        gx_out.wait_send()
        gx_give.wait_send()

    vol_sent()
    hid_sent()
    to_mate.wait_send()
    gf_mate.wait_send()

    @pl.when(sends_part)
    def _():
        part1_copy.wait_send()

    @pl.when(has_outside)
    def _():
        part2_copy.wait_send()

    @pl.when(has_outside)
    def _():
        to_out.wait_send()

    @pl.when(sends)
    def _():
        gf_out.wait_send()


def run_whole(cells, weight_first, weight_second, cotangent):
    dma = pltpu.SemaphoreType.DMA
    vmem, anywhere = pl.BlockSpec(memory_space=pltpu.VMEM), pl.BlockSpec(memory_space=pl.ANY)
    scratch = [
        pltpu.VMEM((27, 256, 128), BF16),
        pltpu.VMEM((27, 512, 128), BF16),
        dma((2,)),
        pltpu.VMEM((4, 2, NF, 64, 512), BF16),
        pltpu.VMEM((8, 40, 512), F32),
        pltpu.VMEM((3, 4, 2, 288, 256), BF16),
        pltpu.VMEM((256, 128), F32),
        pltpu.VMEM((256, 128), BF16),
        pltpu.VMEM((2, 256, 512), BF16),
        pltpu.VMEM((8, 48, 512), F32),
        pltpu.VMEM((3, 2, 320, 512), BF16),
        pltpu.VMEM((2, 256, 128), BF16),
        pltpu.VMEM((2, 256, 128), BF16),
        dma((2,)),
        dma((2,)),
        pltpu.VMEM((3, 256, 128), BF16),
        pltpu.VMEM((8, 48, 128), F32),
        pltpu.VMEM((3, 3, 320, 128), BF16),
        dma((2,)),
        dma((2,)),
        pltpu.VMEM((256, 512), F32),
        pltpu.VMEM((NF, 256, 128), BF16),
        pltpu.VMEM((3, 256, 128), BF16),
        dma((3,)),
        dma((3,)),
        pltpu.VMEM((3, 256, 128), BF16),
        dma((2,)),
        dma((2,)),
        pltpu.VMEM((2, 2, 2, 144, 128), BF16),
        pltpu.VMEM((2, 2, 64, 512), BF16),
        pltpu.VMEM((2, 2, 64, 512), BF16),
        dma((2,)),
        dma((2,)),
        pltpu.VMEM((HALF, 256, 512), BF16),
        pltpu.VMEM((2, 2, 8, 2, 16, 128), F32),
        pltpu.VMEM((2, 2, 64, 512), BF16),
        pltpu.VMEM((9, 512, 512), BF16),
        pltpu.VMEM((2, 512, 128), BF16),
        pltpu.VMEM((2, 512, 128), BF16),
        pltpu.VMEM((2, HALF, 4, 4, 16, 128), BF16),
        dma((4, 3)),
        dma((4, 3)),
        pltpu.VMEM((2, 256, 128), BF16),
        dma((3,)),
        dma((3,)),
        pltpu.VMEM((2, 2, 64, 512), F32),
    ]
    scratch += line_sems() + direct_sems() + reduction_scratch(32) + reduction_scratch(16)
    return pl.pallas_call(
        whole_kernel,
        out_shape=(
            jax.ShapeDtypeStruct((2, 8, 2, 16, 256), BF16),
            jax.ShapeDtypeStruct((27, 4, 128), F32),
            jax.ShapeDtypeStruct((27, 8, 128), F32),
        ),
        in_specs=[vmem, anywhere, anywhere, vmem],
        out_specs=(vmem, vmem, vmem),
        scratch_shapes=scratch,
        compiler_params=pltpu.CompilerParams(collective_id=0, has_side_effects=True, vmem_limit_bytes=52 * 2**20),
        name="bottleneck",
    )(cells, weight_first, weight_second, cotangent)


def per_device(volume, weight_first, weight_second, cotangent):
    grad, grad_first, grad_second = run_whole(volume.reshape(2, 8, 2, 16, 256), weight_first, weight_second, cotangent.reshape(256, 128))
    return (grad.reshape(2, 16, 16, 256), grad_first, grad_second)


def solution(mesh):
    placed = (
        P("space", None, "filt", None),
        P(None, None, "filt"),
        P(None, None, "filt"),
        P("space", None, None, "filt"),
    )
    return jax.shard_map(
        per_device,
        mesh=mesh,
        in_specs=placed,
        out_specs=(
            P("space", None, "filt", None),
            P(None, "space", "filt"),
            P(None, "space", "filt"),
        ),
        check_vma=False,
    )
```

```python
import functools

import jax
import jax.numpy as jnp
from jax import lax
from jax.experimental import pallas as pl
from jax.experimental.pallas import tpu as pltpu
from jax.sharding import PartitionSpec as P

BF16 = jnp.bfloat16
F32 = jnp.float32
MESH = pl.DeviceIdType.MESH
NS = 64
NF = 4
HALF = 14


def place():
    s = lax.axis_index("space")
    f = lax.axis_index("filt")
    return s, f


def remote(src, dst, send, recv, s, f):
    return pltpu.make_async_remote_copy(
        src_ref=src,
        dst_ref=dst,
        send_sem=send,
        recv_sem=recv,
        device_id={"space": s, "filt": f},
        device_id_type=MESH,
    )


def greet(partners):
    barrier = pltpu.get_barrier_semaphore()
    total = 0
    for cond, s, f in partners:
        if cond is True:
            pl.semaphore_signal(barrier, inc=1, device_id={"space": s, "filt": f}, device_id_type=MESH)
            total = total + 1
        else:

            @pl.when(cond)
            def _():
                pl.semaphore_signal(barrier, inc=1, device_id={"space": s, "filt": f}, device_id_type=MESH)

            total = total + cond.astype(jnp.int32)
    pl.semaphore_wait(barrier, total)


def line_gather(own, main, sems, work):
    line_send, line_recv, pair_send, pair_recv, local = sems
    s, f = place()
    mate = s + 1 - 2 * (s % 2)

    keep = [pltpu.make_async_copy(own.at[p], main(f, p), local.at[p]) for p in range(2)]
    for copy in keep:
        copy.start()

    def line_copy(t, way, block, p):
        to = f + 1 if way == 0 else f - 1
        view = main(block, p)
        return remote(own.at[p] if t == 0 else view, view, line_send.at[way, t, p], line_recv.at[way, t, p], s, to)

    def sent_block(t, way):
        return f - t if way == 0 else f + t

    def got_block(t, way):
        return f - 1 - t if way == 0 else f + 1 + t

    def may_send(t, way):
        if way == 0:
            return jnp.logical_and(f < NF - 1, f >= t)
        return jnp.logical_and(f > 0, f + t < NF)

    def may_get(t, way):
        return f > t if way == 0 else f + t < NF - 1

    def send(t, way, p):
        @pl.when(may_send(t, way))
        def _():
            line_copy(t, way, sent_block(t, way), p).start()

    def get(t, way, p):
        @pl.when(may_get(t, way))
        def _():
            line_copy(t, way, got_block(t, way), p).wait_recv()

    def pair_copy(slot, p, view):
        return remote(view, view, pair_send.at[slot, p], pair_recv.at[slot, p], mate, f)

    def pair_start(t, way, p):
        @pl.when(may_get(t, way))
        def _():
            pair_copy(1 + 3 * way + t, p, main(got_block(t, way), p)).start()

    for p in (1, 0):
        for way in range(2):
            send(0, way, p)
    for p in (1, 0):
        keep[p].wait()
        pair_copy(0, p, main(f, p)).start()
    for t in range(NF - 1):
        for p in (1, 0):
            for way in range(2):
                get(t, way, p)
                if t < NF - 2:
                    send(t + 1, way, p)
                pair_start(t, way, p)
            if t == NF - 2 and p == 1:
                work()

    def wait_pair(theirs):
        for p in range(2):
            pair_copy(0, p, theirs(f, p)).wait_recv()
        for t in range(NF - 1):
            for way in range(2):

                @pl.when(may_get(t, way))
                def _():
                    for p in range(2):
                        pair_copy(1 + 3 * way + t, p, theirs(got_block(t, way), p)).wait_recv()

    def wait_sent():
        for p in range(2):
            pair_copy(0, p, main(f, p)).wait_send()
        for t in range(NF - 1):
            for way in range(2):

                @pl.when(may_send(t, way))
                def _():
                    for p in range(2):
                        line_copy(t, way, sent_block(t, way), p).wait_send()

                @pl.when(may_get(t, way))
                def _():
                    for p in range(2):
                        pair_copy(1 + 3 * way + t, p, main(got_block(t, way), p)).wait_send()

    return wait_pair, wait_sent


def line_sems():
    dma = pltpu.SemaphoreType.DMA
    return [dma((2, 3, 2)), dma((2, 3, 2)), dma((7, 2)), dma((7, 2)), dma((2,))]


def direct_gather(own, main, sems, work):
    send, recv, pair_send, pair_recv, local = sems
    s, f = place()
    mate = s + 1 - 2 * (s % 2)
    sent = [remote(own, main(f), send.at[n], recv.at[n], s, (f + n + 1) % NF) for n in range(3)]
    for copy in sent:
        copy.start()
    keep = pltpu.make_async_copy(own, main(f), local.at[0])
    keep.start()

    def pair_copy(n, view):
        return remote(view, view, pair_send.at[n], pair_recv.at[n], mate, f)

    blocks = [(f + NF - n - 1) % NF for n in range(3)] + [f]
    keep.wait()
    pair_copy(3, main(f)).start()
    work()
    for n in (0, 2, 1):
        remote(own, main(blocks[n]), send.at[n], recv.at[n], s, blocks[n]).wait_recv()
        pair_copy(n, main(blocks[n])).start()

    def wait_pair(theirs):
        for n in range(4):
            pair_copy(n, theirs(blocks[n])).wait_recv()

    def wait_sent():
        for copy in sent:
            copy.wait_send()
        for n in range(4):
            pair_copy(n, main(blocks[n])).wait_send()

    return wait_pair, wait_sent


def direct_sems():
    dma = pltpu.SemaphoreType.DMA
    return [dma((3,)), dma((3,)), dma((4,)), dma((4,)), dma((1,))]


def offset_of(slot, core):
    n = jnp.where(slot < 3, slot, jnp.where(slot < 7, slot + 2, jnp.where(slot < 9, slot - 4, slot)))
    return jnp.where(core == 0, HALF - 1 + n, (n + 9) % HALF)


def offsets(core):
    order = [0, 1, 2, 5, 6, 7, 8, 3, 4, 9, 10, 11, 12, 13]
    return [HALF - 1 + n if core == 0 else (n + 9) % HALF for n in order]


EARLY, LATE = ((0, 3), (7, 9)), ((3, 7), (9, 14))


class Spread:
    def __init__(self, w1, wx, send, recv):
        self.w1, self.wx, self.send, self.recv = w1, wx, send, recv
        self.s, self.f = place()
        s = self.s
        self.x, self.y, self.zh, self.core = s // 16, (s // 4) % 4, (s // 2) % 2, s % 2

    def copy(self, stage, n, src, dst, x, y, core, f):
        to = ((x * 4 + y) * 2 + self.zh) * 2 + core
        return remote(src, dst, self.send.at[stage, n], self.recv.at[stage, n], to, f)

    def fetch(self):
        part = pl.ds(pl.multiple_of(16 * (4 * self.x + self.y), 16), 16)
        src = self.w1.at[pl.ds((HALF - 1) * self.core, HALF), part]
        dst = self.wx.at[self.core, :, self.x, self.y]
        return self.copy(0, 0, src, dst, self.x, self.y, self.core, (self.f + 2) % NF)

    def over(self, stage, c, n, got):
        x, y = self.x, self.y
        step = NF - n - 1 if got else n + 1
        along_x = (stage == 1) == (c == 0)
        px, py = ((x + step) % 4, y) if along_x else (x, (y + step) % 4)
        hx, hy = (px, py) if got else (x, y)
        if stage == 1:
            view = self.wx.at[c, :, hx, hy]
        else:
            view = self.wx.at[c, :, hx] if along_x else self.wx.at[c, :, :, hy]
        return self.copy(stage, n, view, view, px, py, c, self.f)

    def each(self, stage, what):
        for c in range(2):

            @pl.when(self.core == c)
            def _():
                for n in range(3):
                    if what == "start":
                        self.over(stage, c, n, False).start()
                    elif what == "get":
                        self.over(stage, c, n, True).wait_recv()
                    else:
                        self.over(stage, c, n, False).wait_send()

    def swap(self, c):
        view = self.wx.at[c]
        return self.copy(3, 0, view, view, self.x, self.y, 1 - self.core, self.f)


class Reduction:
    def __init__(self, rows, d, r1x, r1y, ex, ey, r2x, r2y, total, t_send, r3, send, recv):
        self.rows, self.d, self.r1x, self.r1y, self.ex, self.ey = rows, d, r1x, r1y, ex, ey
        self.r2x, self.r2y, self.total, self.t_send, self.r3 = r2x, r2y, total, t_send, r3
        self.send, self.recv = send, recv
        self.s, self.f = place()
        s = self.s
        self.x, self.y, self.zh, self.core = s // 16, (s // 4) % 4, (s // 2) % 2, s % 2
        self.xs = [(self.x + n) % 4 for n in (1, 2, 3)]
        self.ys = [(self.y + n) % 4 for n in (1, 2, 3)]
        self.ends = [(1 - self.zh, self.core), (self.zh, 1 - self.core), (1 - self.zh, 1 - self.core)]
        self.first = []

    def copy(self, src, dst, stage, way, n, x, y, zh, core):
        to = ((x * 4 + y) * 2 + zh) * 2 + core
        return remote(src, dst, self.send.at[stage, way, n], self.recv.at[stage, way, n], to, self.f)

    def start_first(self, group):
        half = HALF // 2
        stage = 0 if group is EARLY else 3
        (x0, x1), (y0, y1) = group
        made = []
        for n in range(3):
            a, b = self.xs[n], self.ys[n]
            src, dst = self.d.at[pl.ds(x0, x1 - x0), a], self.r1x.at[n, pl.ds(x0, x1 - x0)]
            made.append(self.copy(src, dst, stage, 0, n, a, self.y, self.zh, self.core))
            src, dst = self.d.at[pl.ds(y0, y1 - y0), :, b], self.r1y.at[n, pl.ds(y0 - half, y1 - y0)]
            made.append(self.copy(src, dst, stage, 1, n, self.x, b, self.zh, self.core))
        for c in made:
            c.start()
        self.first += made

    def start_second(self):
        half = HALF // 2
        d, x, y = self.d, self.x, self.y

        def over_x(i, carry):
            acc = d[i, x].astype(F32)
            for n in range(3):
                acc += self.r1x[n, i].astype(F32)
            self.ex[i] = acc.astype(BF16)
            return carry

        def over_y(i, carry):
            acc = d[half + i, :, y].astype(F32)
            for n in range(3):
                acc += self.r1y[n, i].astype(F32)
            self.ey[i] = acc.astype(BF16)
            return carry

        self.second = [[], []]
        for way, body in enumerate((over_x, over_y)):
            for c in self.first[way::2]:
                c.wait_recv()
            lax.fori_loop(0, half, body, 0)
            for n in range(3):
                a, b = self.xs[n], self.ys[n]
                if way == 0:
                    c = self.copy(self.ex.at[:, b], self.r2x.at[n], 1, 0, n, x, b, self.zh, self.core)
                else:
                    c = self.copy(self.ey.at[:, a], self.r2y.at[n], 1, 1, n, a, y, self.zh, self.core)
                c.start()
                self.second[way].append(c)

    def start_third(self):
        half = HALF // 2
        x, y = self.x, self.y

        def over_y(i, carry):
            acc = self.ex[i, y].astype(F32)
            for n in range(3):
                acc += self.r2x[n, i].astype(F32)
            self.total[i] = acc
            return carry

        def over_x(i, carry):
            acc = self.ey[i, x].astype(F32)
            for n in range(3):
                acc += self.r2y[n, i].astype(F32)
            self.total[half + i] = acc
            return carry

        for way, body in enumerate((over_y, over_x)):
            for c in self.second[way]:
                c.wait_recv()
            lax.fori_loop(0, half, body, 0)
        for a in range(2):
            for b in range(2):
                start = 16 * a + 8 * b if self.rows == 32 else 8 * a
                piece = self.total[:, start : start + 8]
                self.t_send[2 * a + b] = piece.reshape(half, 16, 128).astype(BF16)
        self.third = []
        for n, (a, b) in enumerate(self.ends):
            self.third.append(self.copy(self.t_send.at[2 * a + b], self.r3.at[n], 2, 0, n, x, y, a, b))
        for c in self.third:
            c.start()

    def finish(self):
        for c in self.third:
            c.wait_recv()
        start = 16 * self.zh + 8 * self.core if self.rows == 32 else 8 * self.zh
        got = [self.r3[n].astype(F32).reshape(HALF, 8, 128) for n in range(3)]
        mine = self.total[:, pl.ds(pl.multiple_of(start, 8), 8)] + got[0]
        other = got[1] + got[2]
        low = jnp.where(self.core == 1, mine, other)
        high = jnp.where(self.core == 1, other, mine)
        for c in self.first + self.second[0] + self.second[1] + self.third:
            c.wait_send()
        return [(k, low, i) for i, k in enumerate(offsets(1))] + [(k, high, i) for i, k in enumerate(offsets(0)) if k >= HALF]


def reduction_scratch(rows):
    half = HALF // 2
    dma = pltpu.SemaphoreType.DMA
    return [
        pltpu.VMEM((HALF, 4, 4, rows, 128), BF16),
        pltpu.VMEM((3, half, 4, rows, 128), BF16),
        pltpu.VMEM((3, half, 4, rows, 128), BF16),
        pltpu.VMEM((half, 4, rows, 128), BF16),
        pltpu.VMEM((half, 4, rows, 128), BF16),
        pltpu.VMEM((3, half, rows, 128), BF16),
        pltpu.VMEM((3, half, rows, 128), BF16),
        pltpu.VMEM((HALF, rows, 128), F32),
        pltpu.VMEM((4, half, 16, 128), BF16),
        pltpu.VMEM((3, half, 16, 128), BF16),
        dma((4, 2, 3)),
        dma((4, 2, 3)),
    ]


def swish_slope(pre):
    logistic = jax.nn.sigmoid(pre)
    return logistic * (1.0 + pre * (1.0 - logistic))


def dot_nn(a, b):
    return lax.dot_general(a, b, (((1,), (0,)), ((), ())), preferred_element_type=F32)


def dot_nt(a, b):
    return lax.dot_general(a, b, (((1,), (1,)), ((), ())), preferred_element_type=F32)


def dot_tn(a, b):
    return lax.dot_general(a, b, (((0,), (0,)), ((), ())), preferred_element_type=F32)


def rows_from(start):
    return pl.ds(pl.multiple_of(start, 32), 256)


def whole_kernel(
    v_ref, w1_hbm, w2_hbm, cot_ref, gin_ref, gw1_ref, gw2_ref,
    w1, w2, wsem, vg, t1, a1, pre1, hown, hg, t2, h3, part1, part2, part_s, part_r,
    gs, t3, g3, gsem_s, gsem_r, hp, ps, rp, psem_s, psem_r, gf, gfsem_s, gfsem_r, g4, s5, r5, s5_s, s5_r, at, split, vown, ht, gc2, gc1, wx, wx_s, wx_r, gx, gx_s, gx_r, k5,
    *rest,
):
    nsem = 5
    vsems, hsems = rest[:nsem], rest[nsem : 2 * nsem]
    red2 = Reduction(32, *rest[2 * nsem : 2 * nsem + 12])
    red1 = Reduction(16, *rest[2 * nsem + 12 :])
    s, f = place()
    core, zh = s % 2, (s // 2) % 2
    mate = s + 1 - 2 * core
    outside = s - 1 + 2 * core
    has_outside = jnp.logical_and(outside >= 0, outside < NS)
    peers = [(f + n) % NF for n in (1, 2, 3)]

    load1 = pltpu.make_async_copy(w1_hbm, w1, wsem.at[0])
    load2 = pltpu.make_async_copy(w2_hbm, w2, wsem.at[1])
    load1.start()
    load2.start()

    def dev(x_, y_, zh_, core_):
        return ((x_ * 4 + y_) * 2 + zh_) * 2 + core_

    for c in range(2):
        split[c] = v_ref[:, :, :, :, 128 * c : 128 * c + 128].astype(F32)
        for plane in range(2):
            for parity in range(2):
                for half in range(2):
                    part = split[c, plane, :, parity, pl.ds(half, 8, stride=2), :]
                    lane = 256 * half + 128 * c
                    vown[plane, parity, :, lane : lane + 128] = part.reshape(64, 128).astype(BF16)

    partners = [(True, s, p) for p in peers]
    partners += [(True, mate, f), (has_outside, outside, f)]
    partners += [(True, dev(a, red2.y, zh, core), f) for a in red2.xs]
    partners += [(True, dev(red2.x, b, zh, core), f) for b in red2.ys]
    partners += [(True, dev(red2.x, red2.y, 1 - zh, b), f) for b in (core, 1 - core)]
    greet(partners)
    spread = Spread(w1, wx, wx_s, wx_r)

    def part_copy(slot, buf):
        return remote(buf.at[0], buf.at[1], part_s.at[slot], part_r.at[slot], outside, f)

    def vol(c, j, p):
        return vg.at[2 * c + p, :, j]

    t1[:, 0:8, :] = jnp.zeros((8, 8, 512), F32)

    def cells(i, carry):
        plane, parity = i // 2, i % 2
        for j in range(NF):
            t1[:, 8 + 8 * j : 16 + 8 * j, :] = vg[plane, parity, j].astype(F32).reshape(8, 8, 512)
        edge = jnp.zeros((32, 256), BF16)
        for kx in range(3):
            a1[kx, plane, parity, 0:32] = edge
        a1[0, plane, parity, 32:288] = t1[:, 7:39, 256:512].reshape(256, 256).astype(BF16)
        a1[1, plane, parity, 32:288] = t1[:, 8:40, 0:256].reshape(256, 256).astype(BF16)
        a1[2, plane, parity, 32:288] = t1[:, 8:40, 256:512].reshape(256, 256).astype(BF16)
        return carry

    def taps_first(plane, kz):
        def body(ky, acc):
            parity, start = (ky + 1) % 2, jnp.minimum(ky, 1)
            for kx in range(3):
                acc += dot_nn(a1[kx, plane, parity, rows_from(32 * start)], w1[9 * kz + 3 * ky + kx])
            return acc

        return lax.fori_loop(0, 3, body, jnp.zeros((256, 128), F32))

    sends_part = jnp.logical_and(core == 1, has_outside)
    gets_part = jnp.logical_and(core == 0, has_outside)
    part1_copy = part_copy(0, part1)

    def top_plane():
        load1.wait()
        lax.fori_loop(4 * core + 2, 4 * core + 4, cells, 0)

        @pl.when(sends_part)
        def _():
            part1[0] = taps_first(3, 0).astype(BF16)
            part1_copy.start()

    vol_wait, vol_sent = line_gather(vown, lambda j, p: vol(core, j, p), vsems, top_plane)
    spread.fetch().start()
    lax.fori_loop(4 * core, 4 * core + 2, cells, 0)
    pre1[...] = taps_first(2 * core, 1) + taps_first(2 * core + 1, 2)
    vol_wait(lambda j, p: vol(1 - core, j, p))

    @pl.when(core == 1)
    def _():
        lax.fori_loop(2, 4, cells, 0)
        pre1[...] += taps_first(1, 0)

    @pl.when(gets_part)
    def _():
        part1_copy.wait_recv()
        pre1[...] += part1[1].astype(F32)

    pre_first = pre1[...]
    hown[...] = (pre_first * jax.nn.sigmoid(pre_first)).astype(BF16)

    def hid(plane, j):
        return hg.at[plane, :, pl.ds(pl.multiple_of(128 * j, 128), 128)]

    def turn(i, carry):
        k = offset_of(i, core)
        kz, ky, kx = k // 9, (k // 3) % 3, k % 3
        parity, start = (ky + 1) % 2, jnp.minimum(ky, 1)
        plane = jnp.where(kz == 1, 0, 1)
        at[i, :, 0:256] = a1[kx, plane, parity, rows_from(32 * start)].T
        at[i, :, 256:512] = a1[kx, plane + 2, parity, rows_from(32 * start)].T
        return carry

    def windows():
        spread.fetch().wait_recv()
        spread.each(1, "start")
        lax.fori_loop(4 - 4 * core, 8 - 6 * core, cells, 0)
        lax.fori_loop(0, HALF, turn, 0)

    hid_wait, hid_sent = direct_gather(hown, lambda j: hid(core, j), hsems, windows)

    t2[:, 0:8, :] = jnp.zeros((8, 8, 512), F32)
    t2[:, 40:48, :] = jnp.zeros((8, 8, 512), F32)

    def spread_hidden(i):
        t2[:, 8:40, :] = hg[i].astype(F32).reshape(8, 32, 512)
        edge = jnp.zeros((32, 512), BF16)
        for kx in range(3):
            h3[kx, i, 0:32] = edge
            h3[kx, i, 288:320] = edge
        h3[0, i, 32:288] = t2[:, 7:39, :].reshape(256, 512).astype(BF16)
        h3[1, i, 32:288] = hg[i]
        h3[2, i, 32:288] = t2[:, 9:41, :].reshape(256, 512).astype(BF16)

    def taps_second(plane, kz):
        def body(ky, acc):
            for kx in range(3):
                acc += dot_nn(h3[kx, plane, rows_from(32 * ky)], w2[9 * kz + 3 * ky + kx])
            return acc

        return lax.fori_loop(0, 3, body, jnp.zeros((256, 128), F32))

    load2.wait()
    spread_hidden(core)
    part2_copy = part_copy(1, part2)

    @pl.when(has_outside)
    def _():
        part2[0] = taps_second(core, 2 - 2 * core).astype(BF16)
        part2_copy.start()

    pre_second = taps_second(core, 1)
    hid_wait(lambda j: hid(1 - core, j))
    spread_hidden(1 - core)
    pre_second += taps_second(1 - core, 2 - 2 * core)

    def turn_hidden(i, carry):
        ky, kx = i // 3, i % 3
        ht[i, :, 0:256] = h3[kx, core, rows_from(32 * ky)].T
        ht[i, :, 256:512] = h3[kx, 1 - core, rows_from(32 * ky)].T
        return carry

    lax.fori_loop(4 - 4 * core, 9 - 4 * core, turn_hidden, 0)

    @pl.when(jnp.logical_not(has_outside))
    def _():
        part2[1] = jnp.zeros((256, 128), BF16)

    @pl.when(has_outside)
    def _():
        part2_copy.wait_recv()

    pre_second += part2[1].astype(F32)
    gs[1] = (cot_ref[...].astype(F32) * swish_slope(pre_second)).astype(BF16)

    spread.each(1, "get")
    spread.each(2, "start")

    def swap(place_there, to, slot):
        return remote(gs.at[1], gs.at[place_there], gsem_s.at[slot], gsem_r.at[slot], to, f)

    to_mate = swap(2 * core, mate, 0)
    to_out = swap(2 - 2 * core, outside, 1)
    from_mate = swap(2 - 2 * core, mate, 0)
    from_out = swap(2 * core, outside, 1)
    to_mate.start()

    @pl.when(has_outside)
    def _():
        to_out.start()

    @pl.when(jnp.logical_not(has_outside))
    def _():
        gs[2 * core] = jnp.zeros((256, 128), BF16)

    t3[:, 0:8, :] = jnp.zeros((8, 8, 128), F32)
    t3[:, 40:48, :] = jnp.zeros((8, 8, 128), F32)

    def spread_grads(i):
        t3[:, 8:40, :] = gs[i].astype(F32).reshape(8, 32, 128)
        edge = jnp.zeros((32, 128), BF16)
        for kx in range(3):
            g3[kx, i, 0:32] = edge
            g3[kx, i, 288:320] = edge
        g3[0, i, 32:288] = t3[:, 9:41, :].reshape(256, 128).astype(BF16)
        g3[1, i, 32:288] = gs[i]
        g3[2, i, 32:288] = t3[:, 7:39, :].reshape(256, 128).astype(BF16)

    def back_second(plane, kz, first):
        def body(ky, carry):
            acc = hp[...]
            for kx in range(3):
                acc += dot_nt(g3[kx, plane, rows_from(32 * (2 - ky))], w2[9 * kz + 3 * ky + kx])
            hp[...] = acc
            return carry

        if first:
            hp[...] = jnp.zeros((256, 512), F32)
        lax.fori_loop(0, 3, body, 0)

    spread_grads(1)
    back_second(1, 1, True)
    from_mate.wait_recv()
    spread_grads(2 - 2 * core)
    back_second(2 - 2 * core, 2 * core, False)

    gc2[1, 0:256] = gs[1]
    gc2[1, 256:512] = gs[2 - 2 * core]

    def terms_second(i, carry):
        k = offset_of(i, core)
        pairs = jnp.where(k // 9 == 1, 1, 0)
        red2.d[i] = dot_nn(ht[k % 9], gc2[pairs]).reshape(4, 4, 32, 128).astype(BF16)
        return carry

    for first, last in EARLY:
        lax.fori_loop(first, last, terms_second, 0)
    red2.start_first(EARLY)
    lax.fori_loop(5 * core, 4 + 5 * core, turn_hidden, 0)

    @pl.when(has_outside)
    def _():
        from_out.wait_recv()

    spread_grads(2 * core)
    back_second(2 * core, 2 - 2 * core, False)

    for j in range(NF):
        ps[j] = hp[:, 128 * j : 128 * j + 128].astype(BF16)
    shares = [remote(ps.at[p], rp.at[n], psem_s.at[n], psem_r.at[n], s, p) for n, p in enumerate(peers)]
    for c in shares:
        c.start()

    gc2[0, 0:256] = gs[2 * core]
    gc2[0, 256:512] = gs[1]
    for first, last in LATE:
        lax.fori_loop(first, last, terms_second, 0)
    red2.start_first(LATE)
    spread.each(2, "get")
    spread.swap(core).start()

    for c in shares:
        c.wait_recv()
    hidden_grad = ps[f].astype(F32)
    for n in range(3):
        hidden_grad += rp[n].astype(F32)
    gf[0] = (hidden_grad * swish_slope(pre1[...])).astype(BF16)

    gf_mate = remote(gf.at[0], gf.at[1], gfsem_s.at[0], gfsem_r.at[0], mate, f)
    gf_out = remote(gf.at[0], gf.at[2], gfsem_s.at[1], gfsem_r.at[1], outside, f)
    sends = jnp.logical_and(core == 0, has_outside)
    gets = jnp.logical_and(core == 1, has_outside)

    @pl.when(sends)
    def _():
        gf_out.start()

    gf_mate.start()

    far, near = (f + 2) % NF, f + 1 - 2 * (f % 2)
    gx_own = remote(gf.at[0], gx.at[0], gx_s.at[0], gx_r.at[0], s, far)
    gx_out = remote(gf.at[2], gx.at[1], gx_s.at[1], gx_r.at[1], s, far)
    gx_give = remote(gx.at[0], gx.at[1], gx_s.at[2], gx_r.at[2], mate, f)
    t3[:, 40:48, :] = jnp.zeros((8, 8, 128), F32)

    def spread_first(q, z, src):
        t3[:, 8:40, :] = src.astype(F32).reshape(8, 32, 128)
        for i in range(2):
            half = jnp.where(f < 2, t3[:, 8 + i : 24 + i, :], t3[:, 24 + i : 40 + i, :])
            g4[q, i, z, 0:128] = half.reshape(128, 128).astype(BF16)
            g4[q, i, z, 128:144] = jnp.zeros((16, 128), BF16)

    def taps(parity):
        return [(1, 0)] if parity == 0 else [(2, 0), (0, 1)]

    def back_first(zp):
        for yp in range(2):
            for xp in range(2):
                acc = jnp.zeros((128, 256), F32)
                for kz, oz in taps(zp):
                    for ky, oy in taps(yp):
                        for kx, ox in taps(xp):
                            k = 9 * kz + 3 * ky + kx
                            there = wx[k // HALF, k - (HALF - 1) * (k // HALF)].reshape(256, 128)
                            acc += dot_nt(g4[0, ox, oz, 16 * oy : 16 * oy + 128], w1[k])
                            acc += dot_nt(g4[1, ox, oz, 16 * oy : 16 * oy + 128], there)
                acc = acc.reshape(8, 16, 256)
                lower, upper = acc[:, 0:8, :].reshape(64, 256), acc[:, 8:16, :].reshape(64, 256)
                lanes = slice(256 * xp, 256 * xp + 256)
                k5[zp, yp, :, lanes] = jnp.where(f % 2 == 0, lower, upper)
                s5[zp, yp, :, lanes] = jnp.where(f % 2 == 0, upper, lower).astype(BF16)

    def share(zp):
        return remote(s5.at[zp], r5.at[zp], s5_s.at[zp], s5_r.at[zp], s, near)

    gf_mate.wait_recv()

    gc1[1, 0:256] = gf[core]
    gc1[1, 256:512] = gf[1 - core]

    def terms_first(i, carry):
        pairs = jnp.where(offset_of(i, core) // 9 == 1, 1, 0)
        red1.d[i] = dot_nn(at[i], gc1[pairs]).reshape(4, 4, 16, 128).astype(BF16)
        return carry

    for first, last in EARLY:
        lax.fori_loop(first, last, terms_first, 0)
    red1.start_first(EARLY)
    gx_own.start()
    red2.start_second()

    @pl.when(gets)
    def _():
        gf_out.wait_recv()

    @pl.when(jnp.logical_and(core == 1, jnp.logical_not(has_outside)))
    def _():
        gf[2] = jnp.zeros((256, 128), BF16)

    gc1[0, 0:256] = gf[0]
    gc1[0, 256:512] = gf[1 + core]
    for first, last in LATE:
        lax.fori_loop(first, last, terms_first, 0)
    red1.start_first(LATE)

    @pl.when(core == 1)
    def _():
        gx_out.start()

    spread.swap(1 - core).wait_recv()
    spread_first(0, 0, gf[0])
    gx_own.wait_recv()

    @pl.when(core == 1)
    def _():
        gx_give.start()

    spread_first(1, 0, gx[0])
    back_first(0)
    even, odd = share(0), share(1)
    even.start()
    red2.start_third()
    spread_first(0, 1, gf[1 + core])

    @pl.when(core == 1)
    def _():
        gx_out.wait_recv()

    @pl.when(core == 0)
    def _():
        gx_give.wait_recv()

    spread_first(1, 1, gx[1])
    back_first(1)
    odd.start()
    red1.start_second()
    red1.start_third()
    for zp, copy in enumerate((even, odd)):
        copy.wait_recv()
        for yp in range(2):
            total = (k5[zp, yp] + r5[zp, yp].astype(F32)).reshape(8, 8, 512)
            for xp in range(2):
                for c in range(2):
                    lane = 256 * xp + 128 * c
                    split[c, zp, :, yp, pl.ds(xp, 8, stride=2), :] = total[:, :, lane : lane + 128]
        for c in range(2):
            gin_ref[zp, :, :, :, 128 * c : 128 * c + 128] = split[c, zp].astype(BF16)
    for k, values, i in red2.finish():
        gw2_ref[k] = values[i]
    for k, values, i in red1.finish():
        gw1_ref[k] = jnp.where(core == 0, values[i, 0:4], values[i, 4:8])

    for c in shares + [even, odd, gx_own, spread.fetch(), spread.swap(core)]:
        c.wait_send()
    for stage in (1, 2):
        spread.each(stage, "sent")

    @pl.when(core == 1)
    def _():
        gx_out.wait_send()
        gx_give.wait_send()

    vol_sent()
    hid_sent()
    to_mate.wait_send()
    gf_mate.wait_send()

    @pl.when(sends_part)
    def _():
        part1_copy.wait_send()

    @pl.when(has_outside)
    def _():
        part2_copy.wait_send()

    @pl.when(has_outside)
    def _():
        to_out.wait_send()

    @pl.when(sends)
    def _():
        gf_out.wait_send()


def run_whole(cells, weight_first, weight_second, cotangent):
    dma = pltpu.SemaphoreType.DMA
    vmem, anywhere = pl.BlockSpec(memory_space=pltpu.VMEM), pl.BlockSpec(memory_space=pl.ANY)
    scratch = [
        pltpu.VMEM((27, 256, 128), BF16),
        pltpu.VMEM((27, 512, 128), BF16),
        dma((2,)),
        pltpu.VMEM((4, 2, NF, 64, 512), BF16),
        pltpu.VMEM((8, 40, 512), F32),
        pltpu.VMEM((3, 4, 2, 288, 256), BF16),
        pltpu.VMEM((256, 128), F32),
        pltpu.VMEM((256, 128), BF16),
        pltpu.VMEM((2, 256, 512), BF16),
        pltpu.VMEM((8, 48, 512), F32),
        pltpu.VMEM((3, 2, 320, 512), BF16),
        pltpu.VMEM((2, 256, 128), BF16),
        pltpu.VMEM((2, 256, 128), BF16),
        dma((2,)),
        dma((2,)),
        pltpu.VMEM((3, 256, 128), BF16),
        pltpu.VMEM((8, 48, 128), F32),
        pltpu.VMEM((3, 3, 320, 128), BF16),
        dma((2,)),
        dma((2,)),
        pltpu.VMEM((256, 512), F32),
        pltpu.VMEM((NF, 256, 128), BF16),
        pltpu.VMEM((3, 256, 128), BF16),
        dma((3,)),
        dma((3,)),
        pltpu.VMEM((3, 256, 128), BF16),
        dma((2,)),
        dma((2,)),
        pltpu.VMEM((2, 2, 2, 144, 128), BF16),
        pltpu.VMEM((2, 2, 64, 512), BF16),
        pltpu.VMEM((2, 2, 64, 512), BF16),
        dma((2,)),
        dma((2,)),
        pltpu.VMEM((HALF, 256, 512), BF16),
        pltpu.VMEM((2, 2, 8, 2, 16, 128), F32),
        pltpu.VMEM((2, 2, 64, 512), BF16),
        pltpu.VMEM((9, 512, 512), BF16),
        pltpu.VMEM((2, 512, 128), BF16),
        pltpu.VMEM((2, 512, 128), BF16),
        pltpu.VMEM((2, HALF, 4, 4, 16, 128), BF16),
        dma((4, 3)),
        dma((4, 3)),
        pltpu.VMEM((2, 256, 128), BF16),
        dma((3,)),
        dma((3,)),
        pltpu.VMEM((2, 2, 64, 512), F32),
    ]
    scratch += line_sems() + direct_sems() + reduction_scratch(32) + reduction_scratch(16)
    return pl.pallas_call(
        whole_kernel,
        out_shape=(
            jax.ShapeDtypeStruct((2, 8, 2, 16, 256), BF16),
            jax.ShapeDtypeStruct((27, 4, 128), F32),
            jax.ShapeDtypeStruct((27, 8, 128), F32),
        ),
        in_specs=[vmem, anywhere, anywhere, vmem],
        out_specs=(vmem, vmem, vmem),
        scratch_shapes=scratch,
        compiler_params=pltpu.CompilerParams(collective_id=0, has_side_effects=True, vmem_limit_bytes=52 * 2**20),
        name="bottleneck",
    )(cells, weight_first, weight_second, cotangent)


def per_device(volume, weight_first, weight_second, cotangent):
    grad, grad_first, grad_second = run_whole(volume.reshape(2, 8, 2, 16, 256), weight_first, weight_second, cotangent.reshape(256, 128))
    return (grad.reshape(2, 16, 16, 256), grad_first, grad_second)


def solution(mesh):
    placed = (
        P("space", None, "filt", None),
        P(None, None, "filt"),
        P(None, None, "filt"),
        P("space", None, None, "filt"),
    )
    return jax.shard_map(
        per_device,
        mesh=mesh,
        in_specs=placed,
        out_specs=(
            P("space", None, "filt", None),
            P(None, "space", "filt"),
            P(None, "space", "filt"),
        ),
        check_vma=False,
    )
```
